128 devices in a mesh: lat: 8 (over z_lo, x), lon: 16 (over y, z_hi, core).
Axes of the slice: x: 4, y: 4, z: 4 (z_hi: 2, z_lo: 2; z = z_hi * 2 + z_lo), core: 2. Of those that a mesh axis runs over, the one named last changes fastest.
Arguments:
- hidden: bfloat16 [1, 192, 384, 1152], P(None, 'lat', 'lon'), may hold values from -6 to 6
- timestep: int32 [1], replicated, may hold values from 0 to 999
- context: bfloat16 [1, 300, 1152], replicated, may hold values from -6 to 6
- time_weight: bfloat16 [256, 3456], replicated, may hold values from -0.375 to 0.375
- modulation_bias: float32 [3, 1152], replicated, may hold values from -3 to 3
- qkv_weight: bfloat16 [1152, 3456], replicated, may hold values from -0.1875 to 0.1875
- out_weight: bfloat16 [1152, 1152], replicated, may hold values from -0.1875 to 0.1875
- cross_q: bfloat16 [1152, 1152], replicated, may hold values from -0.1875 to 0.1875
- cross_kv: bfloat16 [2, 1152, 1152], P(None, None, 'lon'), may hold values from -0.1875 to 0.1875
- cross_output_projection: bfloat16 [1152, 1152], replicated, may hold values from -0.1875 to 0.1875
Outputs:
- shifted: bfloat16 [1, 192, 384, 1152], P(None, 'lat', 'lon')
The draws below stay inside these ranges and needn't reach their ends.
All inputs are finite; a program needn't handle non-finite values.
Results may differ from the reference program's by a relative error of at most 0.012.
Values may be sent and summed in bfloat16 or wider, within the bound.
No kernel may reach another device: no remote copies, remote signals or barrier semaphores. Data moves between devices by JAX's collectives and lax.ppermute only.
A program may use at most 128 MiB of HBM per device.

```python
import math
import jax
import jax.numpy as jnp
from jax import lax

D = 1152
HEADS = 16
TEXT = 300
FREQ = 256
CORE = 24
HALO = 4
BATCH = 1
NLAT = 192
NLON = 384


def level_of(rng, extent, cuts, low, largest):
    def one(position, blocks):
        steps = jax.random.uniform(jax.random.fold_in(jax.random.fold_in(rng, 6), position), (blocks,), jnp.float32, low / len(cuts), largest / len(cuts))
        return jnp.repeat(jnp.exp(steps), extent[position] // blocks).reshape((-1,) + (1,) * (len(extent) - position - 1))

    loudness = one(*cuts[0])
    for cut in cuts[1:]:
        loudness = loudness * one(*cut)
    return loudness


def scatter_about(rng, dims, deviation, most, pieces=(), kind=jnp.bfloat16):
    values = jax.random.normal(rng, dims, jnp.float32) * deviation
    if len(pieces) > 0:
        values = level_of(rng, dims, pieces, -0.22, 0.18) * values
    return jnp.clip(values, min=-most, max=most).astype(kind)


def setup_inputs(seed: int = 0) -> dict:
    key_of = jax.random.split(jax.random.key(seed), 11)
    hidden = scatter_about(key_of[0], (BATCH, NLAT, NLON, D), 1.0, 6.0, ((1, 8), (2, 16)))
    timestep = jax.random.randint(key_of[1], (BATCH,), 0, 1000).astype(jnp.int32)
    context = scatter_about(key_of[2], (BATCH, TEXT, D), 1.0, 6.0)
    time_weight = scatter_about(key_of[3], (FREQ, 3 * D), FREQ ** -0.5, 0.375)
    modulation_bias = scatter_about(key_of[4], (3, D), 0.5, 3.0, (), jnp.float32)
    qkv_weight = scatter_about(key_of[5], (D, 3 * D), D ** -0.5, 0.1875)
    out_weight = scatter_about(key_of[6], (D, D), D ** -0.5, 0.1875)
    cross_q = scatter_about(key_of[7], (D, D), D ** -0.5, 0.1875)
    cross_kv = scatter_about(key_of[8], (2, D, D), D ** -0.5, 0.1875, ((2, 16),))
    cross_output_projection = scatter_about(key_of[9], (D, D), D ** -0.5, 0.1875)
    return {"hidden": hidden, "timestep": timestep, "context": context, "time_weight": time_weight, "modulation_bias": modulation_bias, "qkv_weight": qkv_weight, "out_weight": out_weight, "cross_q": cross_q, "cross_kv": cross_kv, "cross_output_projection": cross_output_projection}


def modulation(timestep, time_weight, modulation_bias):
    half = time_weight.shape[0] // 2
    freqs = jnp.exp(-math.log(10000.0) * jnp.arange(half, dtype=jnp.float32) / half)
    angle = timestep.astype(jnp.float32)[:, None] * freqs[None, :]
    embed = jnp.concatenate([jnp.cos(angle), jnp.sin(angle)], axis=1)
    embed = jax.nn.silu(embed).astype(jnp.bfloat16)
    mixed = jnp.dot(embed, time_weight, preferred_element_type=jnp.float32) + modulation_bias.reshape(-1)[None, :]
    width = modulation_bias.shape[1]
    return (mixed[:, :width], mixed[:, width:2 * width], mixed[:, 2 * width:])

def layer_norm(value_rows):
    mean = lax.optimization_barrier(jnp.mean(value_rows, axis=-1, keepdims=True))
    centred = value_rows - mean
    var = lax.optimization_barrier(jnp.mean(centred * centred, axis=-1, keepdims=True))
    return centred * lax.rsqrt(var + 1e-06)

def one_head(operands):
    query_rows, key_rows, value_rows = operands
    head_channels = query_rows.shape[-1]
    logit_scores = jnp.einsum('ciw,cpw->cip', query_rows.astype(jnp.float32), key_rows.astype(jnp.float32)) / math.sqrt(head_channels)
    attention_probabilities = jax.nn.softmax(logit_scores, axis=-1).astype(jnp.bfloat16)
    return jnp.einsum('hmy,hyi->hmi', attention_probabilities.astype(jnp.float32), value_rows.astype(jnp.float32)).astype(jnp.bfloat16)

def attend(query_rows, key_rows, value_rows):
    batch, count, width = query_rows.shape
    head_channels = width // HEADS
    qh = jnp.transpose(query_rows.reshape(batch, count, HEADS, head_channels), (2, 0, 1, 3))
    kh = jnp.transpose(key_rows.reshape(batch, key_rows.shape[1], HEADS, head_channels), (2, 0, 1, 3))
    vh = jnp.transpose(value_rows.reshape(batch, value_rows.shape[1], HEADS, head_channels), (2, 0, 1, 3))
    mixed = lax.map(one_head, (qh, kh, vh))
    return jnp.transpose(mixed, (1, 2, 0, 3)).reshape(batch, count, width)

def project(value_rows, weight):
    return jnp.einsum('bnd,de->bne', value_rows.astype(jnp.float32), weight.astype(jnp.float32))

def tile_block(tile, shift, scale, gate, key_rows, value_rows, qkv_weight, out_weight, cross_q, cross_output_projection):
    batch, rows, cols, width = tile.shape
    x_vals = tile.reshape(batch, rows * cols, width).astype(jnp.float32)
    normed = (layer_norm(x_vals) * (1.0 + scale[:, None, :]) + shift[:, None, :]).astype(jnp.bfloat16)
    qkv = project(normed, qkv_weight).astype(jnp.bfloat16)
    attn = attend(qkv[:, :, :width], qkv[:, :, width:2 * width], qkv[:, :, 2 * width:])
    first = x_vals + gate[:, None, :] * project(attn, out_weight)
    cross_query = project(first.astype(jnp.bfloat16), cross_q).astype(jnp.bfloat16)
    crossed = attend(cross_query, key_rows, value_rows)
    second = first + project(crossed, cross_output_projection)
    return second.reshape(batch, rows, cols, width)

def reference(hidden, timestep, context, time_weight, modulation_bias, qkv_weight, out_weight, cross_q, cross_kv, cross_output_projection):
    shift, scale, gate = modulation(timestep, time_weight, modulation_bias)
    key_rows = project(context, cross_kv[0]).astype(jnp.bfloat16)
    value_rows = project(context, cross_kv[1]).astype(jnp.bfloat16)
    batch, nlat, nlon, width = hidden.shape
    padded = jnp.pad(hidden, ((0, 0), (HALO, HALO), (0, 0), (0, 0)))
    padded = jnp.concatenate([padded[:, :, nlon - HALO:], padded, padded[:, :, :HALO]], axis=2)
    span = CORE + 2 * HALO
    tile_cols = nlon // CORE
    count_tiles = nlat // CORE * tile_cols
    total = jnp.zeros((batch, nlat + 2 * HALO, nlon + 2 * HALO, width), jnp.float32)

    def advance(carry, index):
        row_start = index // tile_cols * CORE
        col_start = index % tile_cols * CORE
        zero = jnp.int32(0)
        starts = (zero, row_start.astype(jnp.int32), col_start.astype(jnp.int32), zero)
        piece = lax.dynamic_slice(padded, starts, (batch, span, span, width))
        result = tile_block(piece, shift, scale, gate, key_rows, value_rows, qkv_weight, out_weight, cross_q, cross_output_projection)
        current = lax.dynamic_slice(carry, starts, (batch, span, span, width))
        return (lax.dynamic_update_slice(carry, current + result, starts), None)
    total, _ = lax.scan(advance, total, jnp.arange(count_tiles, dtype=jnp.int32))
    summed = total[:, HALO:HALO + nlat]
    grid = summed[:, :, HALO:HALO + nlon]
    grid = grid.at[:, :, nlon - HALO:].add(summed[:, :, :HALO])
    grid = grid.at[:, :, :HALO].add(summed[:, :, nlon + HALO:])
    row_ids = jnp.arange(nlat)
    lat_factor = (1.0 + jnp.where((row_ids % CORE < HALO) & (row_ids >= CORE), 1.0, 0.0) + jnp.where((row_ids % CORE >= CORE - HALO) & (row_ids < nlat - CORE), 1.0, 0.0)).astype(jnp.float32)
    col_ids = jnp.arange(nlon)
    lon_factor = (1.0 + jnp.where(col_ids % CORE < HALO, 1.0, 0.0) + jnp.where(col_ids % CORE >= CORE - HALO, 1.0, 0.0)).astype(jnp.float32)
    averaged = grid / (lat_factor[:, None] * lon_factor[None, :])[None, :, :, None]
    return jnp.roll(averaged, -(CORE // 2), axis=2).astype(jnp.bfloat16)
```

```python
import functools
import math

import jax
import jax.numpy as jnp
from jax import lax
from jax.experimental import pallas as pl
from jax.experimental.pallas import tpu as pltpu
from jax.sharding import PartitionSpec as P

HEADS = 16
HALO = 4
WIN = 256
QKV_COLS = 384
TEXT_PAD = 384
VMEM = 56 * 1024 * 1024


def modulation(timestep, time_weight, modulation_bias):
    half = time_weight.shape[0] // 2
    freqs = jnp.exp(-math.log(10000.0) * jnp.arange(half, dtype=jnp.float32) / half)
    angle = timestep.astype(jnp.float32)[:, None] * freqs[None, :]
    embed = jnp.concatenate([jnp.cos(angle), jnp.sin(angle)], axis=1)
    embed = jax.nn.silu(embed).astype(jnp.bfloat16)
    mixed = (
        jnp.dot(embed, time_weight, preferred_element_type=jnp.float32)
        + modulation_bias.reshape(-1)[None, :]
    )
    width = modulation_bias.shape[1]
    return (mixed[:, :width], mixed[:, width : 2 * width], mixed[:, 2 * width :])


def qkv_kernel(q_factor, x_ref, shift_ref, scale_ref, w_ref, out_ref, u_ref):
    step = pl.program_id(0)
    count, width = x_ref.shape
    rows = 32

    @pl.when(step == 0)
    def _():
        gain = 1.0 + scale_ref[...]
        shift = shift_ref[...]

        def norm(i, carry):
            part = pl.ds(pl.multiple_of(i * rows, rows), rows)
            x = x_ref[part, :].astype(jnp.float32)
            mean = jnp.mean(x, axis=-1, keepdims=True)
            centred = x - mean
            var = jnp.mean(centred * centred, axis=-1, keepdims=True)
            normed = centred * lax.rsqrt(var + 1e-06)
            u_ref[part, :] = (normed * gain + shift).astype(jnp.bfloat16)
            return carry

        lax.fori_loop(0, count // rows, norm, 0, unroll=2)

    factor = jnp.where(step < width // QKV_COLS, jnp.float32(q_factor), jnp.float32(1.0))
    out_ref[...] = (
        jnp.dot(u_ref[...], w_ref[...], preferred_element_type=jnp.float32) * factor
    ).astype(jnp.bfloat16)


def qkv_of(x, shift, scale, weight):
    count, width = x.shape
    total = weight.shape[1]
    q_factor = math.log2(math.e) / math.sqrt(width // HEADS)
    return pl.pallas_call(
        functools.partial(qkv_kernel, q_factor),
        out_shape=jax.ShapeDtypeStruct((count, total), jnp.bfloat16),
        grid=(total // QKV_COLS,),
        in_specs=[
            pl.BlockSpec((count, width), lambda i: (0, 0)),
            pl.BlockSpec((1, width), lambda i: (0, 0)),
            pl.BlockSpec((1, width), lambda i: (0, 0)),
            pl.BlockSpec((width, QKV_COLS), lambda i: (0, i)),
        ],
        out_specs=pl.BlockSpec((count, QKV_COLS), lambda i: (0, i)),
        scratch_shapes=[pltpu.VMEM((count, width), jnp.bfloat16)],
        compiler_params=pltpu.CompilerParams(vmem_limit_bytes=VMEM),
        cost_estimate=pl.CostEstimate(
            flops=2 * count * width * total,
            bytes_accessed=2 * (width * total + count * (width + total)),
            transcendentals=0,
        ),
    )(x, shift, scale, weight)


def window(h, width, channels):
    start = jnp.minimum((h * channels) // 128, (width - WIN) // 128)
    start = pl.multiple_of(start * 128, 128)
    return start, h * channels - start


def lane_mask(offset, channels, dims, axis):
    ids = lax.broadcasted_iota(jnp.int32, dims, axis)
    return (ids >= offset) & (ids < offset + channels)


def soft_rows(s, valid):
    if valid < s.shape[1]:
        ids = lax.broadcasted_iota(jnp.int32, s.shape, 1)
        s = jnp.where(ids < valid, s, -jnp.inf)
    m = jnp.max(s, axis=-1, keepdims=True)
    return jnp.exp2(s - m).astype(jnp.bfloat16)


NT = (((1,), (1,)), ((), ()))


def heads_loop(channels, chunk, q_ref, load_keys, load_values, key_dims, value_dims, value_axis, valid, s_refs, out_ref):
    count, width = q_ref.shape
    chunks = [slice(c, c + chunk) for c in range(0, count, chunk)]

    def masked_q(h):
        start, offset = window(h, width, channels)
        keep = lane_mask(offset, channels, (1, WIN), 1).astype(jnp.float32).astype(jnp.bfloat16)
        return start, keep

    def scores(h, s_ref, part):
        start, keep = masked_q(h)
        q = q_ref[part, pl.ds(start, WIN)] * keep
        s_ref[part, :] = lax.dot_general(
            q, load_keys(start), key_dims, preferred_element_type=jnp.float32
        )

    def finish(h, s_ref, part):
        start, offset = window(h, width, channels)
        v = load_values(start)
        dims = (1, WIN) if value_axis == 1 else (WIN, 1)
        keep = lane_mask(offset, channels, dims, value_axis).astype(jnp.float32).astype(jnp.bfloat16)
        v = v * keep + (1 - keep)
        p = soft_rows(s_ref[part, :], valid)
        o = lax.dot_general(p, v, value_dims, preferred_element_type=jnp.float32)
        inside = lane_mask(offset, channels, (1, WIN), 1)
        total = jnp.max(jnp.where(inside, 0.0, o), axis=-1, keepdims=True)
        o = o / total
        old = out_ref[part, pl.ds(start, WIN)].astype(jnp.float32)
        out_ref[part, pl.ds(start, WIN)] = jnp.where(inside, o, old).astype(jnp.bfloat16)

    first, second = s_refs
    for part in chunks:
        scores(jnp.int32(0), first, part)

    def step(t, carry):
        h = 2 * t
        for part in chunks:
            scores(h + 1, second, part)
            finish(h, first, part)
        after = jnp.minimum(h + 2, HEADS - 1)
        for part in chunks:
            scores(after, first, part)
            finish(h + 1, second, part)
        return carry

    lax.fori_loop(0, HEADS // 2, step, 0)


def attention_kernel(
    segments,
    parts,
    text,
    chunk,
    x_core,
    x_rim,
    qkv_core,
    qkv_rim,
    text_kv,
    gate_ref,
    out_weight,
    cross_q,
    cross_out,
    *rest,
):
    outs = rest[: len(parts)]
    (x_s, q_s, k_s, v_s, kv_s, wo_s, wq_s, wc_s, attn_s, h1_s, s_a, s_b, c_a, c_b, sems) = rest[
        len(parts) :
    ]
    core_count, width = x_core.shape
    channels = width // HEADS
    sources = {"core": (x_core, qkv_core), "rim": (x_rim, qkv_rim)}
    rim_count = x_rim.shape[0]

    def copies(pairs, sem):
        made = [pltpu.make_async_copy(a, b, sems.at[sem, n]) for n, (a, b) in enumerate(pairs)]
        for c in made:
            c.start()
        return made

    q_pairs, x_pairs = [], []
    for name, src, dst, n in segments:
        x, qkv = sources[name]
        q_pairs.append((qkv.at[pl.ds(src, n), pl.ds(0, width)], q_s.at[pl.ds(dst, n)]))
        x_pairs.append((x.at[pl.ds(src, n)], x_s.at[pl.ds(dst, n)]))
    waits_q = copies(q_pairs, 0)
    waits_k = copies(
        [
            (qkv_core.at[:, pl.ds(width, width)], k_s.at[pl.ds(0, core_count)]),
            (qkv_rim.at[:, pl.ds(width, width)], k_s.at[pl.ds(core_count, rim_count)]),
        ],
        1,
    )
    waits_v = copies(
        [
            (qkv_core.at[:, pl.ds(2 * width, width)], v_s.at[pl.ds(0, core_count)]),
            (qkv_rim.at[:, pl.ds(2 * width, width)], v_s.at[pl.ds(core_count, rim_count)]),
        ],
        2,
    )
    waits_later = copies(
        [(out_weight, wo_s), (cross_q, wq_s), (cross_out, wc_s), (text_kv, kv_s)], 3
    )
    waits_x = copies(x_pairs, 4)
    for c in waits_q + waits_k + waits_v:
        c.wait()

    attn_s[...] = jnp.zeros_like(attn_s)
    heads_loop(
        channels,
        chunk,
        q_s,
        lambda start: k_s[:, pl.ds(start, WIN)],
        lambda start: v_s[:, pl.ds(start, WIN)],
        NT,
        (((1,), (0,)), ((), ())),
        1,
        k_s.shape[0],
        (s_a, s_b),
        attn_s,
    )
    for c in waits_later + waits_x:
        c.wait()
    cols = 384
    q_factor = math.log2(math.e) / math.sqrt(channels)
    for n in range(0, width, cols):
        part = slice(n, n + cols)
        mixed = jnp.dot(attn_s[...], wo_s[:, part], preferred_element_type=jnp.float32)
        h1_s[:, part] = x_s[:, part].astype(jnp.float32) + gate_ref[:, part] * mixed
    x_s[...] = h1_s[...].astype(jnp.bfloat16)
    for n in range(0, width, cols):
        part = slice(n, n + cols)
        q_s[:, part] = (
            jnp.dot(x_s[...], wq_s[:, part], preferred_element_type=jnp.float32) * q_factor
        ).astype(jnp.bfloat16)
    heads_loop(
        channels,
        chunk,
        q_s,
        lambda start: kv_s[0, pl.ds(start, WIN), :],
        lambda start: kv_s[1, pl.ds(start, WIN), :],
        (((1,), (0,)), ((), ())),
        NT,
        0,
        text,
        (c_a, c_b),
        attn_s,
    )
    for n in range(0, width, cols):
        part = slice(n, n + cols)
        h1_s[:, part] += jnp.dot(attn_s[...], wc_s[:, part], preferred_element_type=jnp.float32)
    at = 0
    for out, n in zip(outs, parts):
        out[...] = h1_s[at : at + n, :].astype(jnp.bfloat16)
        at += n


def attention_of(segments, parts, text, chunk, x_core, x_rim, qkv_core, qkv_rim, text_kv, gate, out_weight, cross_q, cross_out):
    width = x_core.shape[1]
    count = sum(parts)
    keys = x_core.shape[0] + x_rim.shape[0]
    anywhere = pl.BlockSpec(memory_space=pl.ANY)
    local = pl.BlockSpec(memory_space=pltpu.VMEM)
    bf16, f32 = jnp.bfloat16, jnp.float32
    padded = text_kv.shape[-1]
    return pl.pallas_call(
        functools.partial(attention_kernel, segments, parts, text, chunk),
        out_shape=[jax.ShapeDtypeStruct((n, width), bf16) for n in parts],
        in_specs=[anywhere] * 5 + [local] + [anywhere] * 3,
        out_specs=[local] * len(parts),
        scratch_shapes=[
            pltpu.VMEM((count, width), bf16),
            pltpu.VMEM((count, width), bf16),
            pltpu.VMEM((keys, width), bf16),
            pltpu.VMEM((keys, width), bf16),
            pltpu.VMEM(text_kv.shape, bf16),
            pltpu.VMEM((width, width), bf16),
            pltpu.VMEM((width, width), bf16),
            pltpu.VMEM((width, width), bf16),
            pltpu.VMEM((count, width), bf16),
            pltpu.VMEM((count, width), f32),
            pltpu.VMEM((count, keys), f32),
            pltpu.VMEM((count, keys), f32),
            pltpu.VMEM((count, padded), f32),
            pltpu.VMEM((count, padded), f32),
            pltpu.SemaphoreType.DMA((5, 8)),
        ],
        compiler_params=pltpu.CompilerParams(vmem_limit_bytes=VMEM),
        cost_estimate=pl.CostEstimate(
            flops=16 * count * width * (keys + padded) + 6 * count * width * width,
            bytes_accessed=2 * (3 * width * width + 3 * keys * width),
            transcendentals=HEADS * count * (keys + text),
        ),
    )(x_core, x_rim, qkv_core, qkv_rim, text_kv, gate, out_weight, cross_q, cross_out)


def send(value, mesh_sizes, down, right):
    rows, cols = mesh_sizes
    pairs = [
        (r * cols + c, (r + down) * cols + (c + right) % cols)
        for r in range(rows)
        for c in range(cols)
        if 0 <= r + down < rows
    ]
    return lax.ppermute(value, ("lat", "lon"), pairs)


def local(
    sizes,
    hidden,
    timestep,
    context,
    time_weight,
    modulation_bias,
    qkv_weight,
    out_weight,
    cross_q,
    cross_kv,
    cross_output_projection,
):
    batch, core, _, width = hidden.shape
    half = core // 2
    rim = HALO
    text = context.shape[1]
    to = functools.partial(send, mesh_sizes=sizes)

    x = jnp.transpose(hidden[0], (1, 0, 2))
    left = to(x[core - rim :], down=0, right=1)
    right = to(x[:rim], down=0, right=-1)
    last, first = x[:, core - rim :], x[:, :rim]
    top = to(last, down=1, right=0)
    bottom = to(first, down=-1, right=0)
    top_left = to(last[core - rim :], down=1, right=1)
    top_right = to(last[:rim], down=1, right=-1)
    bottom_left = to(first[core - rim :], down=-1, right=1)
    bottom_right = to(first[:rim], down=-1, right=-1)

    padded = jnp.pad(context[0], ((0, TEXT_PAD - text), (0, 0)))
    own_heads = jnp.einsum(
        "td,sde->set", padded, cross_kv, preferred_element_type=jnp.float32
    ).astype(jnp.bfloat16)
    text_kv = lax.all_gather(own_heads, "lon", axis=1, tiled=True)

    shift, scale, gate = modulation(timestep, time_weight, modulation_bias)
    x_core = x.reshape(core * core, width)
    qkv_core = qkv_of(x_core, shift, scale, qkv_weight)

    flat = lambda a: a.reshape(-1, width)
    x_rim = jnp.concatenate(
        [
            flat(left),
            flat(right),
            flat(top_left),
            flat(top[:half]),
            flat(bottom_left),
            flat(bottom[:half]),
            flat(top[half:]),
            flat(top_right),
            flat(bottom[half:]),
            flat(bottom_right),
        ],
        axis=0,
    )
    qkv_rim = qkv_of(x_rim, shift, scale, qkv_weight)

    side = rim * core
    inner = half * core
    edge = (half + rim) * rim
    weights = (out_weight, cross_q, cross_output_projection)
    operands = (x_core, x_rim, qkv_core, qkv_rim, text_kv, gate) + weights
    sent = attention_of(
        (("rim", 0, 0, side), ("core", 0, side, inner), ("rim", 2 * side, side + inner, 4 * edge)),
        (side + inner, edge, edge, edge, edge),
        text,
        320,
        *operands,
    )
    main = to(sent[0], down=0, right=-1)
    up_left = to(sent[1], down=-1, right=-1)
    down_left = to(sent[2], down=1, right=-1)
    up = to(sent[3], down=-1, right=0)
    down = to(sent[4], down=1, right=0)
    (own,) = attention_of(
        (("core", inner, 0, inner), ("rim", side, inner, side)),
        (inner + side,),
        text,
        384,
        *operands,
    )

    span = half + rim
    f32 = jnp.float32

    def placed(inside, low, high):
        body = inside.reshape(span, core, width).astype(f32)
        low = low.reshape(span, rim, width).astype(f32)
        high = high.reshape(span, rim, width).astype(f32)
        edges = jnp.concatenate(
            [low, jnp.zeros((span, core - 2 * rim, width), f32), high], axis=1
        )
        return body + edges

    near = placed(own, down, up)
    far = placed(main, down_left, up_left)
    rest = core - span
    total = jnp.concatenate([near[:rest], near[rest:] + far[: span - rest], far[span - rest :]], axis=0)
    lat_index = lax.axis_index("lat")
    ids = jnp.arange(core)
    lat_factor = (
        1.0
        + jnp.where((ids < rim) & (lat_index > 0), 1.0, 0.0)
        + jnp.where((ids >= core - rim) & (lat_index < sizes[0] - 1), 1.0, 0.0)
    ).astype(f32)
    lon_factor = jnp.where((ids >= rest) & (ids < span), 2.0, 1.0).astype(f32)
    averaged = total / (lon_factor[:, None] * lat_factor[None, :])[:, :, None]
    return jnp.transpose(averaged.astype(jnp.bfloat16), (1, 0, 2))[None]


def solution(mesh):
    in_specs = (
        P(None, "lat", "lon", None),
        P(),
        P(),
        P(),
        P(),
        P(),
        P(),
        P(),
        P(None, None, "lon"),
        P(),
    )
    out_specs = P(None, "lat", "lon", None)
    sizes = (mesh.shape["lat"], mesh.shape["lon"])
    return jax.shard_map(
        functools.partial(local, sizes), mesh=mesh, in_specs=in_specs, out_specs=out_specs, check_vma=False
    )
```

```python
import functools
import math

import jax
import jax.numpy as jnp
from jax import lax
from jax.experimental import pallas as pl
from jax.experimental.pallas import tpu as pltpu
from jax.sharding import PartitionSpec as P

HEADS = 16
PAIRS = HEADS // 2
HALO = 4
LANES = 128
WIN = 256
TEXT_PAD = 384
VMEM = 60 * 1024 * 1024
NN = (((1,), (0,)), ((), ()))
NT = (((1,), (1,)), ((), ()))
BF16, F32 = jnp.bfloat16, jnp.float32
ANY = pl.BlockSpec(memory_space=pl.ANY)
LOCAL = pl.BlockSpec(memory_space=pltpu.VMEM)


def modulation(timestep, time_weight, modulation_bias):
    half = time_weight.shape[0] // 2
    freqs = jnp.exp(-math.log(10000.0) * jnp.arange(half, dtype=F32) / half)
    angle = timestep.astype(F32)[:, None] * freqs[None, :]
    embed = jnp.concatenate([jnp.cos(angle), jnp.sin(angle)], axis=1)
    embed = jax.nn.silu(embed).astype(BF16)
    mixed = jnp.dot(embed, time_weight, preferred_element_type=F32) + modulation_bias.reshape(-1)[None, :]
    width = modulation_bias.shape[1]
    return (mixed[:, :width], mixed[:, width : 2 * width], mixed[:, 2 * width :])


def begin(pairs, sems, first):
    made = [pltpu.make_async_copy(a, b, sems.at[first + n]) for n, (a, b) in enumerate(pairs)]
    for c in made:
        c.start()
    return made


def finish_all(made):
    for c in made:
        c.wait()


def normalise(x_ref, at, count, shift_ref, scale_ref, u_ref):
    rows = 32
    gain = 1.0 + scale_ref[...]
    shift = shift_ref[...]

    def norm(i, carry):
        x = x_ref[pl.ds(pl.multiple_of(at + i * rows, rows), rows), :].astype(F32)
        mean = jnp.mean(x, axis=-1, keepdims=True)
        centred = x - mean
        var = jnp.mean(centred * centred, axis=-1, keepdims=True)
        normed = centred * lax.rsqrt(var + 1e-06)
        u_ref[pl.ds(pl.multiple_of(i * rows, rows), rows), :] = (normed * gain + shift).astype(BF16)
        return carry

    lax.fori_loop(0, count // rows, norm, 0, unroll=2)


def column_parts(total, size):
    return [(c, min(size, total - c)) for c in range(0, total, size)]


def weight_pairs(w_hbm, w_s, size):
    return [
        (w_hbm.at[:, pl.ds(c, n)], w_s.at[:, pl.ds(c, n)]) for c, n in column_parts(w_hbm.shape[1], size)
    ]


def project_qkv(u_ref, w_s, waits, size, width, q_factor, out_ref, at):
    count = u_ref.shape[0]
    for wait, (c, n) in zip(waits, column_parts(w_s.shape[1], size)):
        wait.wait()
        made = jnp.dot(u_ref[...], w_s[:, c : c + n], preferred_element_type=F32)
        if c < width:
            ids = lax.broadcasted_iota(jnp.int32, (1, n), 1)
            made = made * jnp.where(ids < width - c, q_factor, 1.0)
        out_ref[at : at + count, c : c + n] = made.astype(BF16)


def band(low, high, dims, axis):
    ids = lax.broadcasted_iota(jnp.int32, dims, axis)
    return ((ids >= low) & (ids < high)).astype(F32).astype(BF16)


def pair_start(t):
    return pl.multiple_of(t * LANES, LANES)


def spare_columns(t, channels):
    gap = 2 * channels - LANES
    return jnp.where(t * gap + 2 * channels <= WIN - 64, WIN - 64, 0)


def pairs_unshifted(channels, q_ref, scores, values, p_refs, bad_ref, rows, out_ref):
    count = q_ref.shape[0]
    parts = [slice(c, c + rows) for c in range(0, count, rows)]
    gap = 2 * channels - LANES

    def close(t, p_ref, v, part):
        spare = spare_columns(t, channels)
        o = lax.dot_general(p_ref[part, :], v[0], v[1], preferred_element_type=F32)
        ids = lax.broadcasted_iota(jnp.int32, (1, WIN), 1)
        sum_a = jnp.max(jnp.where((ids >= spare) & (ids < spare + 32), o, 0.0), axis=-1, keepdims=True)
        sum_b = jnp.max(jnp.where((ids >= spare + 32) & (ids < spare + 64), o, 0.0), axis=-1, keepdims=True)
        low, high = 2.0**-100, 2.0**100
        good = (sum_a >= low) & (sum_a <= high) & (sum_b >= low) & (sum_b <= high)
        bad_ref[...] = jnp.maximum(bad_ref[...], jnp.max(jnp.where(good, 0.0, 1.0), axis=0, keepdims=True))
        start = gap * t
        scale = jnp.where(ids < start + channels, 1.0 / sum_a, 1.0 / sum_b)
        cols = pl.ds(pair_start(t), WIN)
        old = out_ref[part, cols].astype(F32)
        inside = (ids >= start) & (ids < start + 2 * channels)
        out_ref[part, cols] = jnp.where(inside, o * scale, old).astype(BF16)

    def both(t, now, after):
        v = values(t, gap * t)
        for part in parts:
            scores(t + 1, gap * (t + 1), part, after)
            close(t, now, v, part)

    first, second = p_refs
    bad_ref[...] = jnp.zeros_like(bad_ref)
    for part in parts:
        scores(jnp.int32(0), jnp.int32(0), part, first)

    def step(i, carry):
        both(2 * i, first, second)
        both(2 * i + 1, second, first)
        return carry

    lax.fori_loop(0, PAIRS // 2 - 1, step, 0)
    both(jnp.int32(PAIRS - 2), first, second)
    v = values(jnp.int32(PAIRS - 1), jnp.int32(gap * (PAIRS - 1)))
    for part in parts:
        close(jnp.int32(PAIRS - 1), second, v, part)


def heads_shifted(channels, q_ref, keys, key_dims, values, value_dims, valid, out_ref):
    count, width = q_ref.shape
    rows = 64

    def one(n, carry):
        h = n // (count // rows)
        part = pl.ds(pl.multiple_of((n % (count // rows)) * rows, rows), rows)
        t = jnp.minimum((h * channels) // LANES, (width - WIN) // LANES)
        start = pair_start(t)
        offset = h * channels - start
        cols = pl.ds(start, WIN)
        q = q_ref[part, cols] * band(offset, offset + channels, (1, WIN), 1)
        s = lax.dot_general(q, keys(start), key_dims, preferred_element_type=F32)
        if valid < s.shape[1]:
            s = jnp.where(lax.broadcasted_iota(jnp.int32, s.shape, 1) < valid, s, -jnp.inf)
        p = jnp.exp2(s - jnp.max(s, axis=-1, keepdims=True))
        total = jnp.sum(p, axis=-1, keepdims=True)
        o = lax.dot_general(p.astype(BF16), values(start), value_dims, preferred_element_type=F32) / total
        ids = lax.broadcasted_iota(jnp.int32, (1, WIN), 1)
        old = out_ref[part, cols].astype(F32)
        inside = (ids >= offset) & (ids < offset + channels)
        out_ref[part, cols] = jnp.where(inside, o, old).astype(BF16)
        return carry

    lax.fori_loop(0, HEADS * (count // rows), one, 0)


def attend_self(channels, q_ref, k_ref, v_ref, vv_ref, p_refs, bad_ref, rows, out_ref):
    n = k_ref.shape[0]

    def scores(t, start, part, p_ref):
        cols = pl.ds(pair_start(t), WIN)
        q = q_ref[part, cols]
        for j in range(2):
            low = start + j * channels
            s = lax.dot_general(
                q * band(low, low + channels, (1, WIN), 1), k_ref[:, cols], NT, preferred_element_type=F32
            )
            p_ref[part, j * n : (j + 1) * n] = jnp.exp2(s).astype(BF16)

    def values(t, start):
        v = v_ref[:, pl.ds(pair_start(t), WIN)]
        spare = spare_columns(t, channels)
        for j in range(2):
            low, mark = start + j * channels, spare + 32 * j
            vv_ref[j * n : (j + 1) * n, :] = v * band(low, low + channels, (1, WIN), 1) + band(
                mark, mark + 32, (1, WIN), 1
            )
        return vv_ref[...], NN

    out_ref[...] = jnp.zeros_like(out_ref)
    pairs_unshifted(channels, q_ref, scores, values, p_refs, bad_ref, rows, out_ref)

    @pl.when(jnp.max(bad_ref[...]) > 0.0)
    def _():
        heads_shifted(
            channels,
            q_ref,
            lambda start: k_ref[:, pl.ds(start, WIN)],
            NT,
            lambda start: v_ref[:, pl.ds(start, WIN)],
            NN,
            n,
            out_ref,
        )


def attend_text(channels, text, q_ref, kv_ref, p_refs, bad_ref, rows, out_ref):
    n = kv_ref.shape[2]

    def scores(t, start, part, p_ref):
        k = kv_ref[0, pl.ds(pair_start(t), WIN), :]
        pair = [
            k * band(start + j * channels, start + (j + 1) * channels, (WIN, 1), 0) for j in range(2)
        ]
        s = lax.dot_general(
            q_ref[part, pl.ds(pair_start(t), WIN)],
            jnp.concatenate(pair, axis=1),
            NN,
            preferred_element_type=F32,
        )
        p_ref[part, :] = jnp.exp2(s).astype(BF16)

    def values(t, start):
        v = kv_ref[1, pl.ds(pair_start(t), WIN), :]
        valid = band(0, text, (1, n), 1)
        spare = spare_columns(t, channels)
        pair = [
            v * band(start + j * channels, start + (j + 1) * channels, (WIN, 1), 0)
            + band(spare + 32 * j, spare + 32 * j + 32, (WIN, 1), 0) * valid
            for j in range(2)
        ]
        return jnp.concatenate(pair, axis=1), NT

    out_ref[...] = jnp.zeros_like(out_ref)
    pairs_unshifted(channels, q_ref, scores, values, p_refs, bad_ref, rows, out_ref)

    @pl.when(jnp.max(bad_ref[...]) > 0.0)
    def _():
        heads_shifted(
            channels,
            q_ref,
            lambda start: kv_ref[0, pl.ds(start, WIN), :],
            NN,
            lambda start: kv_ref[1, pl.ds(start, WIN), :],
            NT,
            text,
            out_ref,
        )


QKV_PART = 512


def core_kernel(q_factor, x_ref, shift_ref, scale_ref, w_hbm, out_ref, u_s, w_s, sems):
    waits = begin(weight_pairs(w_hbm, w_s, QKV_PART), sems, 0)
    count, width = x_ref.shape
    normalise(x_ref, 0, count, shift_ref, scale_ref, u_s)
    project_qkv(u_s, w_s, waits, QKV_PART, width, q_factor, out_ref, 0)


def core_qkv(q_factor, x, shift, scale, weight):
    count, width = x.shape
    total = weight.shape[1]
    return pl.pallas_call(
        functools.partial(core_kernel, q_factor),
        out_shape=jax.ShapeDtypeStruct((count, total), BF16),
        in_specs=[LOCAL, LOCAL, LOCAL, ANY],
        out_specs=LOCAL,
        scratch_shapes=[
            pltpu.VMEM((count, width), BF16),
            pltpu.VMEM((width, total), BF16),
            pltpu.SemaphoreType.DMA((8,)),
        ],
        compiler_params=pltpu.CompilerParams(vmem_limit_bytes=VMEM),
        cost_estimate=pl.CostEstimate(
            flops=2 * count * width * total,
            bytes_accessed=2 * (width * total + count * (width + total)),
            transcendentals=0,
        ),
    )(x, shift, scale, weight)


def regroup(core, rim, source_ref, target_ref):
    half = core // 2
    inner = core * core
    side = core * rim
    edge = side + 2 * rim * rim
    at = 0

    def take(*pieces):
        nonlocal at
        for start, n in pieces:
            target_ref[at : at + n, :] = source_ref[start : start + n, :]
            at += n

    for r in range(core):
        take((inner + rim * r, rim), (core * r, half))
    for base in (inner + 2 * side, inner + 2 * side + edge):
        for a in range(rim):
            take((base + rim * a, rim), (base + rim * rim + core * a, half))
    for base in (inner + 2 * side, inner + 2 * side + edge):
        for a in range(rim):
            take((base + rim * rim + core * a + half, half), (base + rim * rim + side + rim * a, rim))
    for r in range(core):
        take((core * r + half, half), (inner + side + rim * r, rim))


def tile_kernel(
    core,
    rim,
    rows,
    q_factor,
    x_core,
    left,
    right,
    top,
    bottom,
    qkv_core,
    shift_ref,
    scale_ref,
    gate_ref,
    w_hbm,
    wo_hbm,
    wq_hbm,
    h1_out,
    cq_out,
    x_s,
    qkv_s,
    u_s,
    w_s,
    wo_s,
    wq_s,
    vv_s,
    p_a,
    p_b,
    attn_s,
    h1_s,
    hg_s,
    bad_s,
    sems,
):
    width = x_core.shape[1]
    channels = width // HEADS
    inner = x_core.shape[0]
    outer = sum(a.shape[0] for a in (left, right, top, bottom))
    total = inner + outer
    pairs, at = [], inner
    for part in (left, right, top, bottom):
        pairs.append((part, x_s.at[pl.ds(at, part.shape[0])]))
        at += part.shape[0]
    waits_x = begin(pairs, sems, 0)
    waits_w = begin(weight_pairs(w_hbm, w_s, QKV_PART), sems, 4)
    waits_qkv = begin([(qkv_core, qkv_s.at[pl.ds(0, inner)])], sems, 12)
    waits_later = begin([(x_core, x_s.at[pl.ds(0, inner)]), (wo_hbm, wo_s), (wq_hbm, wq_s)], sems, 13)
    finish_all(waits_x)
    normalise(x_s, inner, outer, shift_ref, scale_ref, u_s)
    project_qkv(u_s, w_s, waits_w, QKV_PART, width, q_factor, qkv_s, inner)
    finish_all(waits_qkv)
    attend_self(
        channels,
        qkv_s.at[:, pl.ds(0, width)],
        qkv_s.at[:, pl.ds(width, width)],
        qkv_s.at[:, pl.ds(2 * width, width)],
        vv_s,
        (p_a, p_b),
        bad_s,
        rows,
        attn_s,
    )
    finish_all(waits_later)
    step = total // 2
    for r in range(0, total, step):
        part = slice(r, r + step)
        mixed = jnp.dot(attn_s[part, :], wo_s[...], preferred_element_type=F32)
        h1_s[part, :] = x_s[part, :].astype(F32) + gate_ref[...] * mixed
    regroup(core, rim, h1_s, hg_s)
    waits_h = begin([(hg_s, h1_out)], sems, 16)
    for r in range(0, total, step):
        part = slice(r, r + step)
        made = jnp.dot(hg_s[part, :].astype(BF16), wq_s[...], preferred_element_type=F32)
        attn_s[part, :] = (made * q_factor).astype(BF16)
        waits_h += begin([(attn_s.at[pl.ds(r, step)], cq_out.at[pl.ds(r, step)])], sems, 17 + r // step)
    finish_all(waits_h)


def tile_self(core, rim, q_factor, x_core, rims, qkv_core, mod, qkv_weight, out_weight, cross_q):
    inner, width = x_core.shape
    outer = sum(a.shape[0] for a in rims)
    total = inner + outer
    wide = qkv_weight.shape[1]
    return pl.pallas_call(
        functools.partial(tile_kernel, core, rim, 512, q_factor),
        out_shape=[
            jax.ShapeDtypeStruct((total, width), F32),
            jax.ShapeDtypeStruct((total, width), BF16),
        ],
        in_specs=[ANY] * 6 + [LOCAL] * 3 + [ANY] * 3,
        out_specs=[ANY, ANY],
        scratch_shapes=[
            pltpu.VMEM((total, width), BF16),
            pltpu.VMEM((total, wide), BF16),
            pltpu.VMEM((outer, width), BF16),
            pltpu.VMEM((width, wide), BF16),
            pltpu.VMEM((width, width), BF16),
            pltpu.VMEM((width, width), BF16),
            pltpu.VMEM((2 * total, WIN), BF16),
            pltpu.VMEM((total, 2 * total), BF16),
            pltpu.VMEM((total, 2 * total), BF16),
            pltpu.VMEM((total, width), BF16),
            pltpu.VMEM((total, width), F32),
            pltpu.VMEM((total, width), F32),
            pltpu.VMEM((1, LANES), F32),
            pltpu.SemaphoreType.DMA((20,)),
        ],
        compiler_params=pltpu.CompilerParams(vmem_limit_bytes=VMEM),
        cost_estimate=pl.CostEstimate(
            flops=2 * outer * width * wide + 16 * total * width * total + 4 * total * width * width,
            bytes_accessed=2 * width * (wide + 2 * width) + 2 * inner * wide + 6 * total * width,
            transcendentals=HEADS * total * total,
        ),
    )(x_core, *rims, qkv_core, *mod, qkv_weight, out_weight, cross_q)


def text_kernel(text, first, parts, rows, column_ref, h1, cq, t0, t1, t2, t3, wc_hbm, *rest):
    outs = rest[: len(parts)]
    q_s, h_s, kv_s, wc_s, p_a, p_b, attn_s, bad_s, sems = rest[len(parts) :]
    count, width = q_s.shape
    waits = begin([(cq.at[pl.ds(first, count)], q_s)], sems, 0)
    pairs = []
    for k, arrived in enumerate((t0, t1, t2, t3)):
        size = arrived.shape[1]
        where = pl.multiple_of(lax.rem(column_ref[0] + k, 4) * size, size)
        for j in range(2):
            pairs.append((arrived.at[j], kv_s.at[j, pl.ds(where, size), :]))
    waits += begin(pairs, sems, 1)
    waits_later = begin([(wc_hbm, wc_s), (h1.at[pl.ds(first, count)], h_s)], sems, 9)
    finish_all(waits)
    attend_text(width // HEADS, text, q_s, kv_s, (p_a, p_b), bad_s, rows, attn_s)
    finish_all(waits_later)
    at = 0
    for out, n in zip(outs, parts):
        at_end = at + n
        made = jnp.dot(attn_s[at:at_end, :], wc_s[...], preferred_element_type=F32)
        out[...] = (h_s[at:at_end, :] + made).astype(BF16)
        at = at_end


def tile_text(text, first, parts, column, h1, cq, arrived, weight):
    count = sum(parts)
    width = h1.shape[1]
    padded = arrived[0].shape[2]
    return pl.pallas_call(
        functools.partial(text_kernel, text, first, parts, count),
        out_shape=[jax.ShapeDtypeStruct((n, width), BF16) for n in parts],
        in_specs=[pl.BlockSpec(memory_space=pltpu.SMEM)] + [ANY] * 7,
        out_specs=[LOCAL] * len(parts),
        scratch_shapes=[
            pltpu.VMEM((count, width), BF16),
            pltpu.VMEM((count, width), F32),
            pltpu.VMEM((2, width, padded), BF16),
            pltpu.VMEM((width, width), BF16),
            pltpu.VMEM((count, 2 * padded), BF16),
            pltpu.VMEM((count, 2 * padded), BF16),
            pltpu.VMEM((count, width), BF16),
            pltpu.VMEM((1, LANES), F32),
            pltpu.SemaphoreType.DMA((11,)),
        ],
        compiler_params=pltpu.CompilerParams(vmem_limit_bytes=VMEM),
        cost_estimate=pl.CostEstimate(
            flops=16 * count * width * padded + 2 * count * width * width,
            bytes_accessed=2 * width * (width + 2 * padded) + 8 * count * width,
            transcendentals=HEADS * count * padded,
        ),
    )(column, h1, cq, *arrived, weight)


def merge_kernel(lat_count, lat_ref, near, far, dn_near, dn_far, up_near, up_far, out_ref):
    step = pl.program_id(0)
    last = pl.num_programs(0) - 1
    lat = lat_ref[0]
    low = jnp.where(step == 0, 1.0, 0.0)
    high = jnp.where(step == last, 1.0, 0.0)
    shared = ((step == 0) & (lat > 0)) | ((step == last) & (lat < lat_count - 1))
    scale = jnp.where(shared, 0.5, 1.0)

    def total(body, dn, up):
        return (body[...].astype(F32) + low * dn[...].astype(F32) + high * up[...].astype(F32)) * scale

    a, b = total(near, dn_near, up_near), total(far, dn_far, up_far)
    out_ref[...] = jnp.concatenate([a[:, :8], (a[:, 8:] + b[:, :8]) * 0.5, b[:, 8:]], axis=1).astype(BF16)


def merge(lat_count, lat, core, rim, near, far, down, down_left, up, up_left):
    span, width = near.shape[1:]
    whole = pl.BlockSpec((rim, span, width), lambda i: (0, 0, 0))
    rows = pl.BlockSpec((rim, span, width), lambda i: (i, 0, 0))
    return pl.pallas_call(
        functools.partial(merge_kernel, lat_count),
        out_shape=jax.ShapeDtypeStruct((core, core, width), BF16),
        grid=(core // rim,),
        in_specs=[pl.BlockSpec(memory_space=pltpu.SMEM), rows, rows, whole, whole, whole, whole],
        out_specs=pl.BlockSpec((rim, core, width), lambda i: (i, 0, 0)),
        cost_estimate=pl.CostEstimate(
            flops=4 * core * core * width, bytes_accessed=8 * core * core * width, transcendentals=0
        ),
    )(lat, near, far, down, down_left, up, up_left)


def send(value, mesh_sizes, down, right):
    rows, cols = mesh_sizes
    pairs = [
        (r * cols + c, (r + down) * cols + (c + right) % cols)
        for r in range(rows)
        for c in range(cols)
        if 0 <= r + down < rows
    ]
    return lax.ppermute(value, ("lat", "lon"), pairs)


def local(
    sizes,
    hidden,
    timestep,
    context,
    time_weight,
    modulation_bias,
    qkv_weight,
    out_weight,
    cross_q,
    cross_kv,
    cross_output_projection,
):
    core, width = hidden.shape[1], hidden.shape[3]
    half = core // 2
    rim = HALO
    text = context.shape[1]
    lon_count = sizes[1]
    lon = lax.axis_index("lon")
    to = functools.partial(send, mesh_sizes=sizes)
    q_factor = math.log2(math.e) / math.sqrt(width // HEADS)

    def among(value, partner):
        return lax.ppermute(value, "lon", [(partner(i), i) for i in range(lon_count)])

    padded = jnp.pad(context[0], ((0, TEXT_PAD - text), (0, 0)))
    own_head = jnp.einsum("td,sde->set", padded, cross_kv, preferred_element_type=F32).astype(BF16)
    x = hidden[0]
    x, own_head = lax.optimization_barrier((x, own_head))
    other = among(own_head, lambda i: i ^ 1)
    left = to(x[:, core - rim :].reshape(-1, width), down=0, right=1)
    right = to(x[:, :rim].reshape(-1, width), down=0, right=-1)

    def joined(bit, mine, theirs):
        low = (lon // bit) % 2 == 0
        return jnp.concatenate([jnp.where(low, mine, theirs), jnp.where(low, theirs, mine)], axis=1)

    two = joined(1, own_head, other)
    four = joined(2, two, among(two, lambda i: i ^ 2))
    arrived = [four] + [among(four, lambda i, k=k: (i + 4 * k) % lon_count) for k in (1, 2, 3)]
    column = (lon // 4).astype(jnp.int32)[None]

    shift, scale, gate = modulation(timestep, time_weight, modulation_bias)
    x_core = x.reshape(core * core, width)
    qkv_core = core_qkv(q_factor, x_core, shift, scale, qkv_weight)

    corner = rim * rim
    low_edge = jnp.concatenate([left[-corner:], x[core - rim :].reshape(-1, width), right[-corner:]], axis=0)
    high_edge = jnp.concatenate([left[:corner], x[:rim].reshape(-1, width), right[:corner]], axis=0)
    top = to(low_edge, down=1, right=0)
    bottom = to(high_edge, down=-1, right=0)

    h1, cq = tile_self(
        core,
        rim,
        q_factor,
        x_core,
        (left, right, top, bottom),
        qkv_core,
        (shift, scale, gate),
        qkv_weight,
        out_weight,
        cross_q,
    )
    span = half + rim
    block, edge = core * span, rim * span
    main, top_left, bottom_left, top_right, bottom_right = tile_text(
        text, 0, (block, edge, edge, edge, edge), column, h1, cq, arrived, cross_output_projection
    )
    far = to(main, down=0, right=-1)
    up_left = to(top_left, down=-1, right=-1)
    down_left = to(bottom_left, down=1, right=-1)
    up = to(top_right, down=-1, right=0)
    down = to(bottom_right, down=1, right=0)
    (near,) = tile_text(
        text, block + 4 * edge, (block,), column, h1, cq, arrived, cross_output_projection
    )
    shape = lambda a: a.reshape(-1, span, width)
    lat = lax.axis_index("lat").astype(jnp.int32)[None]
    out = merge(
        sizes[0], lat, core, rim, *(shape(a) for a in (near, far, down, down_left, up, up_left))
    )
    return out[None]


def solution(mesh):
    in_specs = (
        P(None, "lat", "lon", None),
        P(),
        P(),
        P(),
        P(),
        P(),
        P(),
        P(),
        P(None, None, "lon"),
        P(),
    )
    out_specs = P(None, "lat", "lon", None)
    sizes = (mesh.shape["lat"], mesh.shape["lon"])
    return jax.shard_map(
        functools.partial(local, sizes), mesh=mesh, in_specs=in_specs, out_specs=out_specs, check_vma=False
    )
```

```python
import functools
import math

import jax
import jax.numpy as jnp
from jax import lax
from jax.experimental import pallas as pl
from jax.experimental.pallas import tpu as pltpu
from jax.sharding import PartitionSpec as P

HEADS = 16
PAIRS = HEADS // 2
HALO = 4
LANES = 128
WIN = 256
TEXT_PAD = 384
VMEM = 60 * 1024 * 1024
NN = (((1,), (0,)), ((), ()))
NT = (((1,), (1,)), ((), ()))
BF16, F32 = jnp.bfloat16, jnp.float32
ANY = pl.BlockSpec(memory_space=pl.ANY)
LOCAL = pl.BlockSpec(memory_space=pltpu.VMEM)


def modulation(timestep, time_weight, modulation_bias):
    half = time_weight.shape[0] // 2
    freqs = jnp.exp(-math.log(10000.0) * jnp.arange(half, dtype=F32) / half)
    angle = timestep.astype(F32)[:, None] * freqs[None, :]
    embed = jnp.concatenate([jnp.cos(angle), jnp.sin(angle)], axis=1)
    embed = jax.nn.silu(embed).astype(BF16)
    mixed = jnp.dot(embed, time_weight, preferred_element_type=F32) + modulation_bias.reshape(-1)[None, :]
    width = modulation_bias.shape[1]
    return (mixed[:, :width], mixed[:, width : 2 * width], mixed[:, 2 * width :])


def begin(pairs, sems, first):
    made = [pltpu.make_async_copy(a, b, sems.at[first + n]) for n, (a, b) in enumerate(pairs)]
    for c in made:
        c.start()
    return made


def finish_all(made):
    for c in made:
        c.wait()


def normalise(x_ref, at, count, shift_ref, scale_ref, u_ref):
    rows = 32
    gain = 1.0 + scale_ref[...]
    shift = shift_ref[...]

    def norm(i, carry):
        x = x_ref[pl.ds(pl.multiple_of(at + i * rows, rows), rows), :].astype(F32)
        mean = jnp.mean(x, axis=-1, keepdims=True)
        centred = x - mean
        var = jnp.mean(centred * centred, axis=-1, keepdims=True)
        normed = centred * lax.rsqrt(var + 1e-06)
        u_ref[pl.ds(pl.multiple_of(i * rows, rows), rows), :] = (normed * gain + shift).astype(BF16)
        return carry

    lax.fori_loop(0, count // rows, norm, 0, unroll=2)


def column_parts(total, size):
    return [(c, min(size, total - c)) for c in range(0, total, size)]


def weight_pairs(w_hbm, w_s, size):
    return [
        (w_hbm.at[:, pl.ds(c, n)], w_s.at[:, pl.ds(c, n)]) for c, n in column_parts(w_hbm.shape[1], size)
    ]


def project_qkv(u_ref, w_s, waits, size, width, q_factor, out_ref, at, done=lambda c, n: None):
    count = u_ref.shape[0]
    for wait, (c, n) in zip(waits, column_parts(w_s.shape[1], size)):
        wait.wait()
        made = jnp.dot(u_ref[...], w_s[:, c : c + n], preferred_element_type=F32)
        if c < width:
            ids = lax.broadcasted_iota(jnp.int32, (1, n), 1)
            made = made * jnp.where(ids < width - c, q_factor, 1.0)
        out_ref[at : at + count, c : c + n] = made.astype(BF16)
        done(c, n)


def band(low, high, dims, axis):
    ids = lax.broadcasted_iota(jnp.int32, dims, axis)
    return ((ids >= low) & (ids < high)).astype(F32).astype(BF16)


def pair_start(t):
    return pl.multiple_of(t * LANES, LANES)


def spare_columns(t, channels):
    gap = 2 * channels - LANES
    return jnp.where(t * gap + 2 * channels <= WIN - 64, WIN - 64, 0)


def pairs_unshifted(channels, q_ref, scores, values, p_refs, bad_ref, rows, out_ref):
    count = q_ref.shape[0]
    parts = [slice(c, c + rows) for c in range(0, count, rows)]
    gap = 2 * channels - LANES

    def close(t, p_ref, v, part):
        spare = spare_columns(t, channels)
        o = lax.dot_general(p_ref[part, :], v[0], v[1], preferred_element_type=F32)
        ids = lax.broadcasted_iota(jnp.int32, (1, WIN), 1)
        sum_a = jnp.max(jnp.where((ids >= spare) & (ids < spare + 32), o, 0.0), axis=-1, keepdims=True)
        sum_b = jnp.max(jnp.where((ids >= spare + 32) & (ids < spare + 64), o, 0.0), axis=-1, keepdims=True)
        low, high = 2.0**-100, 2.0**100
        good = (sum_a >= low) & (sum_a <= high) & (sum_b >= low) & (sum_b <= high)
        bad_ref[...] = jnp.maximum(bad_ref[...], jnp.max(jnp.where(good, 0.0, 1.0), axis=0, keepdims=True))
        start = gap * t
        scale = jnp.where(ids < start + channels, 1.0 / sum_a, 1.0 / sum_b)
        cols = pl.ds(pair_start(t), WIN)
        old = out_ref[part, cols].astype(F32)
        inside = (ids >= start) & (ids < start + 2 * channels)
        out_ref[part, cols] = jnp.where(inside, o * scale, old).astype(BF16)

    def both(t, now, after):
        v = values(t, gap * t)
        for part in parts:
            scores(t + 1, gap * (t + 1), part, after)
            close(t, now, v, part)

    first, second = p_refs
    bad_ref[...] = jnp.zeros_like(bad_ref)
    for part in parts:
        scores(jnp.int32(0), jnp.int32(0), part, first)

    def step(i, carry):
        both(2 * i, first, second)
        both(2 * i + 1, second, first)
        return carry

    lax.fori_loop(0, PAIRS // 2 - 1, step, 0)
    both(jnp.int32(PAIRS - 2), first, second)
    v = values(jnp.int32(PAIRS - 1), jnp.int32(gap * (PAIRS - 1)))
    for part in parts:
        close(jnp.int32(PAIRS - 1), second, v, part)


def heads_shifted(channels, q_ref, keys, key_dims, values, value_dims, valid, out_ref):
    count, width = q_ref.shape
    rows = 64

    def one(n, carry):
        h = n // (count // rows)
        part = pl.ds(pl.multiple_of((n % (count // rows)) * rows, rows), rows)
        t = jnp.minimum((h * channels) // LANES, (width - WIN) // LANES)
        start = pair_start(t)
        offset = h * channels - start
        cols = pl.ds(start, WIN)
        q = q_ref[part, cols] * band(offset, offset + channels, (1, WIN), 1)
        s = lax.dot_general(q, keys(start), key_dims, preferred_element_type=F32)
        if valid < s.shape[1]:
            s = jnp.where(lax.broadcasted_iota(jnp.int32, s.shape, 1) < valid, s, -jnp.inf)
        p = jnp.exp2(s - jnp.max(s, axis=-1, keepdims=True))
        total = jnp.sum(p, axis=-1, keepdims=True)
        o = lax.dot_general(p.astype(BF16), values(start), value_dims, preferred_element_type=F32) / total
        ids = lax.broadcasted_iota(jnp.int32, (1, WIN), 1)
        old = out_ref[part, cols].astype(F32)
        inside = (ids >= offset) & (ids < offset + channels)
        out_ref[part, cols] = jnp.where(inside, o, old).astype(BF16)
        return carry

    lax.fori_loop(0, HEADS * (count // rows), one, 0)


def attend_self(channels, q_ref, k_ref, v_ref, vv_ref, p_refs, bad_ref, rows, out_ref):
    n = k_ref.shape[0]

    def scores(t, start, part, p_ref):
        cols = pl.ds(pair_start(t), WIN)
        q = q_ref[part, cols]
        for j in range(2):
            low = start + j * channels
            s = lax.dot_general(
                q * band(low, low + channels, (1, WIN), 1), k_ref[:, cols], NT, preferred_element_type=F32
            )
            p_ref[part, j * n : (j + 1) * n] = jnp.exp2(s).astype(BF16)

    def values(t, start):
        v = v_ref[:, pl.ds(pair_start(t), WIN)]
        spare = spare_columns(t, channels)
        for j in range(2):
            low, mark = start + j * channels, spare + 32 * j
            vv_ref[j * n : (j + 1) * n, :] = v * band(low, low + channels, (1, WIN), 1) + band(
                mark, mark + 32, (1, WIN), 1
            )
        return vv_ref[...], NN

    out_ref[...] = jnp.zeros_like(out_ref)
    pairs_unshifted(channels, q_ref, scores, values, p_refs, bad_ref, rows, out_ref)

    @pl.when(jnp.max(bad_ref[...]) > 0.0)
    def _():
        heads_shifted(
            channels,
            q_ref,
            lambda start: k_ref[:, pl.ds(start, WIN)],
            NT,
            lambda start: v_ref[:, pl.ds(start, WIN)],
            NN,
            n,
            out_ref,
        )


def attend_text(channels, text, q_ref, kv_ref, p_refs, bad_ref, rows, out_ref):
    n = kv_ref.shape[2]

    def scores(t, start, part, p_ref):
        k = kv_ref[0, pl.ds(pair_start(t), WIN), :]
        pair = [
            k * band(start + j * channels, start + (j + 1) * channels, (WIN, 1), 0) for j in range(2)
        ]
        s = lax.dot_general(
            q_ref[part, pl.ds(pair_start(t), WIN)],
            jnp.concatenate(pair, axis=1),
            NN,
            preferred_element_type=F32,
        )
        p_ref[part, :] = jnp.exp2(s).astype(BF16)

    def values(t, start):
        v = kv_ref[1, pl.ds(pair_start(t), WIN), :]
        valid = band(0, text, (1, n), 1)
        spare = spare_columns(t, channels)
        pair = [
            v * band(start + j * channels, start + (j + 1) * channels, (WIN, 1), 0)
            + band(spare + 32 * j, spare + 32 * j + 32, (WIN, 1), 0) * valid
            for j in range(2)
        ]
        return jnp.concatenate(pair, axis=1), NT

    out_ref[...] = jnp.zeros_like(out_ref)
    pairs_unshifted(channels, q_ref, scores, values, p_refs, bad_ref, rows, out_ref)

    @pl.when(jnp.max(bad_ref[...]) > 0.0)
    def _():
        heads_shifted(
            channels,
            q_ref,
            lambda start: kv_ref[0, pl.ds(start, WIN), :],
            NN,
            lambda start: kv_ref[1, pl.ds(start, WIN), :],
            NT,
            text,
            out_ref,
        )


QKV_PART = 512


def core_kernel(q_factor, x_ref, shift_ref, scale_ref, w_hbm, out_hbm, u_s, w_s, out_s, sems):
    waits = begin(weight_pairs(w_hbm, w_s, QKV_PART), sems, 0)
    count, width = x_ref.shape
    normalise(x_ref, 0, count, shift_ref, scale_ref, u_s)
    sent = []

    def done(c, n):
        cols = pl.ds(c, n)
        sent.extend(begin([(out_s.at[:, cols], out_hbm.at[:, cols])], sems, 8 + len(sent)))

    project_qkv(u_s, w_s, waits, QKV_PART, width, q_factor, out_s, 0, done)
    finish_all(sent)


def core_qkv(q_factor, x, shift, scale, weight):
    count, width = x.shape
    total = weight.shape[1]
    return pl.pallas_call(
        functools.partial(core_kernel, q_factor),
        out_shape=jax.ShapeDtypeStruct((count, total), BF16),
        in_specs=[LOCAL, LOCAL, LOCAL, ANY],
        out_specs=ANY,
        scratch_shapes=[
            pltpu.VMEM((count, width), BF16),
            pltpu.VMEM((width, total), BF16),
            pltpu.VMEM((count, total), BF16),
            pltpu.SemaphoreType.DMA((16,)),
        ],
        compiler_params=pltpu.CompilerParams(vmem_limit_bytes=VMEM),
        cost_estimate=pl.CostEstimate(
            flops=2 * count * width * total,
            bytes_accessed=2 * (width * total + count * (width + total)),
            transcendentals=0,
        ),
    )(x, shift, scale, weight)


def regroup(core, rim, source_ref, target_ref):
    half = core // 2
    inner = core * core
    side = core * rim
    edge = side + 2 * rim * rim
    at = 0

    def take(*pieces):
        nonlocal at
        for start, n in pieces:
            target_ref[at : at + n, :] = source_ref[start : start + n, :]
            at += n

    for base in (inner + 2 * side, inner + 2 * side + edge):
        for a in range(rim):
            take((base + rim * a, rim), (base + rim * rim + core * a, half))
        for a in range(rim):
            take((base + rim * rim + core * a + half, half), (base + rim * rim + side + rim * a, rim))
    for r in range(core):
        take((inner + rim * r, rim), (core * r, half))
    for r in range(core):
        take((core * r + half, half), (inner + side + rim * r, rim))


def tile_kernel(
    core,
    rim,
    rows,
    text,
    q_factor,
    x_core,
    left,
    right,
    top,
    bottom,
    qkv_core,
    shift_ref,
    scale_ref,
    gate_ref,
    w_hbm,
    wo_hbm,
    wq_hbm,
    wc_hbm,
    kv_hbm,
    h1_out,
    cq_out,
    top_out,
    bottom_out,
    x_s,
    qkv_s,
    u_s,
    w_s,
    wo_s,
    wq_s,
    wc_s,
    kv_s,
    vv_s,
    p_a,
    p_b,
    attn_s,
    h1_s,
    hg_s,
    bad_s,
    sems,
):
    width = x_core.shape[1]
    channels = width // HEADS
    inner = x_core.shape[0]
    outer = sum(a.shape[0] for a in (left, right, top, bottom))
    total = inner + outer
    pairs, at = [], inner
    for part in (left, right, top, bottom):
        pairs.append((part, x_s.at[pl.ds(at, part.shape[0])]))
        at += part.shape[0]
    waits_x = begin(pairs, sems, 0)
    waits_w = begin(weight_pairs(w_hbm, w_s, QKV_PART), sems, 4)
    waits_qkv = begin([(qkv_core, qkv_s.at[pl.ds(0, inner)])], sems, 12)
    waits_later = begin(
        [(x_core, x_s.at[pl.ds(0, inner)]), (wo_hbm, wo_s), (wq_hbm, wq_s), (wc_hbm, wc_s), (kv_hbm, kv_s)],
        sems,
        13,
    )
    finish_all(waits_x)
    normalise(x_s, inner, outer, shift_ref, scale_ref, u_s)
    project_qkv(u_s, w_s, waits_w, QKV_PART, width, q_factor, qkv_s, inner)
    finish_all(waits_qkv)
    attend_self(
        channels,
        qkv_s.at[:, pl.ds(0, width)],
        qkv_s.at[:, pl.ds(width, width)],
        qkv_s.at[:, pl.ds(2 * width, width)],
        vv_s,
        (p_a, p_b),
        bad_s,
        rows,
        attn_s,
    )
    finish_all(waits_later)
    step = total // 2
    for r in range(0, total, step):
        part = slice(r, r + step)
        mixed = jnp.dot(attn_s[part, :], wo_s[...], preferred_element_type=F32)
        h1_s[part, :] = x_s[part, :].astype(F32) + gate_ref[...] * mixed
    regroup(core, rim, h1_s, hg_s)
    edges = top_out.shape[0] + bottom_out.shape[0]
    kept = pl.ds(edges, total - edges)
    waits_h = begin([(hg_s.at[kept], h1_out)], sems, 18)
    for r in range(0, total, step):
        part = slice(r, r + step)
        made = jnp.dot(hg_s[part, :].astype(BF16), wq_s[...], preferred_element_type=F32)
        x_s[part, :] = (made * q_factor).astype(BF16)
    waits_h += begin([(x_s.at[kept], cq_out)], sems, 19)
    outer_rows = pl.ds(0, edges)
    found = attn_s.at[outer_rows]
    room = (outer_rows, pl.ds(0, 2 * kv_s.shape[2]))
    attend_text(channels, text, x_s.at[outer_rows], kv_s, (p_a.at[room], p_b.at[room]), bad_s, edges, found)
    made = hg_s[:edges, :] + jnp.dot(found[...], wc_s[...], preferred_element_type=F32)
    top_out[...] = made[: edges // 2].astype(BF16)
    bottom_out[...] = made[edges // 2 :].astype(BF16)
    finish_all(waits_h)


def tile_self(core, rim, text, q_factor, x_core, rims, qkv_core, mod, weights, text_kv):
    inner, width = x_core.shape
    outer = sum(a.shape[0] for a in rims)
    total = inner + outer
    wide = weights[0].shape[1]
    edge = rim * (core + 2 * rim)
    kept = total - 2 * edge
    return pl.pallas_call(
        functools.partial(tile_kernel, core, rim, 512, text, q_factor),
        out_shape=[
            jax.ShapeDtypeStruct((kept, width), F32),
            jax.ShapeDtypeStruct((kept, width), BF16),
            jax.ShapeDtypeStruct((edge, width), BF16),
            jax.ShapeDtypeStruct((edge, width), BF16),
        ],
        in_specs=[ANY] * 6 + [LOCAL] * 3 + [ANY] * 5,
        out_specs=[ANY, ANY, LOCAL, LOCAL],
        scratch_shapes=[
            pltpu.VMEM((total, width), BF16),
            pltpu.VMEM((total, wide), BF16),
            pltpu.VMEM((outer, width), BF16),
            pltpu.VMEM((width, wide), BF16),
            pltpu.VMEM((width, width), BF16),
            pltpu.VMEM((width, width), BF16),
            pltpu.VMEM((width, width), BF16),
            pltpu.VMEM(text_kv.shape, BF16),
            pltpu.VMEM((2 * total, WIN), BF16),
            pltpu.VMEM((total, 2 * total), BF16),
            pltpu.VMEM((total, 2 * total), BF16),
            pltpu.VMEM((total, width), BF16),
            pltpu.VMEM((total, width), F32),
            pltpu.VMEM((total, width), F32),
            pltpu.VMEM((1, LANES), F32),
            pltpu.SemaphoreType.DMA((20,)),
        ],
        compiler_params=pltpu.CompilerParams(vmem_limit_bytes=VMEM),
        cost_estimate=pl.CostEstimate(
            flops=2 * outer * width * wide + 16 * total * width * total + 4 * total * width * width,
            bytes_accessed=2 * width * (wide + 2 * width) + 2 * inner * wide + 6 * total * width,
            transcendentals=HEADS * total * total,
        ),
    )(x_core, *rims, qkv_core, *mod, *weights, text_kv)


def text_kernel(text, first, h1, cq, kv_hbm, wc_hbm, *rest):
    *added, out, q_s, h_s, kv_s, wc_s, p_a, p_b, attn_s, bad_s, sems = rest
    count, width = q_s.shape
    rows = pl.ds(first, count)
    waits = begin([(cq.at[rows], q_s), (kv_hbm, kv_s)], sems, 0)
    waits_later = begin([(wc_hbm, wc_s), (h1.at[rows], h_s)], sems, 2)
    finish_all(waits)
    attend_text(width // HEADS, text, q_s, kv_s, (p_a, p_b), bad_s, count, attn_s)
    finish_all(waits_later)
    made = h_s[...] + jnp.dot(attn_s[...], wc_s[...], preferred_element_type=F32)
    if added:
        low, high = (a[a.shape[0] // 2 :, :].astype(F32) for a in added)
        n = low.shape[0]
        made = jnp.concatenate([made[:n] + low, made[n:-n], made[-n:] + high], axis=0)
    out[...] = made.astype(BF16)


def tile_text(text, first, count, h1, cq, text_kv, weight, *added):
    width = h1.shape[1]
    padded = text_kv.shape[2]
    return pl.pallas_call(
        functools.partial(text_kernel, text, first),
        out_shape=jax.ShapeDtypeStruct((count, width), BF16),
        in_specs=[ANY] * 4 + [LOCAL] * len(added),
        out_specs=LOCAL,
        scratch_shapes=[
            pltpu.VMEM((count, width), BF16),
            pltpu.VMEM((count, width), F32),
            pltpu.VMEM((2, width, padded), BF16),
            pltpu.VMEM((width, width), BF16),
            pltpu.VMEM((count, 2 * padded), BF16),
            pltpu.VMEM((count, 2 * padded), BF16),
            pltpu.VMEM((count, width), BF16),
            pltpu.VMEM((1, LANES), F32),
            pltpu.SemaphoreType.DMA((4,)),
        ],
        compiler_params=pltpu.CompilerParams(vmem_limit_bytes=VMEM),
        cost_estimate=pl.CostEstimate(
            flops=16 * count * width * padded + 2 * count * width * width,
            bytes_accessed=2 * width * (width + 2 * padded) + 8 * count * width,
            transcendentals=HEADS * count * padded,
        ),
    )(h1, cq, text_kv, weight, *added)


def merge_kernel(lat_count, rim, lat_ref, near, far, out_ref):
    lat = lat_ref[0]
    rows = near.shape[0]
    ids = lax.broadcasted_iota(jnp.int32, (rows, 1, 1), 0) + pl.program_id(0) * rows
    core = pl.num_programs(0) * rows
    shared = ((ids < rim) & (lat > 0)) | ((ids >= core - rim) & (lat < lat_count - 1))
    scale = jnp.where(shared, 0.5, 1.0)
    a, b = near[...].astype(F32) * scale, far[...].astype(F32) * scale
    out_ref[...] = jnp.concatenate([a[:, :8], (a[:, 8:] + b[:, :8]) * 0.5, b[:, 8:]], axis=1).astype(BF16)


def merge(lat_count, lat, rim, near, far):
    core, span, width = near.shape
    rows = 8
    part = pl.BlockSpec((rows, span, width), lambda i: (i, 0, 0))
    return pl.pallas_call(
        functools.partial(merge_kernel, lat_count, rim),
        out_shape=jax.ShapeDtypeStruct((core, core, width), BF16),
        grid=(core // rows,),
        in_specs=[pl.BlockSpec(memory_space=pltpu.SMEM), part, part],
        out_specs=pl.BlockSpec((rows, core, width), lambda i: (i, 0, 0)),
        cost_estimate=pl.CostEstimate(
            flops=4 * core * core * width, bytes_accessed=8 * core * core * width, transcendentals=0
        ),
    )(lat, near, far)


def send(value, mesh_sizes, down, right):
    rows, cols = mesh_sizes
    pairs = [
        (r * cols + c, (r + down) * cols + (c + right) % cols)
        for r in range(rows)
        for c in range(cols)
        if 0 <= r + down < rows
    ]
    return lax.ppermute(value, ("lat", "lon"), pairs)


def local(
    sizes,
    hidden,
    timestep,
    context,
    time_weight,
    modulation_bias,
    qkv_weight,
    out_weight,
    cross_q,
    cross_kv,
    cross_output_projection,
):
    core, width = hidden.shape[1], hidden.shape[3]
    half = core // 2
    rim = HALO
    text = context.shape[1]
    lon_count = sizes[1]
    to = functools.partial(send, mesh_sizes=sizes)
    q_factor = math.log2(math.e) / math.sqrt(width // HEADS)

    padded = jnp.pad(context[0], ((0, TEXT_PAD - text), (0, 0)))
    own_head = jnp.einsum("td,sde->set", padded, cross_kv, preferred_element_type=F32).astype(BF16)
    x = hidden[0]
    x, own_head = lax.optimization_barrier((x, own_head))
    copies = jnp.broadcast_to(own_head[None], (lon_count,) + own_head.shape)
    all_heads = lax.all_to_all(copies, "lon", 0, 0, tiled=True)
    left = to(x[:, core - rim :].reshape(-1, width), down=0, right=1)
    right = to(x[:, :rim].reshape(-1, width), down=0, right=-1)
    shift, scale, gate = modulation(timestep, time_weight, modulation_bias)
    corner = rim * rim
    low_edge = jnp.concatenate([left[-corner:], x[core - rim :].reshape(-1, width), right[-corner:]], axis=0)
    high_edge = jnp.concatenate([left[:corner], x[:rim].reshape(-1, width), right[:corner]], axis=0)
    x, low_edge, high_edge = lax.optimization_barrier((x, low_edge, high_edge))
    top = to(low_edge, down=1, right=0)
    bottom = to(high_edge, down=-1, right=0)
    x_core = x.reshape(core * core, width)
    qkv_core = core_qkv(q_factor, x_core, shift, scale, qkv_weight)
    text_kv = jnp.transpose(all_heads, (1, 0, 2, 3)).reshape(2, width, TEXT_PAD)

    h1, cq, top_made, bottom_made = tile_self(
        core,
        rim,
        text,
        q_factor,
        x_core,
        (left, right, top, bottom),
        qkv_core,
        (shift, scale, gate),
        (qkv_weight, out_weight, cross_q, cross_output_projection),
        text_kv,
    )
    span = half + rim
    block, edge = core * span, rim * span
    high = to(top_made, down=-1, right=0)
    low = to(bottom_made, down=1, right=0)
    main = tile_text(text, 0, block, h1, cq, text_kv, cross_output_projection)
    main = main.at[:edge].add(low[:edge])
    main = main.at[block - edge :].add(high[:edge])
    far = to(main, down=0, right=-1)
    near = tile_text(text, block, block, h1, cq, text_kv, cross_output_projection, low, high)
    shape = lambda a: a.reshape(core, span, width)
    lat = lax.axis_index("lat").astype(jnp.int32)[None]
    return merge(sizes[0], lat, rim, shape(near), shape(far))[None]


def solution(mesh):
    in_specs = (
        P(None, "lat", "lon", None),
        P(),
        P(),
        P(),
        P(),
        P(),
        P(),
        P(),
        P(None, None, "lon"),
        P(),
    )
    out_specs = P(None, "lat", "lon", None)
    sizes = (mesh.shape["lat"], mesh.shape["lon"])
    return jax.shard_map(
        functools.partial(local, sizes), mesh=mesh, in_specs=in_specs, out_specs=out_specs, check_vma=False
    )
```

```python
import functools
import math

import jax
import jax.numpy as jnp
from jax import lax
from jax.experimental import pallas as pl
from jax.experimental.pallas import tpu as pltpu
from jax.sharding import PartitionSpec as P

HEADS = 16
PAIRS = HEADS // 2
HALO = 4
LANES = 128
WIN = 256
TEXT_PAD = 384
VMEM = 60 * 1024 * 1024
SMALL = 30 * 1024 * 1024
NN = (((1,), (0,)), ((), ()))
NT = (((1,), (1,)), ((), ()))
BF16, F32 = jnp.bfloat16, jnp.float32
ANY = pl.BlockSpec(memory_space=pl.ANY)
LOCAL = pl.BlockSpec(memory_space=pltpu.VMEM)


def embedding(timestep, size):
    half = size // 2
    freqs = jnp.exp(-math.log(10000.0) * jnp.arange(half, dtype=F32) / half)
    angle = timestep.astype(F32)[:, None] * freqs[None, :]
    embed = jnp.concatenate([jnp.cos(angle), jnp.sin(angle)], axis=1)
    return jax.nn.silu(embed).astype(BF16)


def begin(pairs, sems, first):
    made = [pltpu.make_async_copy(a, b, sems.at[first + n]) for n, (a, b) in enumerate(pairs)]
    for c in made:
        c.start()
    return made


def finish_all(made):
    for c in made:
        c.wait()


def normalise(x_ref, at, count, shift_ref, scale_ref, u_ref):
    rows = 32
    gain = 1.0 + scale_ref[...]
    shift = shift_ref[...]

    def norm(i, carry):
        x = x_ref[pl.ds(pl.multiple_of(at + i * rows, rows), rows), :].astype(F32)
        mean = jnp.mean(x, axis=-1, keepdims=True)
        centred = x - mean
        var = jnp.mean(centred * centred, axis=-1, keepdims=True)
        normed = centred * lax.rsqrt(var + 1e-06)
        u_ref[pl.ds(pl.multiple_of(i * rows, rows), rows), :] = (normed * gain + shift).astype(BF16)
        return carry

    lax.fori_loop(0, count // rows, norm, 0, unroll=2)


def column_parts(total, size):
    return [(c, min(size, total - c)) for c in range(0, total, size)]


def weight_pairs(w_hbm, w_s, size):
    return [
        (w_hbm.at[:, pl.ds(c, n)], w_s.at[:, pl.ds(c, n)]) for c, n in column_parts(w_hbm.shape[1], size)
    ]


def project_qkv(u_ref, w_s, waits, size, width, q_factor, out_ref, at, done=lambda c, n: None):
    count = u_ref.shape[0]
    for wait, (c, n) in zip(waits, column_parts(w_s.shape[1], size)):
        wait.wait()
        made = jnp.dot(u_ref[...], w_s[:, c : c + n], preferred_element_type=F32)
        if c < width:
            ids = lax.broadcasted_iota(jnp.int32, (1, n), 1)
            made = made * jnp.where(ids < width - c, q_factor, 1.0)
        out_ref[at : at + count, c : c + n] = made.astype(BF16)
        done(c, n)


def band(low, high, dims, axis):
    ids = lax.broadcasted_iota(jnp.int32, dims, axis)
    return ((ids >= low) & (ids < high)).astype(F32).astype(BF16)


def pair_start(t):
    return pl.multiple_of(t * LANES, LANES)


def spare_columns(t, channels):
    gap = 2 * channels - LANES
    return jnp.where(t * gap + 2 * channels <= WIN - 64, WIN - 64, 0)


def pairs_unshifted(channels, q_ref, scores, values, p_refs, bad_ref, rows, out_ref):
    count = q_ref.shape[0]
    parts = [slice(c, c + rows) for c in range(0, count, rows)]
    gap = 2 * channels - LANES

    def close(t, p_ref, v, part):
        spare = spare_columns(t, channels)
        o = lax.dot_general(p_ref[part, :], v[0], v[1], preferred_element_type=F32)
        ids = lax.broadcasted_iota(jnp.int32, (1, WIN), 1)
        sum_a = jnp.max(jnp.where((ids >= spare) & (ids < spare + 32), o, 0.0), axis=-1, keepdims=True)
        sum_b = jnp.max(jnp.where((ids >= spare + 32) & (ids < spare + 64), o, 0.0), axis=-1, keepdims=True)
        low, high = 2.0**-100, 2.0**100
        good = (sum_a >= low) & (sum_a <= high) & (sum_b >= low) & (sum_b <= high)
        bad_ref[...] = jnp.maximum(bad_ref[...], jnp.max(jnp.where(good, 0.0, 1.0), axis=0, keepdims=True))
        start = gap * t
        scale = jnp.where(ids < start + channels, 1.0 / sum_a, 1.0 / sum_b)
        cols = pl.ds(pair_start(t), WIN)
        old = out_ref[part, cols].astype(F32)
        inside = (ids >= start) & (ids < start + 2 * channels)
        out_ref[part, cols] = jnp.where(inside, o * scale, old).astype(BF16)

    def both(t, now, after):
        v = values(t, gap * t)
        for part in parts:
            scores(t + 1, gap * (t + 1), part, after)
            close(t, now, v, part)

    first, second = p_refs
    bad_ref[...] = jnp.zeros_like(bad_ref)
    for part in parts:
        scores(jnp.int32(0), jnp.int32(0), part, first)

    def step(i, carry):
        both(2 * i, first, second)
        both(2 * i + 1, second, first)
        return carry

    lax.fori_loop(0, PAIRS // 2 - 1, step, 0)
    both(jnp.int32(PAIRS - 2), first, second)
    v = values(jnp.int32(PAIRS - 1), jnp.int32(gap * (PAIRS - 1)))
    for part in parts:
        close(jnp.int32(PAIRS - 1), second, v, part)


def heads_shifted(channels, q_ref, keys, key_dims, values, value_dims, valid, out_ref):
    count, width = q_ref.shape
    rows = 64

    def one(n, carry):
        h = n // (count // rows)
        part = pl.ds(pl.multiple_of((n % (count // rows)) * rows, rows), rows)
        t = jnp.minimum((h * channels) // LANES, (width - WIN) // LANES)
        start = pair_start(t)
        offset = h * channels - start
        cols = pl.ds(start, WIN)
        q = q_ref[part, cols] * band(offset, offset + channels, (1, WIN), 1)
        s = lax.dot_general(q, keys(start), key_dims, preferred_element_type=F32)
        if valid < s.shape[1]:
            s = jnp.where(lax.broadcasted_iota(jnp.int32, s.shape, 1) < valid, s, -jnp.inf)
        p = jnp.exp2(s - jnp.max(s, axis=-1, keepdims=True))
        total = jnp.sum(p, axis=-1, keepdims=True)
        o = lax.dot_general(p.astype(BF16), values(start), value_dims, preferred_element_type=F32) / total
        ids = lax.broadcasted_iota(jnp.int32, (1, WIN), 1)
        old = out_ref[part, cols].astype(F32)
        inside = (ids >= offset) & (ids < offset + channels)
        out_ref[part, cols] = jnp.where(inside, o, old).astype(BF16)
        return carry

    lax.fori_loop(0, HEADS * (count // rows), one, 0)


def attend_self(channels, q_ref, k_ref, v_ref, vv_ref, p_refs, bad_ref, rows, out_ref):
    n = k_ref.shape[0]

    def scores(t, start, part, p_ref):
        cols = pl.ds(pair_start(t), WIN)
        q = q_ref[part, cols]
        for j in range(2):
            low = start + j * channels
            s = lax.dot_general(
                q * band(low, low + channels, (1, WIN), 1), k_ref[:, cols], NT, preferred_element_type=F32
            )
            p_ref[part, j * n : (j + 1) * n] = jnp.exp2(s).astype(BF16)

    def values(t, start):
        v = v_ref[:, pl.ds(pair_start(t), WIN)]
        spare = spare_columns(t, channels)
        for j in range(2):
            low, mark = start + j * channels, spare + 32 * j
            vv_ref[j * n : (j + 1) * n, :] = v * band(low, low + channels, (1, WIN), 1) + band(
                mark, mark + 32, (1, WIN), 1
            )
        return vv_ref[...], NN

    out_ref[...] = jnp.zeros_like(out_ref)
    pairs_unshifted(channels, q_ref, scores, values, p_refs, bad_ref, rows, out_ref)

    @pl.when(jnp.max(bad_ref[...]) > 0.0)
    def _():
        heads_shifted(
            channels,
            q_ref,
            lambda start: k_ref[:, pl.ds(start, WIN)],
            NT,
            lambda start: v_ref[:, pl.ds(start, WIN)],
            NN,
            n,
            out_ref,
        )


def attend_text(channels, text, q_ref, kv_ref, p_refs, bad_ref, rows, out_ref):
    n = kv_ref.shape[1] // 2

    def scores(t, start, part, p_ref):
        k = kv_ref[pl.ds(pair_start(t), WIN), :n]
        pair = [
            k * band(start + j * channels, start + (j + 1) * channels, (WIN, 1), 0) for j in range(2)
        ]
        s = lax.dot_general(
            q_ref[part, pl.ds(pair_start(t), WIN)],
            jnp.concatenate(pair, axis=1),
            NN,
            preferred_element_type=F32,
        )
        p_ref[part, :] = jnp.exp2(s).astype(BF16)

    def values(t, start):
        v = kv_ref[pl.ds(pair_start(t), WIN), n:]
        valid = band(0, text, (1, n), 1)
        spare = spare_columns(t, channels)
        pair = [
            v * band(start + j * channels, start + (j + 1) * channels, (WIN, 1), 0)
            + band(spare + 32 * j, spare + 32 * j + 32, (WIN, 1), 0) * valid
            for j in range(2)
        ]
        return jnp.concatenate(pair, axis=1), NT

    out_ref[...] = jnp.zeros_like(out_ref)
    pairs_unshifted(channels, q_ref, scores, values, p_refs, bad_ref, rows, out_ref)

    @pl.when(jnp.max(bad_ref[...]) > 0.0)
    def _():
        heads_shifted(
            channels,
            q_ref,
            lambda start: kv_ref[pl.ds(start, WIN), :n],
            NN,
            lambda start: kv_ref[pl.ds(start, WIN), n:],
            NT,
            text,
            out_ref,
        )


def prepare_kernel(emb, tw_ref, bias_ref, context_ref, kv_ref, heads_out, shift_ref, scale_ref, gate_ref, own_s, sems):
    width = bias_ref.shape[1]
    text = context_ref.shape[0]
    lanes = own_s.shape[1] // 2
    own_s[...] = jnp.zeros_like(own_s)
    for j in range(2):
        made = jnp.dot(context_ref[...], kv_ref[j], preferred_element_type=F32)
        own_s[:, j * lanes : j * lanes + text] = made.T.astype(BF16)
    sent = begin([(own_s, heads_out.at[h]) for h in range(heads_out.shape[0])], sems, 0)
    for j, out in enumerate((shift_ref, scale_ref, gate_ref)):
        cols = slice(j * width, (j + 1) * width)
        out[...] = jnp.dot(emb[...], tw_ref[:, cols], preferred_element_type=F32) + bias_ref[j : j + 1, :]
    finish_all(sent)


def prepare(copies, emb, time_weight, bias, context, cross_kv):
    width = bias.shape[1]
    channels = cross_kv.shape[2]
    return pl.pallas_call(
        prepare_kernel,
        out_shape=[jax.ShapeDtypeStruct((copies, channels, 2 * TEXT_PAD), BF16)]
        + [jax.ShapeDtypeStruct((1, width), F32)] * 3,
        in_specs=[LOCAL] * 5,
        out_specs=[ANY] + [LOCAL] * 3,
        scratch_shapes=[
            pltpu.VMEM((channels, 2 * TEXT_PAD), BF16),
            pltpu.SemaphoreType.DMA((copies,)),
        ],
        compiler_params=pltpu.CompilerParams(vmem_limit_bytes=SMALL),
        cost_estimate=pl.CostEstimate(
            flops=4 * context.shape[0] * width * channels, bytes_accessed=6 * 1024 * 1024, transcendentals=0
        ),
    )(emb, time_weight, bias, context, cross_kv)


def pack_kernel(x_ref, top_ref, bottom_ref, first_out, last_out, first_s, last_s):
    rim, core = top_ref.shape[0], x_ref.shape[0]
    rows = [(top_ref, a) for a in range(rim)] + [(x_ref, r) for r in range(core)]
    rows += [(bottom_ref, a) for a in range(rim)]
    for n, (ref, r) in enumerate(rows):
        tokens = ref[r].astype(F32)
        first_s[rim * n : rim * (n + 1), :] = tokens[:rim]
        last_s[rim * n : rim * (n + 1), :] = tokens[core - rim :]
    first_out[...] = first_s[...].astype(BF16)
    last_out[...] = last_s[...].astype(BF16)


def pack(x, top, bottom):
    rim, core, width = top.shape
    count = rim * (core + 2 * rim)
    return pl.pallas_call(
        pack_kernel,
        out_shape=[jax.ShapeDtypeStruct((count, width), BF16)] * 2,
        in_specs=[LOCAL] * 3,
        out_specs=[LOCAL] * 2,
        scratch_shapes=[pltpu.VMEM((count, width), F32)] * 2,
        compiler_params=pltpu.CompilerParams(vmem_limit_bytes=SMALL),
        cost_estimate=pl.CostEstimate(flops=0, bytes_accessed=3 * 1024 * 1024, transcendentals=0),
    )(x, top, bottom)


QKV_PART = 512


def core_kernel(q_factor, x_ref, shift_ref, scale_ref, w_hbm, out_hbm, u_s, w_s, out_s, sems):
    waits = begin(weight_pairs(w_hbm, w_s, QKV_PART), sems, 0)
    count, width = x_ref.shape
    normalise(x_ref, 0, count, shift_ref, scale_ref, u_s)
    sent = []

    def done(c, n):
        cols = pl.ds(c, n)
        sent.extend(begin([(out_s.at[:, cols], out_hbm.at[:, cols])], sems, 8 + len(sent)))

    project_qkv(u_s, w_s, waits, QKV_PART, width, q_factor, out_s, 0, done)
    finish_all(sent)


def core_qkv(q_factor, x, shift, scale, weight):
    count, width = x.shape
    total = weight.shape[1]
    return pl.pallas_call(
        functools.partial(core_kernel, q_factor),
        out_shape=jax.ShapeDtypeStruct((count, total), BF16),
        in_specs=[LOCAL, LOCAL, LOCAL, ANY],
        out_specs=ANY,
        scratch_shapes=[
            pltpu.VMEM((count, width), BF16),
            pltpu.VMEM((width, total), BF16),
            pltpu.VMEM((count, total), BF16),
            pltpu.SemaphoreType.DMA((16,)),
        ],
        compiler_params=pltpu.CompilerParams(vmem_limit_bytes=VMEM),
        cost_estimate=pl.CostEstimate(
            flops=2 * count * width * total,
            bytes_accessed=2 * (width * total + count * (width + total)),
            transcendentals=0,
        ),
    )(x, shift, scale, weight)


def regroup(core, rim, source_ref, target_ref):
    half = core // 2
    left = core * core
    right = left + rim * (core + 2 * rim)
    top = right + rim * (core + 2 * rim)
    bottom = top + rim * core
    at = 0

    def take(*pieces):
        nonlocal at
        for start, n in pieces:
            target_ref[at : at + n, :] = source_ref[start : start + n, :]
            at += n

    for base, row in ((top, 0), (bottom, rim + core)):
        for a in range(rim):
            take((left + rim * (row + a), rim), (base + core * a, half))
        for a in range(rim):
            take((base + core * a + half, half), (right + rim * (row + a), rim))
    for r in range(core):
        take((left + rim * (rim + r), rim), (core * r, half))
    for r in range(core):
        take((core * r + half, half), (right + rim * (rim + r), rim))


def tile_kernel(
    core,
    rim,
    rows,
    text,
    q_factor,
    x_core,
    left,
    right,
    top,
    bottom,
    qkv_core,
    shift_ref,
    scale_ref,
    gate_ref,
    w_hbm,
    wo_hbm,
    wq_hbm,
    wc_hbm,
    kv_hbm,
    h1_out,
    cq_out,
    top_out,
    bottom_out,
    x_s,
    qkv_s,
    u_s,
    w_s,
    wo_s,
    wq_s,
    wc_s,
    kv_s,
    vv_s,
    p_a,
    p_b,
    attn_s,
    h1_s,
    hg_s,
    bad_s,
    sems,
):
    width = x_core.shape[1]
    channels = width // HEADS
    inner = x_core.shape[0]
    outer = sum(a.shape[0] for a in (left, right, top, bottom))
    total = inner + outer
    pairs, at = [], inner
    for part in (left, right, top, bottom):
        pairs.append((part, x_s.at[pl.ds(at, part.shape[0])]))
        at += part.shape[0]
    waits_x = begin(pairs, sems, 0)
    waits_w = begin(weight_pairs(w_hbm, w_s, QKV_PART), sems, 4)
    waits_qkv = begin([(qkv_core, qkv_s.at[pl.ds(0, inner)])], sems, 12)
    waits_later = begin(
        [(x_core, x_s.at[pl.ds(0, inner)]), (wo_hbm, wo_s), (wq_hbm, wq_s), (wc_hbm, wc_s), (kv_hbm, kv_s)],
        sems,
        13,
    )
    finish_all(waits_x)
    normalise(x_s, inner, outer, shift_ref, scale_ref, u_s)
    project_qkv(u_s, w_s, waits_w, QKV_PART, width, q_factor, qkv_s, inner)
    finish_all(waits_qkv)
    attend_self(
        channels,
        qkv_s.at[:, pl.ds(0, width)],
        qkv_s.at[:, pl.ds(width, width)],
        qkv_s.at[:, pl.ds(2 * width, width)],
        vv_s,
        (p_a, p_b),
        bad_s,
        rows,
        attn_s,
    )
    finish_all(waits_later)
    step = total // 2
    for r in range(0, total, step):
        part = slice(r, r + step)
        mixed = jnp.dot(attn_s[part, :], wo_s[...], preferred_element_type=F32)
        h1_s[part, :] = x_s[part, :].astype(F32) + gate_ref[...] * mixed
    regroup(core, rim, h1_s, hg_s)
    edges = top_out.shape[0] + bottom_out.shape[0]
    kept = pl.ds(edges, total - edges)
    waits_h = begin([(hg_s.at[kept], h1_out)], sems, 18)
    for r in range(0, total, step):
        part = slice(r, r + step)
        made = jnp.dot(hg_s[part, :].astype(BF16), wq_s[...], preferred_element_type=F32)
        x_s[part, :] = (made * q_factor).astype(BF16)
    waits_h += begin([(x_s.at[kept], cq_out)], sems, 19)
    outer_rows = pl.ds(0, edges)
    found = attn_s.at[outer_rows]
    room = (outer_rows, pl.ds(0, kv_s.shape[1]))
    attend_text(channels, text, x_s.at[outer_rows], kv_s, (p_a.at[room], p_b.at[room]), bad_s, edges, found)
    made = hg_s[:edges, :] + jnp.dot(found[...], wc_s[...], preferred_element_type=F32)
    top_out[...] = made[: edges // 2].astype(BF16)
    bottom_out[...] = made[edges // 2 :].astype(BF16)
    finish_all(waits_h)


def tile_self(core, rim, text, q_factor, x_core, rims, qkv_core, mod, weights, text_kv):
    inner, width = x_core.shape
    outer = sum(a.shape[0] for a in rims)
    total = inner + outer
    wide = weights[0].shape[1]
    edge = rim * (core + 2 * rim)
    kept = total - 2 * edge
    return pl.pallas_call(
        functools.partial(tile_kernel, core, rim, 512, text, q_factor),
        out_shape=[
            jax.ShapeDtypeStruct((kept, width), F32),
            jax.ShapeDtypeStruct((kept, width), BF16),
            jax.ShapeDtypeStruct((edge, width), BF16),
            jax.ShapeDtypeStruct((edge, width), BF16),
        ],
        in_specs=[ANY] * 6 + [LOCAL] * 3 + [ANY] * 5,
        out_specs=[ANY, ANY, LOCAL, LOCAL],
        scratch_shapes=[
            pltpu.VMEM((total, width), BF16),
            pltpu.VMEM((total, wide), BF16),
            pltpu.VMEM((outer, width), BF16),
            pltpu.VMEM((width, wide), BF16),
            pltpu.VMEM((width, width), BF16),
            pltpu.VMEM((width, width), BF16),
            pltpu.VMEM((width, width), BF16),
            pltpu.VMEM(text_kv.shape, BF16),
            pltpu.VMEM((2 * total, WIN), BF16),
            pltpu.VMEM((total, 2 * total), BF16),
            pltpu.VMEM((total, 2 * total), BF16),
            pltpu.VMEM((total, width), BF16),
            pltpu.VMEM((total, width), F32),
            pltpu.VMEM((total, width), F32),
            pltpu.VMEM((1, LANES), F32),
            pltpu.SemaphoreType.DMA((20,)),
        ],
        compiler_params=pltpu.CompilerParams(vmem_limit_bytes=VMEM),
        cost_estimate=pl.CostEstimate(
            flops=2 * outer * width * wide + 16 * total * width * total + 4 * total * width * width,
            bytes_accessed=2 * width * (wide + 2 * width) + 2 * inner * wide + 6 * total * width,
            transcendentals=HEADS * total * total,
        ),
    )(x_core, *rims, qkv_core, *mod, *weights, text_kv)


def text_kernel(text, first, h1, cq, kv_hbm, wc_hbm, *rest):
    *added, out, q_s, h_s, kv_s, wc_s, p_a, p_b, attn_s, bad_s, sems = rest
    count, width = q_s.shape
    rows = pl.ds(first, count)
    waits = begin([(cq.at[rows], q_s), (kv_hbm, kv_s)], sems, 0)
    waits_later = begin([(wc_hbm, wc_s), (h1.at[rows], h_s)], sems, 2)
    finish_all(waits)
    attend_text(width // HEADS, text, q_s, kv_s, (p_a, p_b), bad_s, count, attn_s)
    finish_all(waits_later)
    made = h_s[...] + jnp.dot(attn_s[...], wc_s[...], preferred_element_type=F32)
    if added:
        low, high = (a[a.shape[0] // 2 :, :].astype(F32) for a in added)
        n = low.shape[0]
        made = jnp.concatenate([made[:n] + low, made[n:-n], made[-n:] + high], axis=0)
    out[...] = made.astype(BF16)


def tile_text(text, first, count, h1, cq, text_kv, weight, *added):
    width = h1.shape[1]
    padded = text_kv.shape[1] // 2
    return pl.pallas_call(
        functools.partial(text_kernel, text, first),
        out_shape=jax.ShapeDtypeStruct((count, width), BF16),
        in_specs=[ANY] * 4 + [LOCAL] * len(added),
        out_specs=LOCAL,
        scratch_shapes=[
            pltpu.VMEM((count, width), BF16),
            pltpu.VMEM((count, width), F32),
            pltpu.VMEM(text_kv.shape, BF16),
            pltpu.VMEM((width, width), BF16),
            pltpu.VMEM((count, 2 * padded), BF16),
            pltpu.VMEM((count, 2 * padded), BF16),
            pltpu.VMEM((count, width), BF16),
            pltpu.VMEM((1, LANES), F32),
            pltpu.SemaphoreType.DMA((4,)),
        ],
        compiler_params=pltpu.CompilerParams(vmem_limit_bytes=VMEM),
        cost_estimate=pl.CostEstimate(
            flops=16 * count * width * padded + 2 * count * width * width,
            bytes_accessed=2 * width * (width + 2 * padded) + 8 * count * width,
            transcendentals=HEADS * count * padded,
        ),
    )(h1, cq, text_kv, weight, *added)


def patch_kernel(low, high, main_in, main_out, first_s, last_s, sems):
    del main_in
    n = first_s.shape[0]
    count = main_out.shape[0]
    ends = [(main_out.at[pl.ds(0, n)], first_s, low), (main_out.at[pl.ds(count - n, n)], last_s, high)]
    finish_all(begin([(ref, room) for ref, room, _ in ends], sems, 0))
    for _, room, add in ends:
        room[...] = (room[...].astype(F32) + add[:n, :].astype(F32)).astype(BF16)
    finish_all(begin([(room, ref) for ref, room, _ in ends], sems, 2))


def patch(low, high, main):
    n, width = low.shape[0] // 2, low.shape[1]
    return pl.pallas_call(
        patch_kernel,
        out_shape=jax.ShapeDtypeStruct(main.shape, BF16),
        in_specs=[LOCAL, LOCAL, ANY],
        out_specs=ANY,
        input_output_aliases={2: 0},
        scratch_shapes=[
            pltpu.VMEM((n, width), BF16),
            pltpu.VMEM((n, width), BF16),
            pltpu.SemaphoreType.DMA((4,)),
        ],
        compiler_params=pltpu.CompilerParams(vmem_limit_bytes=SMALL),
        cost_estimate=pl.CostEstimate(flops=0, bytes_accessed=8 * n * width, transcendentals=0),
    )(low, high, main)


def merge_kernel(lat_count, rim, lat_ref, near, far, out_hbm, near_s, out_s, sems):
    lat = lat_ref[0]
    core = near.shape[0]
    rows = 8
    steps = range(core // rows)
    waits = begin([(near.at[pl.ds(i * rows, rows)], near_s.at[pl.ds(i * rows, rows)]) for i in steps], sems, 0)
    sent = []
    for i in steps:
        waits[i].wait()
        part = slice(i * rows, (i + 1) * rows)
        ids = lax.broadcasted_iota(jnp.int32, (rows, 1, 1), 0) + i * rows
        shared = ((ids < rim) & (lat > 0)) | ((ids >= core - rim) & (lat < lat_count - 1))
        scale = jnp.where(shared, 0.5, 1.0)
        a, b = near_s[part].astype(F32) * scale, far[part].astype(F32) * scale
        made = jnp.concatenate([a[:, :8], (a[:, 8:] + b[:, :8]) * 0.5, b[:, 8:]], axis=1)
        out_s[part] = made.astype(BF16)
        here = pl.ds(i * rows, rows)
        sent += begin([(out_s.at[here], out_hbm.at[here])], sems, len(steps) + i)
    finish_all(sent)


def merge(lat_count, lat, rim, near, far):
    core, span, width = near.shape
    return pl.pallas_call(
        functools.partial(merge_kernel, lat_count, rim),
        out_shape=jax.ShapeDtypeStruct((core, core, width), BF16),
        in_specs=[pl.BlockSpec(memory_space=pltpu.SMEM), ANY, LOCAL],
        out_specs=ANY,
        scratch_shapes=[
            pltpu.VMEM((core, span, width), BF16),
            pltpu.VMEM((core, core, width), BF16),
            pltpu.SemaphoreType.DMA((6,)),
        ],
        compiler_params=pltpu.CompilerParams(vmem_limit_bytes=SMALL),
        cost_estimate=pl.CostEstimate(
            flops=4 * core * core * width, bytes_accessed=8 * core * core * width, transcendentals=0
        ),
    )(lat, near, far)


def send(value, mesh_sizes, down, right):
    rows, cols = mesh_sizes
    pairs = [
        (r * cols + c, (r + down) * cols + (c + right) % cols)
        for r in range(rows)
        for c in range(cols)
        if 0 <= r + down < rows
    ]
    return lax.ppermute(value, ("lat", "lon"), pairs)


def local(
    sizes,
    hidden,
    timestep,
    context,
    time_weight,
    modulation_bias,
    qkv_weight,
    out_weight,
    cross_q,
    cross_kv,
    cross_output_projection,
):
    core, width = hidden.shape[1], hidden.shape[3]
    half = core // 2
    rim = HALO
    text = context.shape[1]
    lon_count = sizes[1]
    to = functools.partial(send, mesh_sizes=sizes)
    q_factor = math.log2(math.e) / math.sqrt(width // HEADS)

    x = hidden[0]
    flat = lambda a: a.reshape(-1, width)
    top = to(flat(x[core - rim :]), down=1, right=0)
    bottom = to(flat(x[:rim]), down=-1, right=0)
    emb = embedding(timestep, time_weight.shape[0])
    copies, shift, scale, gate = prepare(lon_count, emb, time_weight, modulation_bias, context[0], cross_kv)
    text_kv = lax.all_to_all(copies, "lon", 0, 0, tiled=True).reshape(width, 2 * TEXT_PAD)
    rows = lambda a: a.reshape(rim, core, width)
    first, last = pack(x, rows(top), rows(bottom))
    left = to(last, down=0, right=1)
    right = to(first, down=0, right=-1)
    x, first, last = lax.optimization_barrier((x, first, last))
    x_core = flat(x)
    qkv_core = core_qkv(q_factor, x_core, shift, scale, qkv_weight)

    h1, cq, top_made, bottom_made = tile_self(
        core,
        rim,
        text,
        q_factor,
        x_core,
        (left, right, top, bottom),
        qkv_core,
        (shift, scale, gate),
        (qkv_weight, out_weight, cross_q, cross_output_projection),
        text_kv,
    )
    span = half + rim
    block = core * span
    high = to(top_made, down=-1, right=0)
    low = to(bottom_made, down=1, right=0)
    main = tile_text(text, 0, block, h1, cq, text_kv, cross_output_projection)
    far = to(patch(low, high, main), down=0, right=-1)
    near = tile_text(text, block, block, h1, cq, text_kv, cross_output_projection, low, high)
    shape = lambda a: a.reshape(core, span, width)
    lat = lax.axis_index("lat").astype(jnp.int32)[None]
    return merge(sizes[0], lat, rim, shape(near), shape(far))[None]


def solution(mesh):
    in_specs = (
        P(None, "lat", "lon", None),
        P(),
        P(),
        P(),
        P(),
        P(),
        P(),
        P(),
        P(None, None, "lon"),
        P(),
    )
    out_specs = P(None, "lat", "lon", None)
    sizes = (mesh.shape["lat"], mesh.shape["lon"])
    return jax.shard_map(
        functools.partial(local, sizes), mesh=mesh, in_specs=in_specs, out_specs=out_specs, check_vma=False
    )
```

```python
import functools
import math

import jax
import jax.numpy as jnp
from jax import lax
from jax.experimental import pallas as pl
from jax.experimental.pallas import tpu as pltpu
from jax.sharding import PartitionSpec as P

HEADS = 16
PAIRS = HEADS // 2
HALO = 4
LANES = 128
WIN = 256
TEXT_PAD = 384
VMEM = 60 * 1024 * 1024
SMALL = 30 * 1024 * 1024
NN = (((1,), (0,)), ((), ()))
NT = (((1,), (1,)), ((), ()))
BF16, F32 = jnp.bfloat16, jnp.float32
ANY = pl.BlockSpec(memory_space=pl.ANY)
LOCAL = pl.BlockSpec(memory_space=pltpu.VMEM)


def embedding(timestep, size):
    half = size // 2
    freqs = jnp.exp(-math.log(10000.0) * jnp.arange(half, dtype=F32) / half)
    angle = timestep.astype(F32)[:, None] * freqs[None, :]
    embed = jnp.concatenate([jnp.cos(angle), jnp.sin(angle)], axis=1)
    return jax.nn.silu(embed).astype(BF16)


def begin(pairs, sems, first):
    made = [pltpu.make_async_copy(a, b, sems.at[first + n]) for n, (a, b) in enumerate(pairs)]
    for c in made:
        c.start()
    return made


def finish_all(made):
    for c in made:
        c.wait()


def normalise(x_ref, at, count, mod_ref, u_ref):
    rows = 32
    blocks = count // rows
    gain = 1.0 + mod_ref[1:2, :]
    shift = mod_ref[0:1, :]

    def norm(i, carry):
        x = x_ref[pl.ds(pl.multiple_of(at + i * rows, rows), rows), :].astype(F32)
        mean = jnp.mean(x, axis=-1, keepdims=True)
        centred = x - mean
        var = jnp.mean(centred * centred, axis=-1, keepdims=True)
        normed = centred * lax.rsqrt(var + 1e-06)
        u_ref[pl.ds(pl.multiple_of(i * rows, rows), rows), :] = (normed * gain + shift).astype(BF16)
        return carry

    lax.fori_loop(0, blocks, norm, 0, unroll=next(n for n in (7, 6, 4, 2, 1) if blocks % n == 0))


def column_parts(total, size):
    return [(c, min(size, total - c)) for c in range(0, total, size)]


def weight_pairs(w_hbm, w_s, size):
    return [
        (w_hbm.at[:, pl.ds(c, n)], w_s.at[:, pl.ds(c, n)]) for c, n in column_parts(w_hbm.shape[1], size)
    ]


def project_qkv(u_ref, w_s, waits, size, width, q_factor, out_ref, at, done=lambda c, n: None):
    count = u_ref.shape[0]
    for wait, (c, n) in zip(waits, column_parts(w_s.shape[1], size)):
        wait.wait()
        made = jnp.dot(u_ref[...], w_s[:, c : c + n], preferred_element_type=F32)
        if c < width:
            ids = lax.broadcasted_iota(jnp.int32, (1, n), 1)
            made = made * jnp.where(ids < width - c, q_factor, 1.0)
        out_ref[at : at + count, c : c + n] = made.astype(BF16)
        done(c, n)


def band(low, high, dims, axis):
    ids = lax.broadcasted_iota(jnp.int32, dims, axis)
    return ((ids >= low) & (ids < high)).astype(F32).astype(BF16)


def pair_start(t):
    return t * LANES


def spare_columns(t, channels):
    return WIN - 64 if t * (2 * channels - LANES) + 2 * channels <= WIN - 64 else 0


def reciprocal(x):
    r = pl.reciprocal(x, approx=True)
    return r * (2.0 - x * r)


def pairs_unshifted(channels, q_ref, scores, values, p_refs, bad_ref, rows, out_ref):
    count = q_ref.shape[0]
    parts = [slice(c, c + rows) for c in range(0, count, rows)]
    gap = 2 * channels - LANES

    def close(t, p_ref, v, part):
        spare = spare_columns(t, channels)
        o = lax.dot_general(p_ref[part, :], v[0], v[1], preferred_element_type=F32)
        ids = lax.broadcasted_iota(jnp.int32, (1, WIN), 1)
        sum_a = o[:, spare : spare + 1]
        sum_b = o[:, spare + 32 : spare + 33]
        low, high = 2.0**-100, 2.0**100
        good = (sum_a >= low) & (sum_a <= high) & (sum_b >= low) & (sum_b <= high)
        bad_ref[...] = jnp.maximum(bad_ref[...], jnp.max(jnp.where(good, 0.0, 1.0), axis=0, keepdims=True))
        start = gap * t
        scale = jnp.where(ids < start + channels, reciprocal(sum_a), reciprocal(sum_b))
        cols = pl.ds(pair_start(t), WIN)
        old = out_ref[part, cols].astype(F32)
        inside = (ids >= start) & (ids < start + 2 * channels)
        out_ref[part, cols] = jnp.where(inside, o * scale, old).astype(BF16)

    bad_ref[...] = jnp.zeros_like(bad_ref)
    for part in parts:
        scores(0, 0, part, p_refs[0])
    for t in range(PAIRS):
        v = values(t, gap * t)
        for part in parts:
            if t + 1 < PAIRS:
                scores(t + 1, gap * (t + 1), part, p_refs[(t + 1) % 2])
            close(t, p_refs[t % 2], v, part)


def heads_shifted(channels, q_ref, keys, key_dims, values, value_dims, valid, out_ref):
    count, width = q_ref.shape
    rows = 64

    def one(n, carry):
        h = n // (count // rows)
        part = pl.ds(pl.multiple_of((n % (count // rows)) * rows, rows), rows)
        t = jnp.minimum((h * channels) // LANES, (width - WIN) // LANES)
        start = pl.multiple_of(t * LANES, LANES)
        offset = h * channels - start
        cols = pl.ds(start, WIN)
        q = q_ref[part, cols] * band(offset, offset + channels, (1, WIN), 1)
        s = lax.dot_general(q, keys(start), key_dims, preferred_element_type=F32)
        if valid < s.shape[1]:
            s = jnp.where(lax.broadcasted_iota(jnp.int32, s.shape, 1) < valid, s, -jnp.inf)
        p = jnp.exp2(s - jnp.max(s, axis=-1, keepdims=True))
        total = jnp.sum(p, axis=-1, keepdims=True)
        o = lax.dot_general(p.astype(BF16), values(start), value_dims, preferred_element_type=F32) / total
        ids = lax.broadcasted_iota(jnp.int32, (1, WIN), 1)
        old = out_ref[part, cols].astype(F32)
        inside = (ids >= offset) & (ids < offset + channels)
        out_ref[part, cols] = jnp.where(inside, o, old).astype(BF16)
        return carry

    lax.fori_loop(0, HEADS * (count // rows), one, 0)


def attend_self(channels, q_ref, k_ref, v_ref, vv_ref, p_refs, bad_ref, rows, out_ref):
    n = k_ref.shape[0]

    def scores(t, start, part, p_ref):
        cols = pl.ds(pair_start(t), WIN)
        q = q_ref[part, cols]
        for j in range(2):
            low = start + j * channels
            s = lax.dot_general(
                q * band(low, low + channels, (1, WIN), 1), k_ref[:, cols], NT, preferred_element_type=F32
            )
            p_ref[part, j * n : (j + 1) * n] = jnp.exp2(s).astype(BF16)

    def values(t, start):
        v = v_ref[:, pl.ds(pair_start(t), WIN)]
        spare = spare_columns(t, channels)
        for j in range(2):
            low, mark = start + j * channels, spare + 32 * j
            vv_ref[j * n : (j + 1) * n, :] = v * band(low, low + channels, (1, WIN), 1) + band(
                mark, mark + 32, (1, WIN), 1
            )
        return vv_ref[...], NN

    pairs_unshifted(channels, q_ref, scores, values, p_refs, bad_ref, rows, out_ref)

    @pl.when(jnp.max(bad_ref[...]) > 0.0)
    def _():
        heads_shifted(
            channels,
            q_ref,
            lambda start: k_ref[:, pl.ds(start, WIN)],
            NT,
            lambda start: v_ref[:, pl.ds(start, WIN)],
            NN,
            n,
            out_ref,
        )


def attend_text(channels, text, q_ref, kv_ref, p_refs, bad_ref, rows, out_ref):
    n = kv_ref.shape[1] // 2

    def scores(t, start, part, p_ref):
        k = kv_ref[pl.ds(pair_start(t), WIN), :n]
        pair = [
            k * band(start + j * channels, start + (j + 1) * channels, (WIN, 1), 0) for j in range(2)
        ]
        s = lax.dot_general(
            q_ref[part, pl.ds(pair_start(t), WIN)],
            jnp.concatenate(pair, axis=1),
            NN,
            preferred_element_type=F32,
        )
        p_ref[part, :] = jnp.exp2(s).astype(BF16)

    def values(t, start):
        v = kv_ref[pl.ds(pair_start(t), WIN), n:]
        valid = band(0, text, (1, n), 1)
        spare = spare_columns(t, channels)
        pair = [
            v * band(start + j * channels, start + (j + 1) * channels, (WIN, 1), 0)
            + band(spare + 32 * j, spare + 32 * j + 32, (WIN, 1), 0) * valid
            for j in range(2)
        ]
        return jnp.concatenate(pair, axis=1), NT

    pairs_unshifted(channels, q_ref, scores, values, p_refs, bad_ref, rows, out_ref)

    @pl.when(jnp.max(bad_ref[...]) > 0.0)
    def _():
        heads_shifted(
            channels,
            q_ref,
            lambda start: kv_ref[pl.ds(start, WIN), :n],
            NN,
            lambda start: kv_ref[pl.ds(start, WIN), n:],
            NT,
            text,
            out_ref,
        )


def prepare_kernel(emb, bias_ref, tw_hbm, context_hbm, kv_ref, heads_out, mod_out, tw_s, context_s, own_s, mod_s, sems):
    width = bias_ref.shape[1]
    text = context_s.shape[0]
    lanes = own_s.shape[1] // 2
    waits = begin([(context_hbm, context_s), (tw_hbm, tw_s)], sems, heads_out.shape[0])
    own_s[...] = jnp.zeros_like(own_s)
    waits[0].wait()
    for j in range(2):
        made = lax.dot_general(kv_ref[j], context_s[...], NT, preferred_element_type=F32)
        own_s[:, j * lanes : j * lanes + text] = made.astype(BF16)
    sent = begin([(own_s, heads_out.at[h]) for h in range(heads_out.shape[0])], sems, 0)
    waits[1].wait()
    for j in range(3):
        cols = slice(j * width, (j + 1) * width)
        mod_s[j : j + 1, :] = (
            jnp.dot(emb[...], tw_s[:, cols], preferred_element_type=F32) + bias_ref[j : j + 1, :]
        )
    sent += begin([(mod_s, mod_out)], sems, heads_out.shape[0] + 2)
    finish_all(sent)


def prepare(copies, emb, time_weight, bias, context, cross_kv):
    width = bias.shape[1]
    channels = cross_kv.shape[1]
    return pl.pallas_call(
        prepare_kernel,
        out_shape=[
            jax.ShapeDtypeStruct((copies, channels, 2 * TEXT_PAD), BF16),
            jax.ShapeDtypeStruct(bias.shape, F32),
        ],
        in_specs=[LOCAL, LOCAL, ANY, ANY, LOCAL],
        out_specs=[ANY, ANY],
        scratch_shapes=[
            pltpu.VMEM(time_weight.shape, BF16),
            pltpu.VMEM(context.shape, BF16),
            pltpu.VMEM((channels, 2 * TEXT_PAD), BF16),
            pltpu.VMEM(bias.shape, F32),
            pltpu.SemaphoreType.DMA((copies + 3,)),
        ],
        compiler_params=pltpu.CompilerParams(vmem_limit_bytes=VMEM),
        cost_estimate=pl.CostEstimate(
            flops=4 * context.shape[0] * width * channels, bytes_accessed=6 * 1024 * 1024, transcendentals=0
        ),
    )(emb, bias, time_weight, context, cross_kv)


def pack_kernel(x_ref, top_ref, bottom_ref, first_out, last_out, first_s, last_s):
    rim, core = top_ref.shape[0], x_ref.shape[0]
    rows = [(top_ref, a) for a in range(rim)] + [(x_ref, r) for r in range(core)]
    rows += [(bottom_ref, a) for a in range(rim)]
    for n, (ref, r) in enumerate(rows):
        tokens = ref[r].astype(F32)
        first_s[rim * n : rim * (n + 1), :] = tokens[:rim]
        last_s[rim * n : rim * (n + 1), :] = tokens[core - rim :]
    first_out[...] = first_s[...].astype(BF16)
    last_out[...] = last_s[...].astype(BF16)


def pack(x, top, bottom):
    rim, core, width = top.shape
    count = rim * (core + 2 * rim)
    return pl.pallas_call(
        pack_kernel,
        out_shape=[jax.ShapeDtypeStruct((count, width), BF16)] * 2,
        in_specs=[LOCAL] * 3,
        out_specs=[LOCAL] * 2,
        scratch_shapes=[pltpu.VMEM((count, width), F32)] * 2,
        compiler_params=pltpu.CompilerParams(vmem_limit_bytes=SMALL),
        cost_estimate=pl.CostEstimate(flops=0, bytes_accessed=3 * 1024 * 1024, transcendentals=0),
    )(x, top, bottom)


QKV_PART = 512


def core_kernel(q_factor, x_ref, mod_ref, w_hbm, out_hbm, u_s, w_s, out_s, sems):
    waits = begin(weight_pairs(w_hbm, w_s, QKV_PART), sems, 0)
    count, width = x_ref.shape
    normalise(x_ref, 0, count, mod_ref, u_s)
    sent = []

    def done(c, n):
        cols = pl.ds(c, n)
        sent.extend(begin([(out_s.at[:, cols], out_hbm.at[:, cols])], sems, 8 + len(sent)))

    project_qkv(u_s, w_s, waits, QKV_PART, width, q_factor, out_s, 0, done)
    finish_all(sent)


def core_qkv(q_factor, x, mod, weight):
    count, width = x.shape
    total = weight.shape[1]
    return pl.pallas_call(
        functools.partial(core_kernel, q_factor),
        out_shape=jax.ShapeDtypeStruct((count, total), BF16),
        in_specs=[LOCAL, LOCAL, ANY],
        out_specs=ANY,
        scratch_shapes=[
            pltpu.VMEM((count, width), BF16),
            pltpu.VMEM((width, total), BF16),
            pltpu.VMEM((count, total), BF16),
            pltpu.SemaphoreType.DMA((16,)),
        ],
        compiler_params=pltpu.CompilerParams(vmem_limit_bytes=VMEM),
        cost_estimate=pl.CostEstimate(
            flops=2 * count * width * total,
            bytes_accessed=2 * (width * total + count * (width + total)),
            transcendentals=0,
        ),
    )(x, mod, weight)


def regroup(core, rim, source_ref, target_ref):
    half = core // 2
    left = core * core
    right = left + rim * (core + 2 * rim)
    top = right + rim * (core + 2 * rim)
    bottom = top + rim * core
    at = 0

    def take(*pieces):
        nonlocal at
        for start, n in pieces:
            target_ref[at : at + n, :] = source_ref[start : start + n, :]
            at += n

    for base, row in ((top, 0), (bottom, rim + core)):
        for a in range(rim):
            take((left + rim * (row + a), rim), (base + core * a, half))
        for a in range(rim):
            take((base + core * a + half, half), (right + rim * (row + a), rim))
    for r in range(core):
        take((left + rim * (rim + r), rim), (core * r, half))
    for r in range(core):
        take((core * r + half, half), (right + rim * (rim + r), rim))


def tile_kernel(
    core,
    rim,
    rows,
    text,
    q_factor,
    x_core,
    left,
    right,
    top,
    bottom,
    qkv_core,
    mod_ref,
    w_hbm,
    wo_hbm,
    wq_hbm,
    wc_hbm,
    kv_hbm,
    h1_out,
    cq_out,
    top_out,
    bottom_out,
    x_s,
    qkv_s,
    u_s,
    w_s,
    wo_s,
    wq_s,
    wc_s,
    kv_s,
    vv_s,
    p_a,
    p_b,
    attn_s,
    h1_s,
    hg_s,
    bad_s,
    sems,
):
    width = x_core.shape[1]
    channels = width // HEADS
    inner = x_core.shape[0]
    outer = sum(a.shape[0] for a in (left, right, top, bottom))
    total = inner + outer
    pairs, at = [], inner
    for part in (left, right, top, bottom):
        pairs.append((part, x_s.at[pl.ds(at, part.shape[0])]))
        at += part.shape[0]
    waits_x = begin(pairs, sems, 0)
    waits_w = begin(weight_pairs(w_hbm, w_s, QKV_PART), sems, 4)
    waits_qkv = begin([(qkv_core, qkv_s.at[pl.ds(0, inner)])], sems, 12)
    waits_later = begin(
        [(x_core, x_s.at[pl.ds(0, inner)]), (wo_hbm, wo_s), (wq_hbm, wq_s), (wc_hbm, wc_s), (kv_hbm, kv_s)],
        sems,
        13,
    )
    finish_all(waits_x)
    normalise(x_s, inner, outer, mod_ref, u_s)
    project_qkv(u_s, w_s, waits_w, QKV_PART, width, q_factor, qkv_s, inner)
    finish_all(waits_qkv)
    attend_self(
        channels,
        qkv_s.at[:, pl.ds(0, width)],
        qkv_s.at[:, pl.ds(width, width)],
        qkv_s.at[:, pl.ds(2 * width, width)],
        vv_s,
        (p_a, p_b),
        bad_s,
        rows,
        attn_s,
    )
    finish_all(waits_later)
    step = total // 2
    for r in range(0, total, step):
        part = slice(r, r + step)
        mixed = jnp.dot(attn_s[part, :], wo_s[...], preferred_element_type=F32)
        h1_s[part, :] = x_s[part, :].astype(F32) + mod_ref[2:3, :] * mixed
    regroup(core, rim, h1_s, hg_s)
    edges = top_out.shape[0] + bottom_out.shape[0]
    kept = pl.ds(edges, total - edges)
    waits_h = begin([(hg_s.at[kept], h1_out)], sems, 18)
    for r in range(0, total, step):
        part = slice(r, r + step)
        made = jnp.dot(hg_s[part, :].astype(BF16), wq_s[...], preferred_element_type=F32)
        x_s[part, :] = (made * q_factor).astype(BF16)
    waits_h += begin([(x_s.at[kept], cq_out)], sems, 19)
    outer_rows = pl.ds(0, edges)
    found = attn_s.at[outer_rows]
    room = (outer_rows, pl.ds(0, kv_s.shape[1]))
    attend_text(channels, text, x_s.at[outer_rows], kv_s, (p_a.at[room], p_b.at[room]), bad_s, edges, found)
    made = hg_s[:edges, :] + jnp.dot(found[...], wc_s[...], preferred_element_type=F32)
    top_out[...] = made[: edges // 2].astype(BF16)
    bottom_out[...] = made[edges // 2 :].astype(BF16)
    finish_all(waits_h)


def tile_self(core, rim, text, q_factor, x_core, rims, qkv_core, mod, weights, text_kv):
    inner, width = x_core.shape
    outer = sum(a.shape[0] for a in rims)
    total = inner + outer
    wide = weights[0].shape[1]
    edge = rim * (core + 2 * rim)
    kept = total - 2 * edge
    return pl.pallas_call(
        functools.partial(tile_kernel, core, rim, 256, text, q_factor),
        out_shape=[
            jax.ShapeDtypeStruct((kept, width), F32),
            jax.ShapeDtypeStruct((kept, width), BF16),
            jax.ShapeDtypeStruct((edge, width), BF16),
            jax.ShapeDtypeStruct((edge, width), BF16),
        ],
        in_specs=[ANY] * 6 + [LOCAL] + [ANY] * 5,
        out_specs=[ANY, ANY, LOCAL, LOCAL],
        scratch_shapes=[
            pltpu.VMEM((total, width), BF16),
            pltpu.VMEM((total, wide), BF16),
            pltpu.VMEM((outer, width), BF16),
            pltpu.VMEM((width, wide), BF16),
            pltpu.VMEM((width, width), BF16),
            pltpu.VMEM((width, width), BF16),
            pltpu.VMEM((width, width), BF16),
            pltpu.VMEM(text_kv.shape, BF16),
            pltpu.VMEM((2 * total, WIN), BF16),
            pltpu.VMEM((total, 2 * total), BF16),
            pltpu.VMEM((total, 2 * total), BF16),
            pltpu.VMEM((total, width), BF16),
            pltpu.VMEM((total, width), F32),
            pltpu.VMEM((total, width), F32),
            pltpu.VMEM((1, LANES), F32),
            pltpu.SemaphoreType.DMA((20,)),
        ],
        compiler_params=pltpu.CompilerParams(vmem_limit_bytes=VMEM),
        cost_estimate=pl.CostEstimate(
            flops=2 * outer * width * wide + 16 * total * width * total + 4 * total * width * width,
            bytes_accessed=2 * width * (wide + 2 * width) + 2 * inner * wide + 6 * total * width,
            transcendentals=HEADS * total * total,
        ),
    )(x_core, *rims, qkv_core, mod, *weights, text_kv)


def text_kernel(text, first, h1, cq, kv_hbm, wc_hbm, *rest):
    *added, out, q_s, h_s, kv_s, wc_s, p_a, p_b, attn_s, bad_s, sems = rest
    count, width = q_s.shape
    rows = pl.ds(first, count)
    waits = begin([(cq.at[rows], q_s), (kv_hbm, kv_s)], sems, 0)
    waits_later = begin([(wc_hbm, wc_s), (h1.at[rows], h_s)], sems, 2)
    finish_all(waits)
    attend_text(width // HEADS, text, q_s, kv_s, (p_a, p_b), bad_s, count, attn_s)
    finish_all(waits_later)
    made = h_s[...] + jnp.dot(attn_s[...], wc_s[...], preferred_element_type=F32)
    if added:
        low, high = (a[a.shape[0] // 2 :, :].astype(F32) for a in added)
        n = low.shape[0]
        made = jnp.concatenate([made[:n] + low, made[n:-n], made[-n:] + high], axis=0)
    out[...] = made.astype(BF16)


def tile_text(text, first, count, h1, cq, text_kv, weight, *added):
    width = h1.shape[1]
    padded = text_kv.shape[1] // 2
    return pl.pallas_call(
        functools.partial(text_kernel, text, first),
        out_shape=jax.ShapeDtypeStruct((count, width), BF16),
        in_specs=[ANY] * 4 + [LOCAL] * len(added),
        out_specs=LOCAL,
        scratch_shapes=[
            pltpu.VMEM((count, width), BF16),
            pltpu.VMEM((count, width), F32),
            pltpu.VMEM(text_kv.shape, BF16),
            pltpu.VMEM((width, width), BF16),
            pltpu.VMEM((count, 2 * padded), BF16),
            pltpu.VMEM((count, 2 * padded), BF16),
            pltpu.VMEM((count, width), BF16),
            pltpu.VMEM((1, LANES), F32),
            pltpu.SemaphoreType.DMA((4,)),
        ],
        compiler_params=pltpu.CompilerParams(vmem_limit_bytes=VMEM),
        cost_estimate=pl.CostEstimate(
            flops=16 * count * width * padded + 2 * count * width * width,
            bytes_accessed=2 * width * (width + 2 * padded) + 8 * count * width,
            transcendentals=HEADS * count * padded,
        ),
    )(h1, cq, text_kv, weight, *added)


def patch_kernel(low, high, main_in, main_out, first_s, last_s, sems):
    del main_in
    n = first_s.shape[0]
    count = main_out.shape[0]
    ends = [(main_out.at[pl.ds(0, n)], first_s, low), (main_out.at[pl.ds(count - n, n)], last_s, high)]
    finish_all(begin([(ref, room) for ref, room, _ in ends], sems, 0))
    for _, room, add in ends:
        room[...] = (room[...].astype(F32) + add[:n, :].astype(F32)).astype(BF16)
    finish_all(begin([(room, ref) for ref, room, _ in ends], sems, 2))


def patch(low, high, main):
    n, width = low.shape[0] // 2, low.shape[1]
    return pl.pallas_call(
        patch_kernel,
        out_shape=jax.ShapeDtypeStruct(main.shape, BF16),
        in_specs=[LOCAL, LOCAL, ANY],
        out_specs=ANY,
        input_output_aliases={2: 0},
        scratch_shapes=[
            pltpu.VMEM((n, width), BF16),
            pltpu.VMEM((n, width), BF16),
            pltpu.SemaphoreType.DMA((4,)),
        ],
        compiler_params=pltpu.CompilerParams(vmem_limit_bytes=SMALL),
        cost_estimate=pl.CostEstimate(flops=0, bytes_accessed=8 * n * width, transcendentals=0),
    )(low, high, main)


def merge_kernel(lat_count, rim, lat_ref, near, far, out_hbm, near_s, out_s, sems):
    lat = lat_ref[0]
    core = near.shape[0]
    rows = 8
    steps = range(core // rows)
    waits = begin([(near.at[pl.ds(i * rows, rows)], near_s.at[pl.ds(i * rows, rows)]) for i in steps], sems, 0)
    sent = []
    for i in steps:
        waits[i].wait()
        part = slice(i * rows, (i + 1) * rows)
        ids = lax.broadcasted_iota(jnp.int32, (rows, 1, 1), 0) + i * rows
        shared = ((ids < rim) & (lat > 0)) | ((ids >= core - rim) & (lat < lat_count - 1))
        scale = jnp.where(shared, 0.5, 1.0)
        a, b = near_s[part].astype(F32) * scale, far[part].astype(F32) * scale
        made = jnp.concatenate([a[:, :8], (a[:, 8:] + b[:, :8]) * 0.5, b[:, 8:]], axis=1)
        out_s[part] = made.astype(BF16)
        here = pl.ds(i * rows, rows)
        sent += begin([(out_s.at[here], out_hbm.at[here])], sems, len(steps) + i)
    finish_all(sent)


def merge(lat_count, lat, rim, near, far):
    core, span, width = near.shape
    return pl.pallas_call(
        functools.partial(merge_kernel, lat_count, rim),
        out_shape=jax.ShapeDtypeStruct((core, core, width), BF16),
        in_specs=[pl.BlockSpec(memory_space=pltpu.SMEM), ANY, LOCAL],
        out_specs=ANY,
        scratch_shapes=[
            pltpu.VMEM((core, span, width), BF16),
            pltpu.VMEM((core, core, width), BF16),
            pltpu.SemaphoreType.DMA((6,)),
        ],
        compiler_params=pltpu.CompilerParams(vmem_limit_bytes=SMALL),
        cost_estimate=pl.CostEstimate(
            flops=4 * core * core * width, bytes_accessed=8 * core * core * width, transcendentals=0
        ),
    )(lat, near, far)


def send(value, mesh_sizes, down, right):
    rows, cols = mesh_sizes
    pairs = [
        (r * cols + c, (r + down) * cols + (c + right) % cols)
        for r in range(rows)
        for c in range(cols)
        if 0 <= r + down < rows
    ]
    return lax.ppermute(value, ("lat", "lon"), pairs)


def local(
    sizes,
    hidden,
    timestep,
    context,
    time_weight,
    modulation_bias,
    qkv_weight,
    out_weight,
    cross_q,
    cross_kv,
    cross_output_projection,
):
    core, width = hidden.shape[1], hidden.shape[3]
    half = core // 2
    rim = HALO
    text = context.shape[1]
    lon_count = sizes[1]
    to = functools.partial(send, mesh_sizes=sizes)
    q_factor = math.log2(math.e) / math.sqrt(width // HEADS)

    x = hidden[0]
    flat = lambda a: a.reshape(-1, width)
    top = to(flat(x[core - rim :]), down=1, right=0)
    bottom = to(flat(x[:rim]), down=-1, right=0)
    emb = embedding(timestep, time_weight.shape[0])
    kv_rows = jnp.transpose(cross_kv, (0, 2, 1))
    copies, mod = prepare(lon_count, emb, time_weight, modulation_bias, context[0], kv_rows)
    copies, top, bottom = lax.optimization_barrier((copies, top, bottom))
    text_kv = lax.all_to_all(copies, "lon", 0, 0, tiled=True).reshape(width, 2 * TEXT_PAD)
    rows = lambda a: a.reshape(rim, core, width)
    first, last = pack(x, rows(top), rows(bottom))
    left = to(last, down=0, right=1)
    right = to(first, down=0, right=-1)
    x, first, last = lax.optimization_barrier((x, first, last))
    x_core = flat(x)
    qkv_core = core_qkv(q_factor, x_core, mod, qkv_weight)

    h1, cq, top_made, bottom_made = tile_self(
        core,
        rim,
        text,
        q_factor,
        x_core,
        (left, right, top, bottom),
        qkv_core,
        mod,
        (qkv_weight, out_weight, cross_q, cross_output_projection),
        text_kv,
    )
    span = half + rim
    block = core * span
    high = to(top_made, down=-1, right=0)
    low = to(bottom_made, down=1, right=0)
    main = tile_text(text, 0, block, h1, cq, text_kv, cross_output_projection)
    far = to(patch(low, high, main), down=0, right=-1)
    near = tile_text(text, block, block, h1, cq, text_kv, cross_output_projection, low, high)
    shape = lambda a: a.reshape(core, span, width)
    lat = lax.axis_index("lat").astype(jnp.int32)[None]
    return merge(sizes[0], lat, rim, shape(near), shape(far))[None]


def solution(mesh):
    in_specs = (
        P(None, "lat", "lon", None),
        P(),
        P(),
        P(),
        P(),
        P(),
        P(),
        P(),
        P(None, None, "lon"),
        P(),
    )
    out_specs = P(None, "lat", "lon", None)
    sizes = (mesh.shape["lat"], mesh.shape["lon"])
    return jax.shard_map(
        functools.partial(local, sizes), mesh=mesh, in_specs=in_specs, out_specs=out_specs, check_vma=False
    )
```

```python
import functools
import math

import jax
import jax.numpy as jnp
from jax import lax
from jax.experimental import pallas as pl
from jax.experimental.pallas import tpu as pltpu
from jax.sharding import PartitionSpec as P

HEADS = 16
PAIRS = HEADS // 2
HALO = 4
LANES = 128
WIN = 256
TEXT_PAD = 384
VMEM = 60 * 1024 * 1024
SMALL = 30 * 1024 * 1024
NN = (((1,), (0,)), ((), ()))
NT = (((1,), (1,)), ((), ()))
BF16, F32 = jnp.bfloat16, jnp.float32
ANY = pl.BlockSpec(memory_space=pl.ANY)
LOCAL = pl.BlockSpec(memory_space=pltpu.VMEM)


def embedding(timestep, size):
    half = size // 2
    freqs = jnp.exp(-math.log(10000.0) * jnp.arange(half, dtype=F32) / half)
    angle = timestep.astype(F32)[:, None] * freqs[None, :]
    embed = jnp.concatenate([jnp.cos(angle), jnp.sin(angle)], axis=1)
    return jax.nn.silu(embed).astype(BF16)


def begin(pairs, sems, first):
    made = [pltpu.make_async_copy(a, b, sems.at[first + n]) for n, (a, b) in enumerate(pairs)]
    for c in made:
        c.start()
    return made


def finish_all(made):
    for c in made:
        c.wait()


def normalise(x_ref, at, count, mod_ref, u_ref):
    rows = 32
    blocks = count // rows
    gain = 1.0 + mod_ref[1:2, :]
    shift = mod_ref[0:1, :]

    def norm(i, carry):
        x = x_ref[pl.ds(pl.multiple_of(at + i * rows, rows), rows), :].astype(F32)
        mean = jnp.mean(x, axis=-1, keepdims=True)
        centred = x - mean
        var = jnp.mean(centred * centred, axis=-1, keepdims=True)
        normed = centred * lax.rsqrt(var + 1e-06)
        u_ref[pl.ds(pl.multiple_of(i * rows, rows), rows), :] = (normed * gain + shift).astype(BF16)
        return carry

    lax.fori_loop(0, blocks, norm, 0, unroll=next(n for n in (7, 6, 4, 2, 1) if blocks % n == 0))


def column_parts(total, size):
    return [(c, min(size, total - c)) for c in range(0, total, size)]


def weight_pairs(w_hbm, w_s, size):
    return [
        (w_hbm.at[:, pl.ds(c, n)], w_s.at[:, pl.ds(c, n)]) for c, n in column_parts(w_hbm.shape[1], size)
    ]


def project_qkv(u_ref, w_s, waits, size, width, q_factor, out_ref, at, done=lambda c, n: None):
    count = u_ref.shape[0]
    for wait, (c, n) in zip(waits, column_parts(w_s.shape[1], size)):
        wait.wait()
        made = jnp.dot(u_ref[...], w_s[:, c : c + n], preferred_element_type=F32)
        if c < width:
            ids = lax.broadcasted_iota(jnp.int32, (1, n), 1)
            made = made * jnp.where(ids < width - c, q_factor, 1.0)
        out_ref[at : at + count, c : c + n] = made.astype(BF16)
        done(c, n)


def band(low, high, dims, axis):
    ids = lax.broadcasted_iota(jnp.int32, dims, axis)
    return ((ids >= low) & (ids < high)).astype(F32).astype(BF16)


def pair_start(t):
    return t * LANES


def spare_columns(t, channels):
    return WIN - 64 if t * (2 * channels - LANES) + 2 * channels <= WIN - 64 else 0


def reciprocal(x):
    r = pl.reciprocal(x, approx=True)
    return r * (2.0 - x * r)


def pairs_unshifted(channels, q_ref, scores, values, p_refs, bad_ref, rows, out_ref):
    count = q_ref.shape[0]
    parts = [slice(c, c + rows) for c in range(0, count, rows)]
    gap = 2 * channels - LANES

    def close(t, p_ref, v, part):
        spare = spare_columns(t, channels)
        o = lax.dot_general(p_ref[part, :], v[0], v[1], preferred_element_type=F32)
        ids = lax.broadcasted_iota(jnp.int32, (1, WIN), 1)
        sum_a = o[:, spare : spare + 1]
        sum_b = o[:, spare + 32 : spare + 33]
        low, high = 2.0**-100, 2.0**100
        good = (sum_a >= low) & (sum_a <= high) & (sum_b >= low) & (sum_b <= high)
        bad_ref[...] = jnp.maximum(bad_ref[...], jnp.max(jnp.where(good, 0.0, 1.0), axis=0, keepdims=True))
        start = gap * t
        scale = jnp.where(ids < start + channels, reciprocal(sum_a), reciprocal(sum_b))
        cols = pl.ds(pair_start(t), WIN)
        old = out_ref[part, cols].astype(F32)
        inside = (ids >= start) & (ids < start + 2 * channels)
        out_ref[part, cols] = jnp.where(inside, o * scale, old).astype(BF16)

    bad_ref[...] = jnp.zeros_like(bad_ref)
    for part in parts:
        scores(0, 0, part, p_refs[0])
    for t in range(PAIRS):
        v = values(t, gap * t)
        for part in parts:
            if t + 1 < PAIRS:
                scores(t + 1, gap * (t + 1), part, p_refs[(t + 1) % 2])
            close(t, p_refs[t % 2], v, part)


def heads_shifted(channels, q_ref, keys, key_dims, values, value_dims, valid, out_ref):
    count, width = q_ref.shape
    rows = 64

    def one(n, carry):
        h = n // (count // rows)
        part = pl.ds(pl.multiple_of((n % (count // rows)) * rows, rows), rows)
        t = jnp.minimum((h * channels) // LANES, (width - WIN) // LANES)
        start = pl.multiple_of(t * LANES, LANES)
        offset = h * channels - start
        cols = pl.ds(start, WIN)
        q = q_ref[part, cols] * band(offset, offset + channels, (1, WIN), 1)
        s = lax.dot_general(q, keys(start), key_dims, preferred_element_type=F32)
        if valid < s.shape[1]:
            s = jnp.where(lax.broadcasted_iota(jnp.int32, s.shape, 1) < valid, s, -jnp.inf)
        p = jnp.exp2(s - jnp.max(s, axis=-1, keepdims=True))
        total = jnp.sum(p, axis=-1, keepdims=True)
        o = lax.dot_general(p.astype(BF16), values(start), value_dims, preferred_element_type=F32) / total
        ids = lax.broadcasted_iota(jnp.int32, (1, WIN), 1)
        old = out_ref[part, cols].astype(F32)
        inside = (ids >= offset) & (ids < offset + channels)
        out_ref[part, cols] = jnp.where(inside, o, old).astype(BF16)
        return carry

    lax.fori_loop(0, HEADS * (count // rows), one, 0)


def attend_self(channels, q_ref, k_ref, v_ref, vv_ref, p_refs, bad_ref, rows, out_ref):
    n = k_ref.shape[0]

    def scores(t, start, part, p_ref):
        cols = pl.ds(pair_start(t), WIN)
        q = q_ref[part, cols]
        for j in range(2):
            low = start + j * channels
            s = lax.dot_general(
                q * band(low, low + channels, (1, WIN), 1), k_ref[:, cols], NT, preferred_element_type=F32
            )
            p_ref[part, j * n : (j + 1) * n] = jnp.exp2(s).astype(BF16)

    def values(t, start):
        v = v_ref[:, pl.ds(pair_start(t), WIN)]
        spare = spare_columns(t, channels)
        for j in range(2):
            low, mark = start + j * channels, spare + 32 * j
            vv_ref[j * n : (j + 1) * n, :] = v * band(low, low + channels, (1, WIN), 1) + band(
                mark, mark + 32, (1, WIN), 1
            )
        return vv_ref[...], NN

    pairs_unshifted(channels, q_ref, scores, values, p_refs, bad_ref, rows, out_ref)

    @pl.when(jnp.max(bad_ref[...]) > 0.0)
    def _():
        heads_shifted(
            channels,
            q_ref,
            lambda start: k_ref[:, pl.ds(start, WIN)],
            NT,
            lambda start: v_ref[:, pl.ds(start, WIN)],
            NN,
            n,
            out_ref,
        )


def attend_text(channels, text, q_ref, kv_ref, p_refs, bad_ref, rows, out_ref):
    n = kv_ref.shape[1] // 2

    def scores(t, start, part, p_ref):
        k = kv_ref[pl.ds(pair_start(t), WIN), :n]
        pair = [
            k * band(start + j * channels, start + (j + 1) * channels, (WIN, 1), 0) for j in range(2)
        ]
        s = lax.dot_general(
            q_ref[part, pl.ds(pair_start(t), WIN)],
            jnp.concatenate(pair, axis=1),
            NN,
            preferred_element_type=F32,
        )
        p_ref[part, :] = jnp.exp2(s).astype(BF16)

    def values(t, start):
        v = kv_ref[pl.ds(pair_start(t), WIN), n:]
        valid = band(0, text, (1, n), 1)
        spare = spare_columns(t, channels)
        pair = [
            v * band(start + j * channels, start + (j + 1) * channels, (WIN, 1), 0)
            + band(spare + 32 * j, spare + 32 * j + 32, (WIN, 1), 0) * valid
            for j in range(2)
        ]
        return jnp.concatenate(pair, axis=1), NT

    pairs_unshifted(channels, q_ref, scores, values, p_refs, bad_ref, rows, out_ref)

    @pl.when(jnp.max(bad_ref[...]) > 0.0)
    def _():
        heads_shifted(
            channels,
            q_ref,
            lambda start: kv_ref[pl.ds(start, WIN), :n],
            NN,
            lambda start: kv_ref[pl.ds(start, WIN), n:],
            NT,
            text,
            out_ref,
        )


def prepare_kernel(emb, bias_ref, tw_hbm, context_hbm, kv_ref, head_out, mod_out, tw_s, context_s, own_s, mod_s, sems):
    width = bias_ref.shape[1]
    text = context_s.shape[0]
    lanes = own_s.shape[1] // 2
    waits = begin([(context_hbm, context_s), (tw_hbm, tw_s)], sems, 0)
    own_s[...] = jnp.zeros_like(own_s)
    waits[0].wait()
    for j in range(2):
        made = lax.dot_general(kv_ref[j], context_s[...], NT, preferred_element_type=F32)
        own_s[:, j * lanes : j * lanes + text] = made.astype(BF16)
    sent = begin([(own_s, head_out)], sems, 2)
    waits[1].wait()
    for j in range(3):
        cols = slice(j * width, (j + 1) * width)
        mod_s[j : j + 1, :] = (
            jnp.dot(emb[...], tw_s[:, cols], preferred_element_type=F32) + bias_ref[j : j + 1, :]
        )
    sent += begin([(mod_s, mod_out)], sems, 3)
    finish_all(sent)


def prepare(emb, time_weight, bias, context, cross_kv):
    width = bias.shape[1]
    channels = cross_kv.shape[1]
    return pl.pallas_call(
        prepare_kernel,
        out_shape=[
            jax.ShapeDtypeStruct((channels, 2 * TEXT_PAD), BF16),
            jax.ShapeDtypeStruct(bias.shape, F32),
        ],
        in_specs=[LOCAL, LOCAL, ANY, ANY, LOCAL],
        out_specs=[ANY, ANY],
        scratch_shapes=[
            pltpu.VMEM(time_weight.shape, BF16),
            pltpu.VMEM(context.shape, BF16),
            pltpu.VMEM((channels, 2 * TEXT_PAD), BF16),
            pltpu.VMEM(bias.shape, F32),
            pltpu.SemaphoreType.DMA((4,)),
        ],
        compiler_params=pltpu.CompilerParams(vmem_limit_bytes=VMEM),
        cost_estimate=pl.CostEstimate(
            flops=4 * context.shape[0] * width * channels, bytes_accessed=6 * 1024 * 1024, transcendentals=0
        ),
    )(emb, bias, time_weight, context, cross_kv)


def pack_kernel(x_ref, top_ref, bottom_ref, first_out, last_out, first_s, last_s):
    rim, core = top_ref.shape[0], x_ref.shape[0]
    rows = [(top_ref, a) for a in range(rim)] + [(x_ref, r) for r in range(core)]
    rows += [(bottom_ref, a) for a in range(rim)]
    for n, (ref, r) in enumerate(rows):
        tokens = ref[r].astype(F32)
        first_s[rim * n : rim * (n + 1), :] = tokens[:rim]
        last_s[rim * n : rim * (n + 1), :] = tokens[core - rim :]
    first_out[...] = first_s[...].astype(BF16)
    last_out[...] = last_s[...].astype(BF16)


def pack(x, top, bottom):
    rim, core, width = top.shape
    count = rim * (core + 2 * rim)
    return pl.pallas_call(
        pack_kernel,
        out_shape=[jax.ShapeDtypeStruct((count, width), BF16)] * 2,
        in_specs=[LOCAL] * 3,
        out_specs=[LOCAL] * 2,
        scratch_shapes=[pltpu.VMEM((count, width), F32)] * 2,
        compiler_params=pltpu.CompilerParams(vmem_limit_bytes=SMALL),
        cost_estimate=pl.CostEstimate(flops=0, bytes_accessed=3 * 1024 * 1024, transcendentals=0),
    )(x, top, bottom)


QKV_PART = 512


def core_kernel(q_factor, x_ref, mod_ref, w_hbm, out_hbm, u_s, w_s, out_s, sems):
    waits = begin(weight_pairs(w_hbm, w_s, QKV_PART), sems, 0)
    count, width = x_ref.shape
    normalise(x_ref, 0, count, mod_ref, u_s)
    sent = []

    def done(c, n):
        cols = pl.ds(c, n)
        sent.extend(begin([(out_s.at[:, cols], out_hbm.at[:, cols])], sems, 8 + len(sent)))

    project_qkv(u_s, w_s, waits, QKV_PART, width, q_factor, out_s, 0, done)
    finish_all(sent)


def core_qkv(q_factor, x, mod, weight):
    count, width = x.shape
    total = weight.shape[1]
    return pl.pallas_call(
        functools.partial(core_kernel, q_factor),
        out_shape=jax.ShapeDtypeStruct((count, total), BF16),
        in_specs=[LOCAL, LOCAL, ANY],
        out_specs=ANY,
        scratch_shapes=[
            pltpu.VMEM((count, width), BF16),
            pltpu.VMEM((width, total), BF16),
            pltpu.VMEM((count, total), BF16),
            pltpu.SemaphoreType.DMA((16,)),
        ],
        compiler_params=pltpu.CompilerParams(vmem_limit_bytes=VMEM),
        cost_estimate=pl.CostEstimate(
            flops=2 * count * width * total,
            bytes_accessed=2 * (width * total + count * (width + total)),
            transcendentals=0,
        ),
    )(x, mod, weight)


def regroup(core, rim, source_ref, target_ref):
    half = core // 2
    left = core * core
    right = left + rim * (core + 2 * rim)
    top = right + rim * (core + 2 * rim)
    bottom = top + rim * core
    at = 0

    def take(*pieces):
        nonlocal at
        for start, n in pieces:
            target_ref[at : at + n, :] = source_ref[start : start + n, :]
            at += n

    for base, row in ((top, 0), (bottom, rim + core)):
        for a in range(rim):
            take((left + rim * (row + a), rim), (base + core * a, half))
        for a in range(rim):
            take((base + core * a + half, half), (right + rim * (row + a), rim))
    for r in range(core):
        take((left + rim * (rim + r), rim), (core * r, half))
    for r in range(core):
        take((core * r + half, half), (right + rim * (rim + r), rim))


def tile_kernel(
    core,
    rim,
    rows,
    q_factor,
    x_core,
    left,
    right,
    top,
    bottom,
    qkv_core,
    mod_ref,
    w_hbm,
    wo_hbm,
    wq_hbm,
    h1_out,
    cq_out,
    x_s,
    qkv_s,
    u_s,
    w_s,
    wo_s,
    wq_s,
    vv_s,
    p_a,
    p_b,
    attn_s,
    h1_s,
    hg_s,
    bad_s,
    sems,
):
    width = x_core.shape[1]
    channels = width // HEADS
    inner = x_core.shape[0]
    outer = sum(a.shape[0] for a in (left, right, top, bottom))
    total = inner + outer
    pairs, at = [], inner
    for part in (left, right, top, bottom):
        pairs.append((part, x_s.at[pl.ds(at, part.shape[0])]))
        at += part.shape[0]
    waits_x = begin(pairs, sems, 0)
    waits_w = begin(weight_pairs(w_hbm, w_s, QKV_PART), sems, 4)
    waits_qkv = begin([(qkv_core, qkv_s.at[pl.ds(0, inner)])], sems, 12)
    waits_later = begin(
        [(x_core, x_s.at[pl.ds(0, inner)]), (wo_hbm, wo_s), (wq_hbm, wq_s)],
        sems,
        13,
    )
    finish_all(waits_x)
    normalise(x_s, inner, outer, mod_ref, u_s)
    project_qkv(u_s, w_s, waits_w, QKV_PART, width, q_factor, qkv_s, inner)
    finish_all(waits_qkv)
    attend_self(
        channels,
        qkv_s.at[:, pl.ds(0, width)],
        qkv_s.at[:, pl.ds(width, width)],
        qkv_s.at[:, pl.ds(2 * width, width)],
        vv_s,
        (p_a, p_b),
        bad_s,
        rows,
        attn_s,
    )
    finish_all(waits_later)
    step = total // 2
    for r in range(0, total, step):
        part = slice(r, r + step)
        mixed = jnp.dot(attn_s[part, :], wo_s[...], preferred_element_type=F32)
        h1_s[part, :] = x_s[part, :].astype(F32) + mod_ref[2:3, :] * mixed
    regroup(core, rim, h1_s, hg_s)
    waits_h = begin([(hg_s, h1_out)], sems, 16)
    for r in range(0, total, step):
        part = slice(r, r + step)
        made = jnp.dot(hg_s[part, :].astype(BF16), wq_s[...], preferred_element_type=F32)
        x_s[part, :] = (made * q_factor).astype(BF16)
        here = pl.ds(r, step)
        waits_h += begin([(x_s.at[here], cq_out.at[here])], sems, 17 + r // step)
    finish_all(waits_h)


def tile_self(core, rim, q_factor, x_core, rims, qkv_core, mod, weights):
    inner, width = x_core.shape
    outer = sum(a.shape[0] for a in rims)
    total = inner + outer
    wide = weights[0].shape[1]
    return pl.pallas_call(
        functools.partial(tile_kernel, core, rim, 256, q_factor),
        out_shape=[
            jax.ShapeDtypeStruct((total, width), F32),
            jax.ShapeDtypeStruct((total, width), BF16),
        ],
        in_specs=[ANY] * 6 + [LOCAL] + [ANY] * 3,
        out_specs=[ANY, ANY],
        scratch_shapes=[
            pltpu.VMEM((total, width), BF16),
            pltpu.VMEM((total, wide), BF16),
            pltpu.VMEM((outer, width), BF16),
            pltpu.VMEM((width, wide), BF16),
            pltpu.VMEM((width, width), BF16),
            pltpu.VMEM((width, width), BF16),
            pltpu.VMEM((2 * total, WIN), BF16),
            pltpu.VMEM((total, 2 * total), BF16),
            pltpu.VMEM((total, 2 * total), BF16),
            pltpu.VMEM((total, width), BF16),
            pltpu.VMEM((total, width), F32),
            pltpu.VMEM((total, width), F32),
            pltpu.VMEM((1, LANES), F32),
            pltpu.SemaphoreType.DMA((20,)),
        ],
        compiler_params=pltpu.CompilerParams(vmem_limit_bytes=VMEM),
        cost_estimate=pl.CostEstimate(
            flops=2 * outer * width * wide + 16 * total * width * total + 4 * total * width * width,
            bytes_accessed=2 * width * (wide + 2 * width) + 2 * inner * wide + 6 * total * width,
            transcendentals=HEADS * total * total,
        ),
    )(x_core, *rims, qkv_core, mod, *weights)


def text_kernel(text, first, parts, column_ref, h1, cq, t0, t1, t2, t3, wc_hbm, *rest):
    outs = rest[: len(parts)]
    q_s, h_s, kv_s, wc_s, p_a, p_b, attn_s, bad_s, sems = rest[len(parts) :]
    count, width = q_s.shape
    rows = pl.ds(first, count)
    pairs = [(cq.at[rows], q_s)]
    for k, arrived in enumerate((t0, t1, t2, t3)):
        size = arrived.shape[0]
        where = pl.multiple_of(lax.rem(column_ref[0] + k, 4) * size, size)
        pairs.append((arrived, kv_s.at[pl.ds(where, size), :]))
    waits = begin(pairs, sems, 0)
    waits_later = begin([(wc_hbm, wc_s), (h1.at[rows], h_s)], sems, 5)
    finish_all(waits)
    attend_text(width // HEADS, text, q_s, kv_s, (p_a, p_b), bad_s, count, attn_s)
    finish_all(waits_later)
    made = h_s[...] + jnp.dot(attn_s[...], wc_s[...], preferred_element_type=F32)
    at = 0
    for out, n in zip(outs, parts):
        out[...] = made[at : at + n].astype(BF16)
        at += n


def tile_text(text, first, parts, column, h1, cq, arrived, weight):
    count = sum(parts)
    width = h1.shape[1]
    padded = arrived[0].shape[1] // 2
    return pl.pallas_call(
        functools.partial(text_kernel, text, first, parts),
        out_shape=[jax.ShapeDtypeStruct((n, width), BF16) for n in parts],
        in_specs=[pl.BlockSpec(memory_space=pltpu.SMEM)] + [ANY] * 7,
        out_specs=[LOCAL] * len(parts),
        scratch_shapes=[
            pltpu.VMEM((count, width), BF16),
            pltpu.VMEM((count, width), F32),
            pltpu.VMEM((width, 2 * padded), BF16),
            pltpu.VMEM((width, width), BF16),
            pltpu.VMEM((count, 2 * padded), BF16),
            pltpu.VMEM((count, 2 * padded), BF16),
            pltpu.VMEM((count, width), BF16),
            pltpu.VMEM((1, LANES), F32),
            pltpu.SemaphoreType.DMA((7,)),
        ],
        compiler_params=pltpu.CompilerParams(vmem_limit_bytes=VMEM),
        cost_estimate=pl.CostEstimate(
            flops=16 * count * width * padded + 2 * count * width * width,
            bytes_accessed=2 * width * (width + 2 * padded) + 8 * count * width,
            transcendentals=HEADS * count * padded,
        ),
    )(column, h1, cq, *arrived, weight)


def merge_kernel(lat_count, rim, lat_ref, near, far, low, high, passed, out_hbm, near_s, out_s, sems):
    lat = lat_ref[0]
    core = near.shape[0]
    rows = 8
    steps = range(core // rows)
    waits = begin([(near.at[pl.ds(i * rows, rows)], near_s.at[pl.ds(i * rows, rows)]) for i in steps], sems, 0)
    sent = []

    def average(body, extra, first):
        n = body.shape[0]
        ids = lax.broadcasted_iota(jnp.int32, (n, 1, 1), 0) + first
        shared = ((ids < rim) & (lat > 0)) | ((ids >= core - rim) & (lat < lat_count - 1))
        body = body.astype(F32) if extra is None else body.astype(F32) + extra.astype(F32)
        return body * jnp.where(shared, 0.5, 1.0)

    for i in steps:
        waits[i].wait()
        for first in range(i * rows, (i + 1) * rows, rim):
            part = slice(first, first + rim)
            extra = (None, None)
            if first == 0:
                extra = (low[rim:], passed[:rim])
            if first == core - rim:
                extra = (high[rim:], passed[rim:])
            a, b = average(near_s[part], extra[0], first), average(far[part], extra[1], first)
            made = jnp.concatenate([a[:, :8], (a[:, 8:] + b[:, :8]) * 0.5, b[:, 8:]], axis=1)
            out_s[part] = made.astype(BF16)
        here = pl.ds(i * rows, rows)
        sent += begin([(out_s.at[here], out_hbm.at[here])], sems, len(steps) + i)
    finish_all(sent)


def merge(lat_count, lat, rim, near, far, low, high, passed):
    core, span, width = near.shape
    return pl.pallas_call(
        functools.partial(merge_kernel, lat_count, rim),
        out_shape=jax.ShapeDtypeStruct((core, core, width), BF16),
        in_specs=[pl.BlockSpec(memory_space=pltpu.SMEM), ANY] + [LOCAL] * 4,
        out_specs=ANY,
        scratch_shapes=[
            pltpu.VMEM((core, span, width), BF16),
            pltpu.VMEM((core, core, width), BF16),
            pltpu.SemaphoreType.DMA((6,)),
        ],
        compiler_params=pltpu.CompilerParams(vmem_limit_bytes=SMALL),
        cost_estimate=pl.CostEstimate(
            flops=4 * core * core * width, bytes_accessed=8 * core * core * width, transcendentals=0
        ),
    )(lat, near, far, low, high, passed)


def send(value, mesh_sizes, down, right):
    rows, cols = mesh_sizes
    pairs = [
        (r * cols + c, (r + down) * cols + (c + right) % cols)
        for r in range(rows)
        for c in range(cols)
        if 0 <= r + down < rows
    ]
    return lax.ppermute(value, ("lat", "lon"), pairs)


def local(
    sizes,
    hidden,
    timestep,
    context,
    time_weight,
    modulation_bias,
    qkv_weight,
    out_weight,
    cross_q,
    cross_kv,
    cross_output_projection,
):
    core, width = hidden.shape[1], hidden.shape[3]
    half = core // 2
    rim = HALO
    text = context.shape[1]
    lon_count = sizes[1]
    to = functools.partial(send, mesh_sizes=sizes)
    q_factor = math.log2(math.e) / math.sqrt(width // HEADS)

    lon_count = sizes[1]
    lon = lax.axis_index("lon")

    def among(value, partner):
        return lax.ppermute(value, "lon", [(partner(i), i) for i in range(lon_count)])

    def joined(bit, mine, theirs):
        low = (lon // bit) % 2 == 0
        return jnp.concatenate([jnp.where(low, mine, theirs), jnp.where(low, theirs, mine)], axis=0)

    x = hidden[0]
    flat = lambda a: a.reshape(-1, width)
    top = to(flat(x[core - rim :]), down=1, right=0)
    bottom = to(flat(x[:rim]), down=-1, right=0)
    emb = embedding(timestep, time_weight.shape[0])
    kv_rows = jnp.transpose(cross_kv, (0, 2, 1))
    own_head, mod = prepare(emb, time_weight, modulation_bias, context[0], kv_rows)
    own_head, top, bottom = lax.optimization_barrier((own_head, top, bottom))
    other = among(own_head, lambda i: i ^ 1)
    rows = lambda a: a.reshape(rim, core, width)
    first, last = pack(x, rows(top), rows(bottom))
    left = to(last, down=0, right=1)
    right = to(first, down=0, right=-1)
    two = joined(1, own_head, other)
    x, first, last, two = lax.optimization_barrier((x, first, last, two))
    far_two = among(two, lambda i: i ^ 2)
    x_core = flat(x)
    qkv_core = core_qkv(q_factor, x_core, mod, qkv_weight)
    four = joined(2, two, far_two)
    qkv_core, four = lax.optimization_barrier((qkv_core, four))
    arrived = [four] + [among(four, lambda i, k=k: (i + 4 * k) % lon_count) for k in (1, 2, 3)]
    column = (lon // 4).astype(jnp.int32)[None]

    h1, cq = tile_self(
        core,
        rim,
        q_factor,
        x_core,
        (left, right, top, bottom),
        qkv_core,
        mod,
        (qkv_weight, out_weight, cross_q),
    )
    span = half + rim
    edge, block = rim * span, core * span
    top_made, bottom_made, main = tile_text(
        text, 0, (2 * edge, 2 * edge, block), column, h1, cq, arrived, cross_output_projection
    )
    high = to(top_made, down=-1, right=0)
    low = to(bottom_made, down=1, right=0)
    far = to(main, down=0, right=-1)
    (near,) = tile_text(
        text, 4 * edge + block, (block,), column, h1, cq, arrived, cross_output_projection
    )
    near, low, high = lax.optimization_barrier((near, low, high))
    passed = to(jnp.concatenate([low[:edge], high[:edge]], axis=0), down=0, right=-1)
    shape = lambda a: a.reshape(-1, span, width)
    lat = lax.axis_index("lat").astype(jnp.int32)[None]
    return merge(sizes[0], lat, rim, *(shape(a) for a in (near, far, low, high, passed)))[None]


def solution(mesh):
    in_specs = (
        P(None, "lat", "lon", None),
        P(),
        P(),
        P(),
        P(),
        P(),
        P(),
        P(),
        P(None, None, "lon"),
        P(),
    )
    out_specs = P(None, "lat", "lon", None)
    sizes = (mesh.shape["lat"], mesh.shape["lon"])
    return jax.shard_map(
        functools.partial(local, sizes), mesh=mesh, in_specs=in_specs, out_specs=out_specs, check_vma=False
    )
```

```python
import functools
import math

import jax
import jax.numpy as jnp
from jax import lax
from jax.experimental import pallas as pl
from jax.experimental.pallas import tpu as pltpu
from jax.sharding import PartitionSpec as P

HEADS = 16
PAIRS = HEADS // 2
HALO = 4
LANES = 128
WIN = 256
TEXT_PAD = 384
VMEM = 60 * 1024 * 1024
SMALL = 30 * 1024 * 1024
NN = (((1,), (0,)), ((), ()))
NT = (((1,), (1,)), ((), ()))
BF16, F32 = jnp.bfloat16, jnp.float32
ANY = pl.BlockSpec(memory_space=pl.ANY)
LOCAL = pl.BlockSpec(memory_space=pltpu.VMEM)


def embedding(timestep, size):
    half = size // 2
    freqs = jnp.exp(-math.log(10000.0) * jnp.arange(half, dtype=F32) / half)
    angle = timestep.astype(F32)[:, None] * freqs[None, :]
    embed = jnp.concatenate([jnp.cos(angle), jnp.sin(angle)], axis=1)
    return jax.nn.silu(embed).astype(BF16)


def begin(pairs, sems, first):
    made = [pltpu.make_async_copy(a, b, sems.at[first + n]) for n, (a, b) in enumerate(pairs)]
    for c in made:
        c.start()
    return made


def finish_all(made):
    for c in made:
        c.wait()


def normalise(x_ref, at, count, mod_ref, u_ref):
    rows = 32
    blocks = count // rows
    gain = 1.0 + mod_ref[1:2, :]
    shift = mod_ref[0:1, :]

    def norm(i, carry):
        x = x_ref[pl.ds(pl.multiple_of(at + i * rows, rows), rows), :].astype(F32)
        mean = jnp.mean(x, axis=-1, keepdims=True)
        centred = x - mean
        var = jnp.mean(centred * centred, axis=-1, keepdims=True)
        normed = centred * lax.rsqrt(var + 1e-06)
        u_ref[pl.ds(pl.multiple_of(i * rows, rows), rows), :] = (normed * gain + shift).astype(BF16)
        return carry

    lax.fori_loop(0, blocks, norm, 0, unroll=next(n for n in (7, 6, 4, 2, 1) if blocks % n == 0))


def column_parts(total, size):
    return [(c, min(size, total - c)) for c in range(0, total, size)]


def weight_pairs(w_hbm, w_s, size):
    return [
        (w_hbm.at[:, pl.ds(c, n)], w_s.at[:, pl.ds(c, n)]) for c, n in column_parts(w_hbm.shape[1], size)
    ]


def project_qkv(u_ref, w_s, waits, size, width, q_factor, out_ref, at, done=lambda c, n: None):
    count = u_ref.shape[0]
    for wait, (c, n) in zip(waits, column_parts(w_s.shape[1], size)):
        wait.wait()
        made = jnp.dot(u_ref[...], w_s[:, c : c + n], preferred_element_type=F32)
        if c < width:
            ids = lax.broadcasted_iota(jnp.int32, (1, n), 1)
            made = made * jnp.where(ids < width - c, q_factor, 1.0)
        out_ref[at : at + count, c : c + n] = made.astype(BF16)
        done(c, n)


def band(low, high, dims, axis):
    ids = lax.broadcasted_iota(jnp.int32, dims, axis)
    return ((ids >= low) & (ids < high)).astype(F32).astype(BF16)


def pair_start(t):
    return t * LANES


def spare_columns(t, channels):
    return WIN - 64 if t * (2 * channels - LANES) + 2 * channels <= WIN - 64 else 0


def reciprocal(x):
    r = pl.reciprocal(x, approx=True)
    return r * (2.0 - x * r)


def pairs_unshifted(channels, q_ref, scores, values, p_refs, bad_ref, rows, out_ref):
    count = q_ref.shape[0]
    parts = [slice(c, c + rows) for c in range(0, count, rows)]
    gap = 2 * channels - LANES

    def close(t, p_ref, v, part):
        spare = spare_columns(t, channels)
        o = lax.dot_general(p_ref[part, :], v[0], v[1], preferred_element_type=F32)
        ids = lax.broadcasted_iota(jnp.int32, (1, WIN), 1)
        sum_a = o[:, spare : spare + 1]
        sum_b = o[:, spare + 32 : spare + 33]
        low, high = 2.0**-100, 2.0**100
        good = (sum_a >= low) & (sum_a <= high) & (sum_b >= low) & (sum_b <= high)
        bad_ref[...] = jnp.maximum(bad_ref[...], jnp.max(jnp.where(good, 0.0, 1.0), axis=0, keepdims=True))
        start = gap * t
        scale = jnp.where(ids < start + channels, reciprocal(sum_a), reciprocal(sum_b))
        cols = pl.ds(pair_start(t), WIN)
        old = out_ref[part, cols].astype(F32)
        inside = (ids >= start) & (ids < start + 2 * channels)
        out_ref[part, cols] = jnp.where(inside, o * scale, old).astype(BF16)

    bad_ref[...] = jnp.zeros_like(bad_ref)
    for part in parts:
        scores(0, 0, part, p_refs[0])
    for t in range(PAIRS):
        v = values(t, gap * t)
        for part in parts:
            if t + 1 < PAIRS:
                scores(t + 1, gap * (t + 1), part, p_refs[(t + 1) % 2])
            close(t, p_refs[t % 2], v, part)


def heads_shifted(channels, q_ref, keys, key_dims, values, value_dims, valid, out_ref):
    count, width = q_ref.shape
    rows = 64

    def one(n, carry):
        h = n // (count // rows)
        part = pl.ds(pl.multiple_of((n % (count // rows)) * rows, rows), rows)
        t = jnp.minimum((h * channels) // LANES, (width - WIN) // LANES)
        start = pl.multiple_of(t * LANES, LANES)
        offset = h * channels - start
        cols = pl.ds(start, WIN)
        q = q_ref[part, cols] * band(offset, offset + channels, (1, WIN), 1)
        s = lax.dot_general(q, keys(start), key_dims, preferred_element_type=F32)
        if valid < s.shape[1]:
            s = jnp.where(lax.broadcasted_iota(jnp.int32, s.shape, 1) < valid, s, -jnp.inf)
        p = jnp.exp2(s - jnp.max(s, axis=-1, keepdims=True))
        total = jnp.sum(p, axis=-1, keepdims=True)
        o = lax.dot_general(p.astype(BF16), values(start), value_dims, preferred_element_type=F32) / total
        ids = lax.broadcasted_iota(jnp.int32, (1, WIN), 1)
        old = out_ref[part, cols].astype(F32)
        inside = (ids >= offset) & (ids < offset + channels)
        out_ref[part, cols] = jnp.where(inside, o, old).astype(BF16)
        return carry

    lax.fori_loop(0, HEADS * (count // rows), one, 0)


def attend_self(channels, q_ref, k_ref, v_ref, vv_ref, p_refs, bad_ref, rows, out_ref):
    n = k_ref.shape[0]

    def scores(t, start, part, p_ref):
        cols = pl.ds(pair_start(t), WIN)
        q = q_ref[part, cols]
        for j in range(2):
            low = start + j * channels
            s = lax.dot_general(
                q * band(low, low + channels, (1, WIN), 1), k_ref[:, cols], NT, preferred_element_type=F32
            )
            p_ref[part, j * n : (j + 1) * n] = jnp.exp2(s).astype(BF16)

    def values(t, start):
        v = v_ref[:, pl.ds(pair_start(t), WIN)]
        spare = spare_columns(t, channels)
        for j in range(2):
            low, mark = start + j * channels, spare + 32 * j
            vv_ref[j * n : (j + 1) * n, :] = v * band(low, low + channels, (1, WIN), 1) + band(
                mark, mark + 32, (1, WIN), 1
            )
        return vv_ref[...], NN

    pairs_unshifted(channels, q_ref, scores, values, p_refs, bad_ref, rows, out_ref)

    @pl.when(jnp.max(bad_ref[...]) > 0.0)
    def _():
        heads_shifted(
            channels,
            q_ref,
            lambda start: k_ref[:, pl.ds(start, WIN)],
            NT,
            lambda start: v_ref[:, pl.ds(start, WIN)],
            NN,
            n,
            out_ref,
        )


def attend_text(channels, text, q_ref, kv_ref, p_refs, bad_ref, rows, out_ref):
    n = kv_ref.shape[1] // 2

    def scores(t, start, part, p_ref):
        k = kv_ref[pl.ds(pair_start(t), WIN), :n]
        pair = [
            k * band(start + j * channels, start + (j + 1) * channels, (WIN, 1), 0) for j in range(2)
        ]
        s = lax.dot_general(
            q_ref[part, pl.ds(pair_start(t), WIN)],
            jnp.concatenate(pair, axis=1),
            NN,
            preferred_element_type=F32,
        )
        p_ref[part, :] = jnp.exp2(s).astype(BF16)

    def values(t, start):
        v = kv_ref[pl.ds(pair_start(t), WIN), n:]
        valid = band(0, text, (1, n), 1)
        spare = spare_columns(t, channels)
        pair = [
            v * band(start + j * channels, start + (j + 1) * channels, (WIN, 1), 0)
            + band(spare + 32 * j, spare + 32 * j + 32, (WIN, 1), 0) * valid
            for j in range(2)
        ]
        return jnp.concatenate(pair, axis=1), NT

    pairs_unshifted(channels, q_ref, scores, values, p_refs, bad_ref, rows, out_ref)

    @pl.when(jnp.max(bad_ref[...]) > 0.0)
    def _():
        heads_shifted(
            channels,
            q_ref,
            lambda start: kv_ref[pl.ds(start, WIN), :n],
            NN,
            lambda start: kv_ref[pl.ds(start, WIN), n:],
            NT,
            text,
            out_ref,
        )


def prepare_kernel(emb, bias_ref, tw_hbm, context_hbm, kv_ref, head_out, mod_out, tw_s, context_s, own_s, mod_s, sems):
    width = bias_ref.shape[1]
    text = context_s.shape[0]
    lanes = own_s.shape[1] // 2
    waits = begin([(context_hbm, context_s), (tw_hbm, tw_s)], sems, 0)
    own_s[...] = jnp.zeros_like(own_s)
    waits[0].wait()
    for j in range(2):
        made = lax.dot_general(kv_ref[j], context_s[...], NT, preferred_element_type=F32)
        own_s[:, j * lanes : j * lanes + text] = made.astype(BF16)
    sent = begin([(own_s, head_out)], sems, 2)
    waits[1].wait()
    for j in range(3):
        cols = slice(j * width, (j + 1) * width)
        mod_s[j : j + 1, :] = (
            jnp.dot(emb[...], tw_s[:, cols], preferred_element_type=F32) + bias_ref[j : j + 1, :]
        )
    sent += begin([(mod_s, mod_out)], sems, 3)
    finish_all(sent)


def prepare(emb, time_weight, bias, context, cross_kv):
    width = bias.shape[1]
    channels = cross_kv.shape[1]
    return pl.pallas_call(
        prepare_kernel,
        out_shape=[
            jax.ShapeDtypeStruct((channels, 2 * TEXT_PAD), BF16),
            jax.ShapeDtypeStruct(bias.shape, F32),
        ],
        in_specs=[LOCAL, LOCAL, ANY, ANY, LOCAL],
        out_specs=[ANY, ANY],
        scratch_shapes=[
            pltpu.VMEM(time_weight.shape, BF16),
            pltpu.VMEM(context.shape, BF16),
            pltpu.VMEM((channels, 2 * TEXT_PAD), BF16),
            pltpu.VMEM(bias.shape, F32),
            pltpu.SemaphoreType.DMA((4,)),
        ],
        compiler_params=pltpu.CompilerParams(vmem_limit_bytes=VMEM),
        cost_estimate=pl.CostEstimate(
            flops=4 * context.shape[0] * width * channels, bytes_accessed=6 * 1024 * 1024, transcendentals=0
        ),
    )(emb, bias, time_weight, context, cross_kv)


def pack_kernel(x_ref, top_ref, bottom_ref, first_out, last_out, first_s, last_s):
    rim, core = top_ref.shape[0], x_ref.shape[0]
    rows = [(top_ref, a) for a in range(rim)] + [(x_ref, r) for r in range(core)]
    rows += [(bottom_ref, a) for a in range(rim)]
    for n, (ref, r) in enumerate(rows):
        tokens = ref[r].astype(F32)
        first_s[rim * n : rim * (n + 1), :] = tokens[:rim]
        last_s[rim * n : rim * (n + 1), :] = tokens[core - rim :]
    first_out[...] = first_s[...].astype(BF16)
    last_out[...] = last_s[...].astype(BF16)


def pack(x, top, bottom):
    rim, core, width = top.shape
    count = rim * (core + 2 * rim)
    return pl.pallas_call(
        pack_kernel,
        out_shape=[jax.ShapeDtypeStruct((count, width), BF16)] * 2,
        in_specs=[LOCAL] * 3,
        out_specs=[LOCAL] * 2,
        scratch_shapes=[pltpu.VMEM((count, width), F32)] * 2,
        compiler_params=pltpu.CompilerParams(vmem_limit_bytes=SMALL),
        cost_estimate=pl.CostEstimate(flops=0, bytes_accessed=3 * 1024 * 1024, transcendentals=0),
    )(x, top, bottom)


QKV_PART = 512


def core_kernel(q_factor, x_ref, mod_ref, w_hbm, out_hbm, u_s, w_s, out_s, sems):
    waits = begin(weight_pairs(w_hbm, w_s, QKV_PART), sems, 0)
    count, width = x_ref.shape
    normalise(x_ref, 0, count, mod_ref, u_s)
    sent = []

    def done(c, n):
        cols = pl.ds(c, n)
        sent.extend(begin([(out_s.at[:, cols], out_hbm.at[:, cols])], sems, 8 + len(sent)))

    project_qkv(u_s, w_s, waits, QKV_PART, width, q_factor, out_s, 0, done)
    finish_all(sent)


def core_qkv(q_factor, x, mod, weight):
    count, width = x.shape
    total = weight.shape[1]
    return pl.pallas_call(
        functools.partial(core_kernel, q_factor),
        out_shape=jax.ShapeDtypeStruct((count, total), BF16),
        in_specs=[LOCAL, LOCAL, ANY],
        out_specs=ANY,
        scratch_shapes=[
            pltpu.VMEM((count, width), BF16),
            pltpu.VMEM((width, total), BF16),
            pltpu.VMEM((count, total), BF16),
            pltpu.SemaphoreType.DMA((16,)),
        ],
        compiler_params=pltpu.CompilerParams(vmem_limit_bytes=VMEM),
        cost_estimate=pl.CostEstimate(
            flops=2 * count * width * total,
            bytes_accessed=2 * (width * total + count * (width + total)),
            transcendentals=0,
        ),
    )(x, mod, weight)


def regroup(core, rim):
    half = core // 2
    left = core * core
    right = left + rim * (core + 2 * rim)
    top = right + rim * (core + 2 * rim)
    bottom = top + rim * core
    taken = []

    def take(*pieces):
        taken.append(pieces)

    for base, row in ((top, 0), (bottom, rim + core)):
        for a in range(rim):
            take((left + rim * (row + a), rim), (base + core * a, half))
        for a in range(rim):
            take((base + core * a + half, half), (right + rim * (row + a), rim))
    for r in range(core):
        take((left + rim * (rim + r), rim), (core * r, half))
    for r in range(core):
        take((core * r + half, half), (right + rim * (rim + r), rim))
    return taken


def tile_kernel(
    core,
    rim,
    rows,
    q_factor,
    x_core,
    left,
    right,
    top,
    bottom,
    qkv_core,
    mod_ref,
    w_hbm,
    wo_hbm,
    wq_hbm,
    h1_out,
    cq_out,
    x_s,
    qkv_s,
    u_s,
    w_s,
    wo_s,
    wq_s,
    vv_s,
    p_a,
    p_b,
    attn_s,
    h1_s,
    hg_s,
    bad_s,
    sems,
):
    width = x_core.shape[1]
    channels = width // HEADS
    inner = x_core.shape[0]
    outer = sum(a.shape[0] for a in (left, right, top, bottom))
    total = inner + outer
    pairs, at = [], inner
    for part in (left, right, top, bottom):
        pairs.append((part, x_s.at[pl.ds(at, part.shape[0])]))
        at += part.shape[0]
    waits_x = begin(pairs, sems, 0)
    waits_w = begin(weight_pairs(w_hbm, w_s, QKV_PART), sems, 4)
    waits_qkv = begin([(qkv_core, qkv_s.at[pl.ds(0, inner)])], sems, 12)
    waits_later = begin(
        [(x_core, x_s.at[pl.ds(0, inner)]), (wo_hbm, wo_s), (wq_hbm, wq_s)],
        sems,
        13,
    )
    finish_all(waits_x)
    normalise(x_s, inner, outer, mod_ref, u_s)
    project_qkv(u_s, w_s, waits_w, QKV_PART, width, q_factor, qkv_s, inner)
    finish_all(waits_qkv)
    attend_self(
        channels,
        qkv_s.at[:, pl.ds(0, width)],
        qkv_s.at[:, pl.ds(width, width)],
        qkv_s.at[:, pl.ds(2 * width, width)],
        vv_s,
        (p_a, p_b),
        bad_s,
        rows,
        attn_s,
    )
    finish_all(waits_later)
    step = total // 2
    for r in range(0, total, step):
        part = slice(r, r + step)
        mixed = jnp.dot(attn_s[part, :], wo_s[...], preferred_element_type=F32)
        h1_s[part, :] = x_s[part, :].astype(F32) + mod_ref[2:3, :] * mixed
    waits_h = []
    groups = regroup(core, rim)
    span = total // len(groups)
    for r in range(0, total, step):
        at = r
        for pieces in groups[r // span : (r + step) // span]:
            for start, n in pieces:
                hg_s[at : at + n, :] = h1_s[start : start + n, :]
                at += n
        part, here = slice(r, r + step), pl.ds(r, step)
        waits_h += begin([(hg_s.at[here], h1_out.at[here])], sems, 16 + r // step)
        made = jnp.dot(hg_s[part, :].astype(BF16), wq_s[...], preferred_element_type=F32)
        x_s[part, :] = (made * q_factor).astype(BF16)
        waits_h += begin([(x_s.at[here], cq_out.at[here])], sems, 18 + r // step)
    finish_all(waits_h)


def tile_self(core, rim, q_factor, x_core, rims, qkv_core, mod, weights):
    inner, width = x_core.shape
    outer = sum(a.shape[0] for a in rims)
    total = inner + outer
    wide = weights[0].shape[1]
    return pl.pallas_call(
        functools.partial(tile_kernel, core, rim, 256, q_factor),
        out_shape=[
            jax.ShapeDtypeStruct((total, width), F32),
            jax.ShapeDtypeStruct((total, width), BF16),
        ],
        in_specs=[ANY] * 6 + [LOCAL] + [ANY] * 3,
        out_specs=[ANY, ANY],
        scratch_shapes=[
            pltpu.VMEM((total, width), BF16),
            pltpu.VMEM((total, wide), BF16),
            pltpu.VMEM((outer, width), BF16),
            pltpu.VMEM((width, wide), BF16),
            pltpu.VMEM((width, width), BF16),
            pltpu.VMEM((width, width), BF16),
            pltpu.VMEM((2 * total, WIN), BF16),
            pltpu.VMEM((total, 2 * total), BF16),
            pltpu.VMEM((total, 2 * total), BF16),
            pltpu.VMEM((total, width), BF16),
            pltpu.VMEM((total, width), F32),
            pltpu.VMEM((total, width), F32),
            pltpu.VMEM((1, LANES), F32),
            pltpu.SemaphoreType.DMA((20,)),
        ],
        compiler_params=pltpu.CompilerParams(vmem_limit_bytes=VMEM),
        cost_estimate=pl.CostEstimate(
            flops=2 * outer * width * wide + 16 * total * width * total + 4 * total * width * width,
            bytes_accessed=2 * width * (wide + 2 * width) + 2 * inner * wide + 6 * total * width,
            transcendentals=HEADS * total * total,
        ),
    )(x_core, *rims, qkv_core, mod, *weights)


def text_kernel(text, first, parts, column_ref, h1, cq, t0, t1, t2, t3, wc_hbm, *rest):
    outs = rest[: len(parts)]
    q_s, h_s, kv_s, wc_s, p_a, p_b, attn_s, bad_s, sems = rest[len(parts) :]
    count, width = q_s.shape
    rows = pl.ds(first, count)
    pairs = [(cq.at[rows], q_s)]
    for k, arrived in enumerate((t0, t1, t2, t3)):
        size = arrived.shape[0]
        where = pl.multiple_of(lax.rem(column_ref[0] + k, 4) * size, size)
        pairs.append((arrived, kv_s.at[pl.ds(where, size), :]))
    waits = begin(pairs, sems, 0)
    waits_later = begin([(wc_hbm, wc_s), (h1.at[rows], h_s)], sems, 5)
    finish_all(waits)
    attend_text(width // HEADS, text, q_s, kv_s, (p_a, p_b), bad_s, count, attn_s)
    finish_all(waits_later)
    made = h_s[...] + jnp.dot(attn_s[...], wc_s[...], preferred_element_type=F32)
    at = 0
    for out, n in zip(outs, parts):
        out[...] = made[at : at + n].astype(BF16)
        at += n


def tile_text(text, first, parts, column, h1, cq, arrived, weight):
    count = sum(parts)
    width = h1.shape[1]
    padded = arrived[0].shape[1] // 2
    return pl.pallas_call(
        functools.partial(text_kernel, text, first, parts),
        out_shape=[jax.ShapeDtypeStruct((n, width), BF16) for n in parts],
        in_specs=[pl.BlockSpec(memory_space=pltpu.SMEM)] + [ANY] * 7,
        out_specs=[LOCAL] * len(parts),
        scratch_shapes=[
            pltpu.VMEM((count, width), BF16),
            pltpu.VMEM((count, width), F32),
            pltpu.VMEM((width, 2 * padded), BF16),
            pltpu.VMEM((width, width), BF16),
            pltpu.VMEM((count, 2 * padded), BF16),
            pltpu.VMEM((count, 2 * padded), BF16),
            pltpu.VMEM((count, width), BF16),
            pltpu.VMEM((1, LANES), F32),
            pltpu.SemaphoreType.DMA((7,)),
        ],
        compiler_params=pltpu.CompilerParams(vmem_limit_bytes=VMEM),
        cost_estimate=pl.CostEstimate(
            flops=16 * count * width * padded + 2 * count * width * width,
            bytes_accessed=2 * width * (width + 2 * padded) + 8 * count * width,
            transcendentals=HEADS * count * padded,
        ),
    )(column, h1, cq, *arrived, weight)


def merge_kernel(lat_count, rim, lat_ref, near, far, low, high, passed, out_hbm, near_s, out_s, sems):
    lat = lat_ref[0]
    core = near.shape[0]
    rows = 8
    steps = range(core // rows)
    waits = begin([(near.at[pl.ds(i * rows, rows)], near_s.at[pl.ds(i * rows, rows)]) for i in steps], sems, 0)
    sent = []

    def average(body, extra, first):
        n = body.shape[0]
        ids = lax.broadcasted_iota(jnp.int32, (n, 1, 1), 0) + first
        shared = ((ids < rim) & (lat > 0)) | ((ids >= core - rim) & (lat < lat_count - 1))
        body = body.astype(F32) if extra is None else body.astype(F32) + extra.astype(F32)
        return body * jnp.where(shared, 0.5, 1.0)

    for i in steps:
        waits[i].wait()
        for first in range(i * rows, (i + 1) * rows, rim):
            part = slice(first, first + rim)
            extra = (None, None)
            if first == 0:
                extra = (low[rim:], passed[:rim])
            if first == core - rim:
                extra = (high[rim:], passed[rim:])
            a, b = average(near_s[part], extra[0], first), average(far[part], extra[1], first)
            made = jnp.concatenate([a[:, :8], (a[:, 8:] + b[:, :8]) * 0.5, b[:, 8:]], axis=1)
            out_s[part] = made.astype(BF16)
        here = pl.ds(i * rows, rows)
        sent += begin([(out_s.at[here], out_hbm.at[here])], sems, len(steps) + i)
    finish_all(sent)


def merge(lat_count, lat, rim, near, far, low, high, passed):
    core, span, width = near.shape
    return pl.pallas_call(
        functools.partial(merge_kernel, lat_count, rim),
        out_shape=jax.ShapeDtypeStruct((core, core, width), BF16),
        in_specs=[pl.BlockSpec(memory_space=pltpu.SMEM), ANY] + [LOCAL] * 4,
        out_specs=ANY,
        scratch_shapes=[
            pltpu.VMEM((core, span, width), BF16),
            pltpu.VMEM((core, core, width), BF16),
            pltpu.SemaphoreType.DMA((6,)),
        ],
        compiler_params=pltpu.CompilerParams(vmem_limit_bytes=SMALL),
        cost_estimate=pl.CostEstimate(
            flops=4 * core * core * width, bytes_accessed=8 * core * core * width, transcendentals=0
        ),
    )(lat, near, far, low, high, passed)


def send(value, mesh_sizes, down, right):
    rows, cols = mesh_sizes
    pairs = [
        (r * cols + c, (r + down) * cols + (c + right) % cols)
        for r in range(rows)
        for c in range(cols)
        if 0 <= r + down < rows
    ]
    return lax.ppermute(value, ("lat", "lon"), pairs)


def local(
    sizes,
    hidden,
    timestep,
    context,
    time_weight,
    modulation_bias,
    qkv_weight,
    out_weight,
    cross_q,
    cross_kv,
    cross_output_projection,
):
    core, width = hidden.shape[1], hidden.shape[3]
    half = core // 2
    rim = HALO
    text = context.shape[1]
    lon_count = sizes[1]
    to = functools.partial(send, mesh_sizes=sizes)
    q_factor = math.log2(math.e) / math.sqrt(width // HEADS)

    lon_count = sizes[1]
    lon = lax.axis_index("lon")

    def among(value, partner):
        return lax.ppermute(value, "lon", [(partner(i), i) for i in range(lon_count)])

    def joined(bit, mine, theirs):
        low = (lon // bit) % 2 == 0
        return jnp.concatenate([jnp.where(low, mine, theirs), jnp.where(low, theirs, mine)], axis=0)

    x = hidden[0]
    flat = lambda a: a.reshape(-1, width)
    top = to(flat(x[core - rim :]), down=1, right=0)
    bottom = to(flat(x[:rim]), down=-1, right=0)
    emb = embedding(timestep, time_weight.shape[0])
    kv_rows = jnp.transpose(cross_kv, (0, 2, 1))
    own_head, mod = prepare(emb, time_weight, modulation_bias, context[0], kv_rows)
    own_head, top, bottom = lax.optimization_barrier((own_head, top, bottom))
    other = among(own_head, lambda i: i ^ 1)
    rows = lambda a: a.reshape(rim, core, width)
    first, last = pack(x, rows(top), rows(bottom))
    left = to(last, down=0, right=1)
    right = to(first, down=0, right=-1)
    two = joined(1, own_head, other)
    x, first, last, two = lax.optimization_barrier((x, first, last, two))
    far_two = among(two, lambda i: i ^ 2)
    x_core = flat(x)
    qkv_core = core_qkv(q_factor, x_core, mod, qkv_weight)
    four = joined(2, two, far_two)
    qkv_core, four = lax.optimization_barrier((qkv_core, four))
    arrived = [four] + [among(four, lambda i, k=k: (i + 4 * k) % lon_count) for k in (1, 2, 3)]
    column = (lon // 4).astype(jnp.int32)[None]

    h1, cq = tile_self(
        core,
        rim,
        q_factor,
        x_core,
        (left, right, top, bottom),
        qkv_core,
        mod,
        (qkv_weight, out_weight, cross_q),
    )
    span = half + rim
    edge, block = rim * span, core * span
    top_made, bottom_made, main = tile_text(
        text, 0, (2 * edge, 2 * edge, block), column, h1, cq, arrived, cross_output_projection
    )
    high = to(top_made, down=-1, right=0)
    low = to(bottom_made, down=1, right=0)
    far = to(main, down=0, right=-1)
    passed_on = jnp.concatenate([low[:edge], high[:edge]], axis=0)
    h1, low, high, passed_on = lax.optimization_barrier((h1, low, high, passed_on))
    passed = to(passed_on, down=0, right=-1)
    (near,) = tile_text(
        text, 4 * edge + block, (block,), column, h1, cq, arrived, cross_output_projection
    )
    shape = lambda a: a.reshape(-1, span, width)
    lat = lax.axis_index("lat").astype(jnp.int32)[None]
    return merge(sizes[0], lat, rim, *(shape(a) for a in (near, far, low, high, passed)))[None]


def solution(mesh):
    in_specs = (
        P(None, "lat", "lon", None),
        P(),
        P(),
        P(),
        P(),
        P(),
        P(),
        P(),
        P(None, None, "lon"),
        P(),
    )
    out_specs = P(None, "lat", "lon", None)
    sizes = (mesh.shape["lat"], mesh.shape["lon"])
    return jax.shard_map(
        functools.partial(local, sizes), mesh=mesh, in_specs=in_specs, out_specs=out_specs, check_vma=False
    )
```

```python
import functools
import math

import jax
import jax.numpy as jnp
from jax import lax
from jax.experimental import pallas as pl
from jax.experimental.pallas import tpu as pltpu
from jax.sharding import PartitionSpec as P

HEADS = 16
PAIRS = HEADS // 2
HALO = 4
LANES = 128
WIN = 256
TEXT_PAD = 384
VMEM = 60 * 1024 * 1024
SMALL = 30 * 1024 * 1024
NN = (((1,), (0,)), ((), ()))
NT = (((1,), (1,)), ((), ()))
BF16, F32 = jnp.bfloat16, jnp.float32
ANY = pl.BlockSpec(memory_space=pl.ANY)
LOCAL = pl.BlockSpec(memory_space=pltpu.VMEM)


def waves(timestep, size):
    half = size // 2
    freqs = jnp.exp(-math.log(10000.0) * jnp.arange(half, dtype=F32) / half)
    angle = timestep.astype(F32)[:, None] * freqs[None, :]
    return jnp.cos(angle), jnp.sin(angle)


def begin(pairs, sems, first):
    made = [pltpu.make_async_copy(a, b, sems.at[first + n]) for n, (a, b) in enumerate(pairs)]
    for c in made:
        c.start()
    return made


def finish_all(made):
    for c in made:
        c.wait()


def normalise(x_ref, at, count, mod_ref, u_ref):
    rows = 32
    blocks = count // rows
    gain = 1.0 + mod_ref[1:2, :]
    shift = mod_ref[0:1, :]

    def norm(i, carry):
        x = x_ref[pl.ds(pl.multiple_of(at + i * rows, rows), rows), :].astype(F32)
        mean = jnp.mean(x, axis=-1, keepdims=True)
        centred = x - mean
        var = jnp.mean(centred * centred, axis=-1, keepdims=True)
        normed = centred * lax.rsqrt(var + 1e-06)
        u_ref[pl.ds(pl.multiple_of(i * rows, rows), rows), :] = (normed * gain + shift).astype(BF16)
        return carry

    lax.fori_loop(0, blocks, norm, 0, unroll=next(n for n in (7, 6, 4, 2, 1) if blocks % n == 0))


def column_parts(total, size):
    return [(c, min(size, total - c)) for c in range(0, total, size)]


def weight_pairs(w_hbm, w_s, size):
    return [
        (w_hbm.at[:, pl.ds(c, n)], w_s.at[:, pl.ds(c, n)]) for c, n in column_parts(w_hbm.shape[1], size)
    ]


def project_qkv(u_ref, w_s, waits, size, width, q_factor, out_ref, at, done=lambda c, n: None):
    count = u_ref.shape[0]
    for wait, (c, n) in zip(waits, column_parts(w_s.shape[1], size)):
        wait.wait()
        made = jnp.dot(u_ref[...], w_s[:, c : c + n], preferred_element_type=F32)
        if c < width:
            ids = lax.broadcasted_iota(jnp.int32, (1, n), 1)
            made = made * jnp.where(ids < width - c, q_factor, 1.0)
        out_ref[at : at + count, c : c + n] = made.astype(BF16)
        done(c, n)


def band(low, high, dims, axis):
    ids = lax.broadcasted_iota(jnp.int32, dims, axis)
    return ((ids >= low) & (ids < high)).astype(F32).astype(BF16)


def pair_start(t):
    return t * LANES


def spare_columns(t, channels):
    return WIN - 64 if t * (2 * channels - LANES) + 2 * channels <= WIN - 64 else 0


def reciprocal(x):
    r = pl.reciprocal(x, approx=True)
    return r * (2.0 - x * r)


def pairs_unshifted(channels, q_ref, scores, values, p_refs, bad_ref, rows, out_ref):
    count = q_ref.shape[0]
    parts = [slice(c, c + rows) for c in range(0, count, rows)]
    gap = 2 * channels - LANES

    def close(t, p_ref, v, part):
        spare = spare_columns(t, channels)
        o = lax.dot_general(p_ref[part, :], v[0], v[1], preferred_element_type=F32)
        ids = lax.broadcasted_iota(jnp.int32, (1, WIN), 1)
        sum_a = o[:, spare : spare + 1]
        sum_b = o[:, spare + 32 : spare + 33]
        low, high = 2.0**-100, 2.0**100
        good = (sum_a >= low) & (sum_a <= high) & (sum_b >= low) & (sum_b <= high)
        bad_ref[...] = jnp.maximum(bad_ref[...], jnp.max(jnp.where(good, 0.0, 1.0), axis=0, keepdims=True))
        start = gap * t
        scale = jnp.where(ids < start + channels, reciprocal(sum_a), reciprocal(sum_b))
        cols = pl.ds(pair_start(t), WIN)
        old = out_ref[part, cols].astype(F32)
        inside = (ids >= start) & (ids < start + 2 * channels)
        out_ref[part, cols] = jnp.where(inside, o * scale, old).astype(BF16)

    bad_ref[...] = jnp.zeros_like(bad_ref)
    for part in parts:
        scores(0, 0, part, p_refs[0])
    for t in range(PAIRS):
        v = values(t, gap * t)
        for part in parts:
            if t + 1 < PAIRS:
                scores(t + 1, gap * (t + 1), part, p_refs[(t + 1) % 2])
            close(t, p_refs[t % 2], v, part)


def heads_shifted(channels, q_ref, keys, key_dims, values, value_dims, valid, out_ref):
    count, width = q_ref.shape
    rows = 64

    def one(n, carry):
        h = n // (count // rows)
        part = pl.ds(pl.multiple_of((n % (count // rows)) * rows, rows), rows)
        t = jnp.minimum((h * channels) // LANES, (width - WIN) // LANES)
        start = pl.multiple_of(t * LANES, LANES)
        offset = h * channels - start
        cols = pl.ds(start, WIN)
        q = q_ref[part, cols] * band(offset, offset + channels, (1, WIN), 1)
        s = lax.dot_general(q, keys(start), key_dims, preferred_element_type=F32)
        if valid < s.shape[1]:
            s = jnp.where(lax.broadcasted_iota(jnp.int32, s.shape, 1) < valid, s, -jnp.inf)
        p = jnp.exp2(s - jnp.max(s, axis=-1, keepdims=True))
        total = jnp.sum(p, axis=-1, keepdims=True)
        o = lax.dot_general(p.astype(BF16), values(start), value_dims, preferred_element_type=F32) / total
        ids = lax.broadcasted_iota(jnp.int32, (1, WIN), 1)
        old = out_ref[part, cols].astype(F32)
        inside = (ids >= offset) & (ids < offset + channels)
        out_ref[part, cols] = jnp.where(inside, o, old).astype(BF16)
        return carry

    lax.fori_loop(0, HEADS * (count // rows), one, 0)


def attend_self(channels, q_ref, k_ref, v_ref, vv_ref, p_refs, bad_ref, rows, out_ref):
    n = k_ref.shape[0]

    def scores(t, start, part, p_ref):
        cols = pl.ds(pair_start(t), WIN)
        q = q_ref[part, cols]
        for j in range(2):
            low = start + j * channels
            s = lax.dot_general(
                q * band(low, low + channels, (1, WIN), 1), k_ref[:, cols], NT, preferred_element_type=F32
            )
            p_ref[part, j * n : (j + 1) * n] = jnp.exp2(s).astype(BF16)

    def values(t, start):
        v = v_ref[:, pl.ds(pair_start(t), WIN)]
        spare = spare_columns(t, channels)
        for j in range(2):
            low, mark = start + j * channels, spare + 32 * j
            vv_ref[j * n : (j + 1) * n, :] = v * band(low, low + channels, (1, WIN), 1) + band(
                mark, mark + 32, (1, WIN), 1
            )
        return vv_ref[...], NN

    pairs_unshifted(channels, q_ref, scores, values, p_refs, bad_ref, rows, out_ref)

    @pl.when(jnp.max(bad_ref[...]) > 0.0)
    def _():
        heads_shifted(
            channels,
            q_ref,
            lambda start: k_ref[:, pl.ds(start, WIN)],
            NT,
            lambda start: v_ref[:, pl.ds(start, WIN)],
            NN,
            n,
            out_ref,
        )


def attend_text(channels, text, q_ref, kv_ref, p_refs, bad_ref, rows, out_ref):
    n = kv_ref.shape[1] // 2

    def scores(t, start, part, p_ref):
        k = kv_ref[pl.ds(pair_start(t), WIN), :n]
        pair = [
            k * band(start + j * channels, start + (j + 1) * channels, (WIN, 1), 0) for j in range(2)
        ]
        s = lax.dot_general(
            q_ref[part, pl.ds(pair_start(t), WIN)],
            jnp.concatenate(pair, axis=1),
            NN,
            preferred_element_type=F32,
        )
        p_ref[part, :] = jnp.exp2(s).astype(BF16)

    def values(t, start):
        v = kv_ref[pl.ds(pair_start(t), WIN), n:]
        valid = band(0, text, (1, n), 1)
        spare = spare_columns(t, channels)
        pair = [
            v * band(start + j * channels, start + (j + 1) * channels, (WIN, 1), 0)
            + band(spare + 32 * j, spare + 32 * j + 32, (WIN, 1), 0) * valid
            for j in range(2)
        ]
        return jnp.concatenate(pair, axis=1), NT

    pairs_unshifted(channels, q_ref, scores, values, p_refs, bad_ref, rows, out_ref)

    @pl.when(jnp.max(bad_ref[...]) > 0.0)
    def _():
        heads_shifted(
            channels,
            q_ref,
            lambda start: kv_ref[pl.ds(start, WIN), :n],
            NN,
            lambda start: kv_ref[pl.ds(start, WIN), n:],
            NT,
            text,
            out_ref,
        )


def prepare_kernel(
    cos_ref, sin_ref, tw_hbm, bias_hbm, context_hbm, kv_hbm, head_out, mod_out, tw_s, bias_s, context_s, kv_s, own_s, mod_s, sems
):
    width = bias_s.shape[1]
    text = context_s.shape[0]
    half = cos_ref.shape[1]
    lanes = own_s.shape[1] // 2
    waits = begin([(context_hbm, context_s), (kv_hbm, kv_s), (tw_hbm, tw_s), (bias_hbm, bias_s)], sems, 2)
    own_s[...] = jnp.zeros_like(own_s)
    embed = [(w / (1.0 + jnp.exp(-w))).astype(BF16) for w in (cos_ref[...], sin_ref[...])]
    finish_all(waits[:2])
    for j in range(2):
        made = lax.dot_general(kv_s[j], context_s[...], NT, preferred_element_type=F32)
        own_s[:, j * lanes : j * lanes + text] = made.astype(BF16)
    sent = begin([(own_s, head_out)], sems, 0)
    finish_all(waits[2:])
    for j in range(3):
        cols = slice(j * width, (j + 1) * width)
        made = bias_s[j : j + 1, :]
        for n, part in enumerate(embed):
            rows = slice(n * half, (n + 1) * half)
            made = made + jnp.dot(part, tw_s[rows, cols], preferred_element_type=F32)
        mod_s[j : j + 1, :] = made
    sent += begin([(mod_s, mod_out)], sems, 1)
    finish_all(sent)


def prepare(cos, sin, time_weight, bias, context, cross_kv):
    width = bias.shape[1]
    channels = cross_kv.shape[1]
    return pl.pallas_call(
        prepare_kernel,
        out_shape=[
            jax.ShapeDtypeStruct((channels, 2 * TEXT_PAD), BF16),
            jax.ShapeDtypeStruct(bias.shape, F32),
        ],
        in_specs=[LOCAL] * 2 + [ANY] * 4,
        out_specs=[ANY, ANY],
        scratch_shapes=[
            pltpu.VMEM(time_weight.shape, BF16),
            pltpu.VMEM(bias.shape, F32),
            pltpu.VMEM(context.shape, BF16),
            pltpu.VMEM(cross_kv.shape, BF16),
            pltpu.VMEM((channels, 2 * TEXT_PAD), BF16),
            pltpu.VMEM(bias.shape, F32),
            pltpu.SemaphoreType.DMA((6,)),
        ],
        compiler_params=pltpu.CompilerParams(vmem_limit_bytes=VMEM),
        cost_estimate=pl.CostEstimate(
            flops=4 * context.shape[0] * width * channels, bytes_accessed=6 * 1024 * 1024, transcendentals=0
        ),
    )(cos, sin, time_weight, bias, context, cross_kv)


def pack_kernel(x_ref, top_ref, bottom_ref, first_out, last_out, first_s, last_s):
    rim, core = top_ref.shape[0], x_ref.shape[0]
    rows = [(top_ref, a) for a in range(rim)] + [(x_ref, r) for r in range(core)]
    rows += [(bottom_ref, a) for a in range(rim)]
    for n, (ref, r) in enumerate(rows):
        tokens = ref[r].astype(F32)
        first_s[rim * n : rim * (n + 1), :] = tokens[:rim]
        last_s[rim * n : rim * (n + 1), :] = tokens[core - rim :]
    first_out[...] = first_s[...].astype(BF16)
    last_out[...] = last_s[...].astype(BF16)


def pack(x, top, bottom):
    rim, core, width = top.shape
    count = rim * (core + 2 * rim)
    return pl.pallas_call(
        pack_kernel,
        out_shape=[jax.ShapeDtypeStruct((count, width), BF16)] * 2,
        in_specs=[LOCAL] * 3,
        out_specs=[LOCAL] * 2,
        scratch_shapes=[pltpu.VMEM((count, width), F32)] * 2,
        compiler_params=pltpu.CompilerParams(vmem_limit_bytes=SMALL),
        cost_estimate=pl.CostEstimate(flops=0, bytes_accessed=3 * 1024 * 1024, transcendentals=0),
    )(x, top, bottom)


QKV_PART = 512


def core_kernel(q_factor, x_ref, mod_ref, w_hbm, out_hbm, u_s, w_s, out_s, sems):
    waits = begin(weight_pairs(w_hbm, w_s, QKV_PART), sems, 0)
    count, width = x_ref.shape
    normalise(x_ref, 0, count, mod_ref, u_s)
    sent = []

    def done(c, n):
        cols = pl.ds(c, n)
        sent.extend(begin([(out_s.at[:, cols], out_hbm.at[:, cols])], sems, 8 + len(sent)))

    project_qkv(u_s, w_s, waits, QKV_PART, width, q_factor, out_s, 0, done)
    finish_all(sent)


def core_qkv(q_factor, x, mod, weight):
    count, width = x.shape
    total = weight.shape[1]
    return pl.pallas_call(
        functools.partial(core_kernel, q_factor),
        out_shape=jax.ShapeDtypeStruct((count, total), BF16),
        in_specs=[LOCAL, LOCAL, ANY],
        out_specs=ANY,
        scratch_shapes=[
            pltpu.VMEM((count, width), BF16),
            pltpu.VMEM((width, total), BF16),
            pltpu.VMEM((count, total), BF16),
            pltpu.SemaphoreType.DMA((16,)),
        ],
        compiler_params=pltpu.CompilerParams(vmem_limit_bytes=VMEM),
        cost_estimate=pl.CostEstimate(
            flops=2 * count * width * total,
            bytes_accessed=2 * (width * total + count * (width + total)),
            transcendentals=0,
        ),
    )(x, mod, weight)


def regroup(core, rim, source_ref, target_ref):
    half = core // 2
    left = core * core
    right = left + rim * (core + 2 * rim)
    top = right + rim * (core + 2 * rim)
    bottom = top + rim * core
    at = 0

    def take(*pieces):
        nonlocal at
        for start, n in pieces:
            target_ref[at : at + n, :] = source_ref[start : start + n, :]
            at += n

    for base, row in ((top, 0), (bottom, rim + core)):
        for a in range(rim):
            take((left + rim * (row + a), rim), (base + core * a, half))
        for a in range(rim):
            take((base + core * a + half, half), (right + rim * (row + a), rim))
    for r in range(core):
        take((left + rim * (rim + r), rim), (core * r, half))
    for r in range(core):
        take((core * r + half, half), (right + rim * (rim + r), rim))


def tile_kernel(
    core,
    rim,
    rows,
    q_factor,
    x_core,
    left,
    right,
    top,
    bottom,
    qkv_core,
    mod_ref,
    w_hbm,
    wo_hbm,
    wq_hbm,
    h1_out,
    cq_out,
    x_s,
    qkv_s,
    u_s,
    w_s,
    wo_s,
    wq_s,
    vv_s,
    p_a,
    p_b,
    attn_s,
    h1_s,
    hg_s,
    bad_s,
    sems,
):
    width = x_core.shape[1]
    channels = width // HEADS
    inner = x_core.shape[0]
    outer = sum(a.shape[0] for a in (left, right, top, bottom))
    total = inner + outer
    pairs, at = [], inner
    for part in (left, right, top, bottom):
        pairs.append((part, x_s.at[pl.ds(at, part.shape[0])]))
        at += part.shape[0]
    waits_x = begin(pairs, sems, 0)
    waits_w = begin(weight_pairs(w_hbm, w_s, QKV_PART), sems, 4)
    waits_qkv = begin([(qkv_core, qkv_s.at[pl.ds(0, inner)])], sems, 12)
    waits_later = begin(
        [(x_core, x_s.at[pl.ds(0, inner)]), (wo_hbm, wo_s), (wq_hbm, wq_s)],
        sems,
        13,
    )
    finish_all(waits_x)
    normalise(x_s, inner, outer, mod_ref, u_s)
    project_qkv(u_s, w_s, waits_w, QKV_PART, width, q_factor, qkv_s, inner)
    finish_all(waits_qkv)
    attend_self(
        channels,
        qkv_s.at[:, pl.ds(0, width)],
        qkv_s.at[:, pl.ds(width, width)],
        qkv_s.at[:, pl.ds(2 * width, width)],
        vv_s,
        (p_a, p_b),
        bad_s,
        rows,
        attn_s,
    )
    finish_all(waits_later)
    step = total // 2
    for r in range(0, total, step):
        part = slice(r, r + step)
        mixed = jnp.dot(attn_s[part, :], wo_s[...], preferred_element_type=F32)
        h1_s[part, :] = x_s[part, :].astype(F32) + mod_ref[2:3, :] * mixed
    regroup(core, rim, h1_s, hg_s)
    waits_h = begin([(hg_s, h1_out)], sems, 16)
    for r in range(0, total, step):
        part = slice(r, r + step)
        made = jnp.dot(hg_s[part, :].astype(BF16), wq_s[...], preferred_element_type=F32)
        x_s[part, :] = (made * q_factor).astype(BF16)
        here = pl.ds(r, step)
        waits_h += begin([(x_s.at[here], cq_out.at[here])], sems, 17 + r // step)
    finish_all(waits_h)


def tile_self(core, rim, q_factor, x_core, rims, qkv_core, mod, weights):
    inner, width = x_core.shape
    outer = sum(a.shape[0] for a in rims)
    total = inner + outer
    wide = weights[0].shape[1]
    return pl.pallas_call(
        functools.partial(tile_kernel, core, rim, 256, q_factor),
        out_shape=[
            jax.ShapeDtypeStruct((total, width), F32),
            jax.ShapeDtypeStruct((total, width), BF16),
        ],
        in_specs=[ANY] + [LOCAL] * 4 + [ANY, LOCAL] + [ANY] * 3,
        out_specs=[ANY, ANY],
        scratch_shapes=[
            pltpu.VMEM((total, width), BF16),
            pltpu.VMEM((total, wide), BF16),
            pltpu.VMEM((outer, width), BF16),
            pltpu.VMEM((width, wide), BF16),
            pltpu.VMEM((width, width), BF16),
            pltpu.VMEM((width, width), BF16),
            pltpu.VMEM((2 * total, WIN), BF16),
            pltpu.VMEM((total, 2 * total), BF16),
            pltpu.VMEM((total, 2 * total), BF16),
            pltpu.VMEM((total, width), BF16),
            pltpu.VMEM((total, width), F32),
            pltpu.VMEM((total, width), F32),
            pltpu.VMEM((1, LANES), F32),
            pltpu.SemaphoreType.DMA((20,)),
        ],
        compiler_params=pltpu.CompilerParams(vmem_limit_bytes=50 * 1024 * 1024),
        cost_estimate=pl.CostEstimate(
            flops=2 * outer * width * wide + 16 * total * width * total + 4 * total * width * width,
            bytes_accessed=2 * width * (wide + 2 * width) + 2 * inner * wide + 6 * total * width,
            transcendentals=HEADS * total * total,
        ),
    )(x_core, *rims, qkv_core, mod, *weights)


def text_kernel(text, first, parts, column_ref, h1, cq, t0, t1, t2, t3, wc_hbm, *rest):
    outs = rest[: len(parts)]
    q_s, h_s, kv_s, wc_s, p_a, p_b, attn_s, bad_s, sems = rest[len(parts) :]
    count, width = q_s.shape
    rows = pl.ds(first, count)
    pairs = [(cq.at[rows], q_s)]
    for k, arrived in enumerate((t0, t1, t2, t3)):
        size = arrived.shape[0]
        where = pl.multiple_of(lax.rem(column_ref[0] + k, 4) * size, size)
        pairs.append((arrived, kv_s.at[pl.ds(where, size), :]))
    waits = begin(pairs, sems, 0)
    waits_later = begin([(wc_hbm, wc_s), (h1.at[rows], h_s)], sems, 5)
    finish_all(waits)
    attend_text(width // HEADS, text, q_s, kv_s, (p_a, p_b), bad_s, count, attn_s)
    finish_all(waits_later)
    made = h_s[...] + jnp.dot(attn_s[...], wc_s[...], preferred_element_type=F32)
    at = 0
    for out, n in zip(outs, parts):
        out[...] = made[at : at + n].astype(BF16)
        at += n


def tile_text(text, first, parts, column, h1, cq, arrived, weight):
    count = sum(parts)
    width = h1.shape[1]
    padded = arrived[0].shape[1] // 2
    return pl.pallas_call(
        functools.partial(text_kernel, text, first, parts),
        out_shape=[jax.ShapeDtypeStruct((n, width), BF16) for n in parts],
        in_specs=[pl.BlockSpec(memory_space=pltpu.SMEM)] + [ANY] * 2 + [LOCAL] * 4 + [ANY],
        out_specs=[LOCAL] * len(parts),
        scratch_shapes=[
            pltpu.VMEM((count, width), BF16),
            pltpu.VMEM((count, width), F32),
            pltpu.VMEM((width, 2 * padded), BF16),
            pltpu.VMEM((width, width), BF16),
            pltpu.VMEM((count, 2 * padded), BF16),
            pltpu.VMEM((count, 2 * padded), BF16),
            pltpu.VMEM((count, width), BF16),
            pltpu.VMEM((1, LANES), F32),
            pltpu.SemaphoreType.DMA((7,)),
        ],
        compiler_params=pltpu.CompilerParams(vmem_limit_bytes=50 * 1024 * 1024),
        cost_estimate=pl.CostEstimate(
            flops=16 * count * width * padded + 2 * count * width * width,
            bytes_accessed=2 * width * (width + 2 * padded) + 8 * count * width,
            transcendentals=HEADS * count * padded,
        ),
    )(column, h1, cq, *arrived, weight)


def merge_kernel(lat_count, rim, lat_ref, near, far, low, high, passed, out_hbm, near_s, out_s, sems):
    lat = lat_ref[0]
    core = near.shape[0]
    rows = 8
    steps = range(core // rows)
    waits = begin([(near.at[pl.ds(i * rows, rows)], near_s.at[pl.ds(i * rows, rows)]) for i in steps], sems, 0)
    sent = []

    def average(body, extra, first):
        n = body.shape[0]
        ids = lax.broadcasted_iota(jnp.int32, (n, 1, 1), 0) + first
        shared = ((ids < rim) & (lat > 0)) | ((ids >= core - rim) & (lat < lat_count - 1))
        body = body.astype(F32) if extra is None else body.astype(F32) + extra.astype(F32)
        return body * jnp.where(shared, 0.5, 1.0)

    for i in steps:
        waits[i].wait()
        for first in range(i * rows, (i + 1) * rows, rim):
            part = slice(first, first + rim)
            extra = (None, None)
            if first == 0:
                extra = (low[rim:], passed[:rim])
            if first == core - rim:
                extra = (high[rim:], passed[rim:])
            a, b = average(near_s[part], extra[0], first), average(far[part], extra[1], first)
            made = jnp.concatenate([a[:, :8], (a[:, 8:] + b[:, :8]) * 0.5, b[:, 8:]], axis=1)
            out_s[part] = made.astype(BF16)
        here = pl.ds(i * rows, rows)
        sent += begin([(out_s.at[here], out_hbm.at[here])], sems, len(steps) + i)
    finish_all(sent)


def merge(lat_count, lat, rim, near, far, low, high, passed):
    core, span, width = near.shape
    return pl.pallas_call(
        functools.partial(merge_kernel, lat_count, rim),
        out_shape=jax.ShapeDtypeStruct((core, core, width), BF16),
        in_specs=[pl.BlockSpec(memory_space=pltpu.SMEM), ANY] + [LOCAL] * 4,
        out_specs=ANY,
        scratch_shapes=[
            pltpu.VMEM((core, span, width), BF16),
            pltpu.VMEM((core, core, width), BF16),
            pltpu.SemaphoreType.DMA((6,)),
        ],
        compiler_params=pltpu.CompilerParams(vmem_limit_bytes=SMALL),
        cost_estimate=pl.CostEstimate(
            flops=4 * core * core * width, bytes_accessed=8 * core * core * width, transcendentals=0
        ),
    )(lat, near, far, low, high, passed)


def send(value, mesh_sizes, down, right):
    rows, cols = mesh_sizes
    pairs = [
        (r * cols + c, (r + down) * cols + (c + right) % cols)
        for r in range(rows)
        for c in range(cols)
        if 0 <= r + down < rows
    ]
    return lax.ppermute(value, ("lat", "lon"), pairs)


def local(
    sizes,
    hidden,
    timestep,
    context,
    time_weight,
    modulation_bias,
    qkv_weight,
    out_weight,
    cross_q,
    cross_kv,
    cross_output_projection,
):
    core, width = hidden.shape[1], hidden.shape[3]
    half = core // 2
    rim = HALO
    text = context.shape[1]
    lon_count = sizes[1]
    to = functools.partial(send, mesh_sizes=sizes)
    q_factor = math.log2(math.e) / math.sqrt(width // HEADS)

    lon_count = sizes[1]
    lon = lax.axis_index("lon")

    def among(value, partner):
        return lax.ppermute(value, "lon", [(partner(i), i) for i in range(lon_count)])

    def joined(bit, mine, theirs):
        low = (lon // bit) % 2 == 0
        return jnp.concatenate([jnp.where(low, mine, theirs), jnp.where(low, theirs, mine)], axis=0)

    x = hidden[0]
    flat = lambda a: a.reshape(-1, width)
    top = to(flat(x[core - rim :]), down=1, right=0)
    bottom = to(flat(x[:rim]), down=-1, right=0)
    cos, sin = waves(timestep, time_weight.shape[0])
    kv_rows = jnp.transpose(cross_kv, (0, 2, 1))
    own_head, mod = prepare(cos, sin, time_weight, modulation_bias, context[0], kv_rows)
    own_head, top, bottom = lax.optimization_barrier((own_head, top, bottom))
    other = among(own_head, lambda i: i ^ 1)
    rows = lambda a: a.reshape(rim, core, width)
    first, last = pack(x, rows(top), rows(bottom))
    left = to(last, down=0, right=1)
    right = to(first, down=0, right=-1)
    two = joined(1, own_head, other)
    x, first, last, two = lax.optimization_barrier((x, first, last, two))
    far_two = among(two, lambda i: i ^ 2)
    x_core = flat(x)
    qkv_core = core_qkv(q_factor, x_core, mod, qkv_weight)
    four = joined(2, two, far_two)
    qkv_core, four = lax.optimization_barrier((qkv_core, four))
    arrived = [four] + [among(four, lambda i, k=k: (i + 4 * k) % lon_count) for k in (1, 2, 3)]
    column = (lon // 4).astype(jnp.int32)[None]

    h1, cq = tile_self(
        core,
        rim,
        q_factor,
        x_core,
        (left, right, top, bottom),
        qkv_core,
        mod,
        (qkv_weight, out_weight, cross_q),
    )
    span = half + rim
    edge, block = rim * span, core * span
    top_made, bottom_made, main = tile_text(
        text, 0, (2 * edge, 2 * edge, block), column, h1, cq, arrived, cross_output_projection
    )
    high = to(top_made, down=-1, right=0)
    low = to(bottom_made, down=1, right=0)
    far = to(main, down=0, right=-1)
    (near,) = tile_text(
        text, 4 * edge + block, (block,), column, h1, cq, arrived, cross_output_projection
    )
    near, low, high = lax.optimization_barrier((near, low, high))
    passed = to(jnp.concatenate([low[:edge], high[:edge]], axis=0), down=0, right=-1)
    shape = lambda a: a.reshape(-1, span, width)
    lat = lax.axis_index("lat").astype(jnp.int32)[None]
    return merge(sizes[0], lat, rim, *(shape(a) for a in (near, far, low, high, passed)))[None]


def solution(mesh):
    in_specs = (
        P(None, "lat", "lon", None),
        P(),
        P(),
        P(),
        P(),
        P(),
        P(),
        P(),
        P(None, None, "lon"),
        P(),
    )
    out_specs = P(None, "lat", "lon", None)
    sizes = (mesh.shape["lat"], mesh.shape["lon"])
    return jax.shard_map(
        functools.partial(local, sizes), mesh=mesh, in_specs=in_specs, out_specs=out_specs, check_vma=False
    )
```

```python
import functools
import math

import jax
import jax.numpy as jnp
from jax import lax
from jax.experimental import pallas as pl
from jax.experimental.pallas import tpu as pltpu
from jax.sharding import PartitionSpec as P

HEADS = 16
PAIRS = HEADS // 2
HALO = 4
LANES = 128
WIN = 256
TEXT_PAD = 384
VMEM = 60 * 1024 * 1024
SMALL = 30 * 1024 * 1024
NN = (((1,), (0,)), ((), ()))
NT = (((1,), (1,)), ((), ()))
BF16, F32 = jnp.bfloat16, jnp.float32
ANY = pl.BlockSpec(memory_space=pl.ANY)
LOCAL = pl.BlockSpec(memory_space=pltpu.VMEM)


def waves(timestep, size):
    half = size // 2
    freqs = jnp.exp(-math.log(10000.0) * jnp.arange(half, dtype=F32) / half)
    angle = timestep.astype(F32)[:, None] * freqs[None, :]
    return jnp.cos(angle), jnp.sin(angle)


def begin(pairs, sems, first):
    made = [pltpu.make_async_copy(a, b, sems.at[first + n]) for n, (a, b) in enumerate(pairs)]
    for c in made:
        c.start()
    return made


def finish_all(made):
    for c in made:
        c.wait()


def normalise(x_ref, at, count, mod_ref, u_ref):
    rows = 32
    blocks = count // rows
    gain = 1.0 + mod_ref[1:2, :]
    shift = mod_ref[0:1, :]

    def norm(i, carry):
        x = x_ref[pl.ds(pl.multiple_of(at + i * rows, rows), rows), :].astype(F32)
        mean = jnp.mean(x, axis=-1, keepdims=True)
        centred = x - mean
        var = jnp.mean(centred * centred, axis=-1, keepdims=True)
        normed = centred * lax.rsqrt(var + 1e-06)
        u_ref[pl.ds(pl.multiple_of(i * rows, rows), rows), :] = (normed * gain + shift).astype(BF16)
        return carry

    lax.fori_loop(0, blocks, norm, 0, unroll=next(n for n in (7, 6, 4, 2, 1) if blocks % n == 0))


def column_parts(total, size):
    return [(c, min(size, total - c)) for c in range(0, total, size)]


def weight_pairs(w_hbm, w_s, size):
    return [
        (w_hbm.at[:, pl.ds(c, n)], w_s.at[:, pl.ds(c, n)]) for c, n in column_parts(w_hbm.shape[1], size)
    ]


def project_qkv(u_ref, w_s, waits, size, width, q_factor, out_ref, at, done=lambda c, n: None):
    count = u_ref.shape[0]
    for wait, (c, n) in zip(waits, column_parts(w_s.shape[1], size)):
        wait.wait()
        made = jnp.dot(u_ref[...], w_s[:, c : c + n], preferred_element_type=F32)
        if c < width:
            ids = lax.broadcasted_iota(jnp.int32, (1, n), 1)
            made = made * jnp.where(ids < width - c, q_factor, 1.0)
        out_ref[at : at + count, c : c + n] = made.astype(BF16)
        done(c, n)


def band(low, high, dims, axis):
    ids = lax.broadcasted_iota(jnp.int32, dims, axis)
    return ((ids >= low) & (ids < high)).astype(F32).astype(BF16)


def pair_start(t):
    return t * LANES


def spare_columns(t, channels):
    return WIN - 64 if t * (2 * channels - LANES) + 2 * channels <= WIN - 64 else 0


def reciprocal(x):
    r = pl.reciprocal(x, approx=True)
    return r * (2.0 - x * r)


def pairs_unshifted(channels, q_ref, scores, values, p_refs, bad_ref, rows, out_ref):
    count = q_ref.shape[0]
    parts = [slice(c, c + rows) for c in range(0, count, rows)]
    gap = 2 * channels - LANES

    def close(t, p_ref, v, part):
        spare = spare_columns(t, channels)
        o = lax.dot_general(p_ref[part, :], v[0], v[1], preferred_element_type=F32)
        ids = lax.broadcasted_iota(jnp.int32, (1, WIN), 1)
        sum_a = o[:, spare : spare + 1]
        sum_b = o[:, spare + 32 : spare + 33]
        low, high = 2.0**-100, 2.0**100
        good = (sum_a >= low) & (sum_a <= high) & (sum_b >= low) & (sum_b <= high)
        bad_ref[...] = jnp.maximum(bad_ref[...], jnp.max(jnp.where(good, 0.0, 1.0), axis=0, keepdims=True))
        start = gap * t
        scale = jnp.where(ids < start + channels, reciprocal(sum_a), reciprocal(sum_b))
        cols = pl.ds(pair_start(t), WIN)
        old = out_ref[part, cols].astype(F32)
        inside = (ids >= start) & (ids < start + 2 * channels)
        out_ref[part, cols] = jnp.where(inside, o * scale, old).astype(BF16)

    bad_ref[...] = jnp.zeros_like(bad_ref)
    for part in parts:
        scores(0, 0, part, p_refs[0])
    for t in range(PAIRS):
        v = values(t, gap * t)
        for part in parts:
            if t + 1 < PAIRS:
                scores(t + 1, gap * (t + 1), part, p_refs[(t + 1) % 2])
            close(t, p_refs[t % 2], v, part)


def heads_shifted(channels, q_ref, keys, key_dims, values, value_dims, valid, out_ref):
    count, width = q_ref.shape
    rows = 64

    def one(n, carry):
        h = n // (count // rows)
        part = pl.ds(pl.multiple_of((n % (count // rows)) * rows, rows), rows)
        t = jnp.minimum((h * channels) // LANES, (width - WIN) // LANES)
        start = pl.multiple_of(t * LANES, LANES)
        offset = h * channels - start
        cols = pl.ds(start, WIN)
        q = q_ref[part, cols] * band(offset, offset + channels, (1, WIN), 1)
        s = lax.dot_general(q, keys(start), key_dims, preferred_element_type=F32)
        if valid < s.shape[1]:
            s = jnp.where(lax.broadcasted_iota(jnp.int32, s.shape, 1) < valid, s, -jnp.inf)
        p = jnp.exp2(s - jnp.max(s, axis=-1, keepdims=True))
        total = jnp.sum(p, axis=-1, keepdims=True)
        o = lax.dot_general(p.astype(BF16), values(start), value_dims, preferred_element_type=F32) / total
        ids = lax.broadcasted_iota(jnp.int32, (1, WIN), 1)
        old = out_ref[part, cols].astype(F32)
        inside = (ids >= offset) & (ids < offset + channels)
        out_ref[part, cols] = jnp.where(inside, o, old).astype(BF16)
        return carry

    lax.fori_loop(0, HEADS * (count // rows), one, 0)


def attend_self(channels, q_ref, k_ref, v_ref, vv_ref, p_refs, bad_ref, rows, out_ref):
    n = k_ref.shape[0]

    def scores(t, start, part, p_ref):
        cols = pl.ds(pair_start(t), WIN)
        q = q_ref[part, cols]
        for j in range(2):
            low = start + j * channels
            s = lax.dot_general(
                q * band(low, low + channels, (1, WIN), 1), k_ref[:, cols], NT, preferred_element_type=F32
            )
            p_ref[part, j * n : (j + 1) * n] = jnp.exp2(s).astype(BF16)

    def values(t, start):
        v = v_ref[:, pl.ds(pair_start(t), WIN)]
        spare = spare_columns(t, channels)
        for j in range(2):
            low, mark = start + j * channels, spare + 32 * j
            vv_ref[j * n : (j + 1) * n, :] = v * band(low, low + channels, (1, WIN), 1) + band(
                mark, mark + 32, (1, WIN), 1
            )
        return vv_ref[...], NN

    pairs_unshifted(channels, q_ref, scores, values, p_refs, bad_ref, rows, out_ref)

    @pl.when(jnp.max(bad_ref[...]) > 0.0)
    def _():
        heads_shifted(
            channels,
            q_ref,
            lambda start: k_ref[:, pl.ds(start, WIN)],
            NT,
            lambda start: v_ref[:, pl.ds(start, WIN)],
            NN,
            n,
            out_ref,
        )


def attend_text(channels, text, q_ref, kv_ref, p_refs, bad_ref, rows, out_ref):
    n = kv_ref.shape[1] // 2

    def scores(t, start, part, p_ref):
        k = kv_ref[pl.ds(pair_start(t), WIN), :n]
        pair = [
            k * band(start + j * channels, start + (j + 1) * channels, (WIN, 1), 0) for j in range(2)
        ]
        s = lax.dot_general(
            q_ref[part, pl.ds(pair_start(t), WIN)],
            jnp.concatenate(pair, axis=1),
            NN,
            preferred_element_type=F32,
        )
        p_ref[part, :] = jnp.exp2(s).astype(BF16)

    def values(t, start):
        v = kv_ref[pl.ds(pair_start(t), WIN), n:]
        valid = band(0, text, (1, n), 1)
        spare = spare_columns(t, channels)
        pair = [
            v * band(start + j * channels, start + (j + 1) * channels, (WIN, 1), 0)
            + band(spare + 32 * j, spare + 32 * j + 32, (WIN, 1), 0) * valid
            for j in range(2)
        ]
        return jnp.concatenate(pair, axis=1), NT

    pairs_unshifted(channels, q_ref, scores, values, p_refs, bad_ref, rows, out_ref)

    @pl.when(jnp.max(bad_ref[...]) > 0.0)
    def _():
        heads_shifted(
            channels,
            q_ref,
            lambda start: kv_ref[pl.ds(start, WIN), :n],
            NN,
            lambda start: kv_ref[pl.ds(start, WIN), n:],
            NT,
            text,
            out_ref,
        )


def prepare_kernel(
    cos_ref, sin_ref, tw_hbm, bias_hbm, context_hbm, kv_hbm, head_out, mod_out, tw_s, bias_s, context_s, kv_s, own_s, mod_s, sems
):
    width = bias_s.shape[1]
    text = context_s.shape[0]
    half = cos_ref.shape[1]
    lanes = own_s.shape[1] // 2
    waits = begin([(context_hbm, context_s), (kv_hbm, kv_s), (tw_hbm, tw_s), (bias_hbm, bias_s)], sems, 2)
    own_s[...] = jnp.zeros_like(own_s)
    embed = [(w / (1.0 + jnp.exp(-w))).astype(BF16) for w in (cos_ref[...], sin_ref[...])]
    finish_all(waits[:2])
    for j in range(2):
        made = lax.dot_general(kv_s[j], context_s[...], NT, preferred_element_type=F32)
        own_s[:, j * lanes : j * lanes + text] = made.astype(BF16)
    sent = begin([(own_s, head_out)], sems, 0)
    finish_all(waits[2:])
    for j in range(3):
        cols = slice(j * width, (j + 1) * width)
        made = bias_s[j : j + 1, :]
        for n, part in enumerate(embed):
            rows = slice(n * half, (n + 1) * half)
            made = made + jnp.dot(part, tw_s[rows, cols], preferred_element_type=F32)
        mod_s[j : j + 1, :] = made
    sent += begin([(mod_s, mod_out)], sems, 1)
    finish_all(sent)


def prepare(cos, sin, time_weight, bias, context, cross_kv):
    width = bias.shape[1]
    channels = cross_kv.shape[1]
    return pl.pallas_call(
        prepare_kernel,
        out_shape=[
            jax.ShapeDtypeStruct((channels, 2 * TEXT_PAD), BF16),
            jax.ShapeDtypeStruct(bias.shape, F32),
        ],
        in_specs=[LOCAL] * 2 + [ANY] * 4,
        out_specs=[ANY, ANY],
        scratch_shapes=[
            pltpu.VMEM(time_weight.shape, BF16),
            pltpu.VMEM(bias.shape, F32),
            pltpu.VMEM(context.shape, BF16),
            pltpu.VMEM(cross_kv.shape, BF16),
            pltpu.VMEM((channels, 2 * TEXT_PAD), BF16),
            pltpu.VMEM(bias.shape, F32),
            pltpu.SemaphoreType.DMA((6,)),
        ],
        compiler_params=pltpu.CompilerParams(vmem_limit_bytes=VMEM),
        cost_estimate=pl.CostEstimate(
            flops=4 * context.shape[0] * width * channels, bytes_accessed=6 * 1024 * 1024, transcendentals=0
        ),
    )(cos, sin, time_weight, bias, context, cross_kv)


def join_kernel(place_ref, mine, theirs, out_ref):
    own, other = mine[...].astype(F32), theirs[...].astype(F32)

    @pl.when(place_ref[0] == 0)
    def _():
        out_ref[...] = jnp.concatenate([own, other], axis=0).astype(BF16)

    @pl.when(place_ref[0] != 0)
    def _():
        out_ref[...] = jnp.concatenate([other, own], axis=0).astype(BF16)


def join(place, mine, theirs):
    rows, lanes = mine.shape
    return pl.pallas_call(
        join_kernel,
        out_shape=jax.ShapeDtypeStruct((2 * rows, lanes), BF16),
        in_specs=[pl.BlockSpec(memory_space=pltpu.SMEM), LOCAL, LOCAL],
        out_specs=LOCAL,
        compiler_params=pltpu.CompilerParams(vmem_limit_bytes=SMALL),
        cost_estimate=pl.CostEstimate(flops=0, bytes_accessed=8 * rows * lanes, transcendentals=0),
    )(place, mine, theirs)


def pack_kernel(x_ref, top_ref, bottom_ref, first_out, last_out, first_s, last_s):
    rim, core = top_ref.shape[0], x_ref.shape[0]
    rows = [(top_ref, a) for a in range(rim)] + [(x_ref, r) for r in range(core)]
    rows += [(bottom_ref, a) for a in range(rim)]
    for n, (ref, r) in enumerate(rows):
        tokens = ref[r].astype(F32)
        first_s[rim * n : rim * (n + 1), :] = tokens[:rim]
        last_s[rim * n : rim * (n + 1), :] = tokens[core - rim :]
    first_out[...] = first_s[...].astype(BF16)
    last_out[...] = last_s[...].astype(BF16)


def pack(x, top, bottom):
    rim, core, width = top.shape
    count = rim * (core + 2 * rim)
    return pl.pallas_call(
        pack_kernel,
        out_shape=[jax.ShapeDtypeStruct((count, width), BF16)] * 2,
        in_specs=[LOCAL] * 3,
        out_specs=[LOCAL] * 2,
        scratch_shapes=[pltpu.VMEM((count, width), F32)] * 2,
        compiler_params=pltpu.CompilerParams(vmem_limit_bytes=SMALL),
        cost_estimate=pl.CostEstimate(flops=0, bytes_accessed=3 * 1024 * 1024, transcendentals=0),
    )(x, top, bottom)


QKV_PART = 512


def core_kernel(q_factor, x_ref, mod_ref, w_hbm, out_hbm, u_s, w_s, out_s, sems):
    waits = begin(weight_pairs(w_hbm, w_s, QKV_PART), sems, 0)
    count, width = x_ref.shape
    normalise(x_ref, 0, count, mod_ref, u_s)
    sent = []

    def done(c, n):
        cols = pl.ds(c, n)
        sent.extend(begin([(out_s.at[:, cols], out_hbm.at[:, cols])], sems, 8 + len(sent)))

    project_qkv(u_s, w_s, waits, QKV_PART, width, q_factor, out_s, 0, done)
    finish_all(sent)


def core_qkv(q_factor, x, mod, weight):
    count, width = x.shape
    total = weight.shape[1]
    return pl.pallas_call(
        functools.partial(core_kernel, q_factor),
        out_shape=jax.ShapeDtypeStruct((count, total), BF16),
        in_specs=[LOCAL, LOCAL, ANY],
        out_specs=ANY,
        scratch_shapes=[
            pltpu.VMEM((count, width), BF16),
            pltpu.VMEM((width, total), BF16),
            pltpu.VMEM((count, total), BF16),
            pltpu.SemaphoreType.DMA((16,)),
        ],
        compiler_params=pltpu.CompilerParams(vmem_limit_bytes=VMEM),
        cost_estimate=pl.CostEstimate(
            flops=2 * count * width * total,
            bytes_accessed=2 * (width * total + count * (width + total)),
            transcendentals=0,
        ),
    )(x, mod, weight)


def regroup(core, rim, source_ref, target_ref):
    half = core // 2
    left = core * core
    right = left + rim * (core + 2 * rim)
    top = right + rim * (core + 2 * rim)
    bottom = top + rim * core
    at = 0

    def take(*pieces):
        nonlocal at
        for start, n in pieces:
            target_ref[at : at + n, :] = source_ref[start : start + n, :]
            at += n

    for base, row in ((top, 0), (bottom, rim + core)):
        for a in range(rim):
            take((left + rim * (row + a), rim), (base + core * a, half))
        for a in range(rim):
            take((base + core * a + half, half), (right + rim * (row + a), rim))
    for r in range(core):
        take((left + rim * (rim + r), rim), (core * r, half))
    for r in range(core):
        take((core * r + half, half), (right + rim * (rim + r), rim))


def tile_kernel(
    core,
    rim,
    rows,
    q_factor,
    x_core,
    left,
    right,
    top,
    bottom,
    qkv_core,
    mod_ref,
    w_hbm,
    wo_hbm,
    wq_hbm,
    h1_out,
    cq_out,
    x_s,
    qkv_s,
    u_s,
    w_s,
    wo_s,
    wq_s,
    vv_s,
    p_a,
    p_b,
    attn_s,
    h1_s,
    hg_s,
    bad_s,
    sems,
):
    width = x_core.shape[1]
    channels = width // HEADS
    inner = x_core.shape[0]
    outer = sum(a.shape[0] for a in (left, right, top, bottom))
    total = inner + outer
    pairs, at = [], inner
    for part in (left, right, top, bottom):
        pairs.append((part, x_s.at[pl.ds(at, part.shape[0])]))
        at += part.shape[0]
    waits_x = begin(pairs, sems, 0)
    waits_w = begin(weight_pairs(w_hbm, w_s, QKV_PART), sems, 4)
    waits_qkv = begin([(qkv_core, qkv_s.at[pl.ds(0, inner)])], sems, 12)
    waits_later = begin(
        [(x_core, x_s.at[pl.ds(0, inner)]), (wo_hbm, wo_s), (wq_hbm, wq_s)],
        sems,
        13,
    )
    finish_all(waits_x)
    normalise(x_s, inner, outer, mod_ref, u_s)
    project_qkv(u_s, w_s, waits_w, QKV_PART, width, q_factor, qkv_s, inner)
    finish_all(waits_qkv)
    attend_self(
        channels,
        qkv_s.at[:, pl.ds(0, width)],
        qkv_s.at[:, pl.ds(width, width)],
        qkv_s.at[:, pl.ds(2 * width, width)],
        vv_s,
        (p_a, p_b),
        bad_s,
        rows,
        attn_s,
    )
    finish_all(waits_later)
    step = total // 2
    for r in range(0, total, step):
        part = slice(r, r + step)
        mixed = jnp.dot(attn_s[part, :], wo_s[...], preferred_element_type=F32)
        h1_s[part, :] = x_s[part, :].astype(F32) + mod_ref[2:3, :] * mixed
    regroup(core, rim, h1_s, hg_s)
    waits_h = begin([(hg_s, h1_out)], sems, 16)
    for r in range(0, total, step):
        part = slice(r, r + step)
        made = jnp.dot(hg_s[part, :].astype(BF16), wq_s[...], preferred_element_type=F32)
        x_s[part, :] = (made * q_factor).astype(BF16)
        here = pl.ds(r, step)
        waits_h += begin([(x_s.at[here], cq_out.at[here])], sems, 17 + r // step)
    finish_all(waits_h)


def tile_self(core, rim, q_factor, x_core, rims, qkv_core, mod, weights):
    inner, width = x_core.shape
    outer = sum(a.shape[0] for a in rims)
    total = inner + outer
    wide = weights[0].shape[1]
    return pl.pallas_call(
        functools.partial(tile_kernel, core, rim, 256, q_factor),
        out_shape=[
            jax.ShapeDtypeStruct((total, width), F32),
            jax.ShapeDtypeStruct((total, width), BF16),
        ],
        in_specs=[ANY] + [LOCAL] * 4 + [ANY, LOCAL] + [ANY] * 3,
        out_specs=[ANY, ANY],
        scratch_shapes=[
            pltpu.VMEM((total, width), BF16),
            pltpu.VMEM((total, wide), BF16),
            pltpu.VMEM((outer, width), BF16),
            pltpu.VMEM((width, wide), BF16),
            pltpu.VMEM((width, width), BF16),
            pltpu.VMEM((width, width), BF16),
            pltpu.VMEM((2 * total, WIN), BF16),
            pltpu.VMEM((total, 2 * total), BF16),
            pltpu.VMEM((total, 2 * total), BF16),
            pltpu.VMEM((total, width), BF16),
            pltpu.VMEM((total, width), F32),
            pltpu.VMEM((total, width), F32),
            pltpu.VMEM((1, LANES), F32),
            pltpu.SemaphoreType.DMA((20,)),
        ],
        compiler_params=pltpu.CompilerParams(vmem_limit_bytes=50 * 1024 * 1024),
        cost_estimate=pl.CostEstimate(
            flops=2 * outer * width * wide + 16 * total * width * total + 4 * total * width * width,
            bytes_accessed=2 * width * (wide + 2 * width) + 2 * inner * wide + 6 * total * width,
            transcendentals=HEADS * total * total,
        ),
    )(x_core, *rims, qkv_core, mod, *weights)


def text_kernel(text, first, parts, column_ref, h1, cq, t0, t1, t2, t3, wc_hbm, *rest):
    outs = rest[: len(parts)]
    q_s, h_s, kv_s, wc_s, p_a, p_b, attn_s, bad_s, sems = rest[len(parts) :]
    count, width = q_s.shape
    rows = pl.ds(first, count)
    pairs = [(cq.at[rows], q_s)]
    for k, arrived in enumerate((t0, t1, t2, t3)):
        size = arrived.shape[0]
        where = pl.multiple_of(lax.rem(column_ref[0] + k, 4) * size, size)
        pairs.append((arrived, kv_s.at[pl.ds(where, size), :]))
    waits = begin(pairs, sems, 0)
    waits_later = begin([(wc_hbm, wc_s), (h1.at[rows], h_s)], sems, 5)
    finish_all(waits)
    attend_text(width // HEADS, text, q_s, kv_s, (p_a, p_b), bad_s, count, attn_s)
    finish_all(waits_later)
    made = h_s[...] + jnp.dot(attn_s[...], wc_s[...], preferred_element_type=F32)
    at = 0
    for out, n in zip(outs, parts):
        out[...] = made[at : at + n].astype(BF16)
        at += n


def tile_text(text, first, parts, column, h1, cq, arrived, weight):
    count = sum(parts)
    width = h1.shape[1]
    padded = arrived[0].shape[1] // 2
    return pl.pallas_call(
        functools.partial(text_kernel, text, first, parts),
        out_shape=[jax.ShapeDtypeStruct((n, width), BF16) for n in parts],
        in_specs=[pl.BlockSpec(memory_space=pltpu.SMEM)] + [ANY] * 2 + [LOCAL] * 4 + [ANY],
        out_specs=[LOCAL] * len(parts),
        scratch_shapes=[
            pltpu.VMEM((count, width), BF16),
            pltpu.VMEM((count, width), F32),
            pltpu.VMEM((width, 2 * padded), BF16),
            pltpu.VMEM((width, width), BF16),
            pltpu.VMEM((count, 2 * padded), BF16),
            pltpu.VMEM((count, 2 * padded), BF16),
            pltpu.VMEM((count, width), BF16),
            pltpu.VMEM((1, LANES), F32),
            pltpu.SemaphoreType.DMA((7,)),
        ],
        compiler_params=pltpu.CompilerParams(vmem_limit_bytes=50 * 1024 * 1024),
        cost_estimate=pl.CostEstimate(
            flops=16 * count * width * padded + 2 * count * width * width,
            bytes_accessed=2 * width * (width + 2 * padded) + 8 * count * width,
            transcendentals=HEADS * count * padded,
        ),
    )(column, h1, cq, *arrived, weight)


def merge_kernel(lat_count, rim, lat_ref, near, far, low, high, passed, out_hbm, near_s, out_s, sems):
    lat = lat_ref[0]
    core = near.shape[0]
    rows = 8
    steps = range(core // rows)
    waits = begin([(near.at[pl.ds(i * rows, rows)], near_s.at[pl.ds(i * rows, rows)]) for i in steps], sems, 0)
    sent = []

    def average(body, extra, first):
        n = body.shape[0]
        ids = lax.broadcasted_iota(jnp.int32, (n, 1, 1), 0) + first
        shared = ((ids < rim) & (lat > 0)) | ((ids >= core - rim) & (lat < lat_count - 1))
        body = body.astype(F32) if extra is None else body.astype(F32) + extra.astype(F32)
        return body * jnp.where(shared, 0.5, 1.0)

    for i in steps:
        waits[i].wait()
        for first in range(i * rows, (i + 1) * rows, rim):
            part = slice(first, first + rim)
            extra = (None, None)
            if first == 0:
                extra = (low[rim:], passed[:rim])
            if first == core - rim:
                extra = (high[rim:], passed[rim:])
            a, b = average(near_s[part], extra[0], first), average(far[part], extra[1], first)
            made = jnp.concatenate([a[:, :8], (a[:, 8:] + b[:, :8]) * 0.5, b[:, 8:]], axis=1)
            out_s[part] = made.astype(BF16)
        here = pl.ds(i * rows, rows)
        sent += begin([(out_s.at[here], out_hbm.at[here])], sems, len(steps) + i)
    finish_all(sent)


def merge(lat_count, lat, rim, near, far, low, high, passed):
    core, span, width = near.shape
    return pl.pallas_call(
        functools.partial(merge_kernel, lat_count, rim),
        out_shape=jax.ShapeDtypeStruct((core, core, width), BF16),
        in_specs=[pl.BlockSpec(memory_space=pltpu.SMEM), ANY] + [LOCAL] * 4,
        out_specs=ANY,
        scratch_shapes=[
            pltpu.VMEM((core, span, width), BF16),
            pltpu.VMEM((core, core, width), BF16),
            pltpu.SemaphoreType.DMA((6,)),
        ],
        compiler_params=pltpu.CompilerParams(vmem_limit_bytes=SMALL),
        cost_estimate=pl.CostEstimate(
            flops=4 * core * core * width, bytes_accessed=8 * core * core * width, transcendentals=0
        ),
    )(lat, near, far, low, high, passed)


def send(value, mesh_sizes, down, right):
    rows, cols = mesh_sizes
    pairs = [
        (r * cols + c, (r + down) * cols + (c + right) % cols)
        for r in range(rows)
        for c in range(cols)
        if 0 <= r + down < rows
    ]
    return lax.ppermute(value, ("lat", "lon"), pairs)


def local(
    sizes,
    hidden,
    timestep,
    context,
    time_weight,
    modulation_bias,
    qkv_weight,
    out_weight,
    cross_q,
    cross_kv,
    cross_output_projection,
):
    core, width = hidden.shape[1], hidden.shape[3]
    half = core // 2
    rim = HALO
    text = context.shape[1]
    lon_count = sizes[1]
    to = functools.partial(send, mesh_sizes=sizes)
    q_factor = math.log2(math.e) / math.sqrt(width // HEADS)

    lon_count = sizes[1]
    lon = lax.axis_index("lon")

    def among(value, partner):
        return lax.ppermute(value, "lon", [(partner(i), i) for i in range(lon_count)])

    def joined(bit, mine, theirs):
        return join(((lon // bit) % 2).astype(jnp.int32)[None], mine, theirs)

    x = hidden[0]
    flat = lambda a: a.reshape(-1, width)
    top = to(flat(x[core - rim :]), down=1, right=0)
    bottom = to(flat(x[:rim]), down=-1, right=0)
    cos, sin = waves(timestep, time_weight.shape[0])
    kv_rows = jnp.transpose(cross_kv, (0, 2, 1))
    own_head, mod = prepare(cos, sin, time_weight, modulation_bias, context[0], kv_rows)
    own_head, top, bottom = lax.optimization_barrier((own_head, top, bottom))
    other = among(own_head, lambda i: i ^ 1)
    rows = lambda a: a.reshape(rim, core, width)
    first, last = pack(x, rows(top), rows(bottom))
    left = to(last, down=0, right=1)
    right = to(first, down=0, right=-1)
    two = joined(1, own_head, other)
    x, first, last, two = lax.optimization_barrier((x, first, last, two))
    far_two = among(two, lambda i: i ^ 2)
    x_core = flat(x)
    qkv_core = core_qkv(q_factor, x_core, mod, qkv_weight)
    four = joined(2, two, far_two)
    qkv_core, four = lax.optimization_barrier((qkv_core, four))
    arrived = [four] + [among(four, lambda i, k=k: (i + 4 * k) % lon_count) for k in (1, 2, 3)]
    column = (lon // 4).astype(jnp.int32)[None]

    h1, cq = tile_self(
        core,
        rim,
        q_factor,
        x_core,
        (left, right, top, bottom),
        qkv_core,
        mod,
        (qkv_weight, out_weight, cross_q),
    )
    span = half + rim
    edge, block = rim * span, core * span
    top_made, bottom_made, main = tile_text(
        text, 0, (2 * edge, 2 * edge, block), column, h1, cq, arrived, cross_output_projection
    )
    high = to(top_made, down=-1, right=0)
    low = to(bottom_made, down=1, right=0)
    far = to(main, down=0, right=-1)
    (near,) = tile_text(
        text, 4 * edge + block, (block,), column, h1, cq, arrived, cross_output_projection
    )
    near, low, high = lax.optimization_barrier((near, low, high))
    passed = to(jnp.concatenate([low[:edge], high[:edge]], axis=0), down=0, right=-1)
    shape = lambda a: a.reshape(-1, span, width)
    lat = lax.axis_index("lat").astype(jnp.int32)[None]
    return merge(sizes[0], lat, rim, *(shape(a) for a in (near, far, low, high, passed)))[None]


def solution(mesh):
    in_specs = (
        P(None, "lat", "lon", None),
        P(),
        P(),
        P(),
        P(),
        P(),
        P(),
        P(),
        P(None, None, "lon"),
        P(),
    )
    out_specs = P(None, "lat", "lon", None)
    sizes = (mesh.shape["lat"], mesh.shape["lon"])
    return jax.shard_map(
        functools.partial(local, sizes), mesh=mesh, in_specs=in_specs, out_specs=out_specs, check_vma=False
    )
```
